32 devices in a mesh: canvas: 8 (over y, x, core), rows: 4 (over z).
Axes of the slice: x: 2, y: 2, z: 4, core: 2. Of those that a mesh axis runs over, the one named last changes fastest.
Arguments:
- tokens: bfloat16 [16, 1024, 768], P('canvas', 'rows'), may hold values from -6 to 6
- latent: int32 [16, 1024], P('canvas', 'rows'), may hold values from 0 to 3, as said below
- condition: float32 [16, 4, 768], P('canvas'), may hold values from -6 to 6
- w_ada: bfloat16 [768, 4608], replicated, may hold values from -0.21875 to 0.21875
- b_ada: bfloat16 [4608], replicated, may hold values from -1.5 to 1.5
- conv_attn: bfloat16 [9, 768], replicated, may hold values from -2 to 2
- w_qkv: bfloat16 [768, 2304], replicated, may hold values from -0.21875 to 0.21875
- bias_qv: bfloat16 [1536], replicated, may hold values from -1.5 to 1.5
- w_out: bfloat16 [768, 768], replicated, may hold values from -0.875 to 0.875
- b_out: bfloat16 [768], replicated, may hold values from -1.5 to 1.5
- w_up: bfloat16 [768, 3072], replicated, may hold values from -0.21875 to 0.21875
- b_up: bfloat16 [3072], replicated, may hold values from -1.5 to 1.5
- conv_ffn: bfloat16 [9, 3072], replicated, may hold values from -2 to 2
- w_down: bfloat16 [3072, 768], replicated, may hold values from -0.109375 to 0.109375
- b_down: bfloat16 [768], replicated, may hold values from -1.5 to 1.5
- cotangent: bfloat16 [16, 1024, 768], P('canvas', 'rows'), may hold values from -6 to 6
Outputs:
- output: bfloat16 [16, 1024, 768], P('canvas', 'rows')
- grad_input: float32 [16, 1024, 768], P('canvas', 'rows')
- grad_condition: float32 [16, 4, 768], P('canvas')
- grad_w_ada: float32 [768, 4608], P('canvas')
- grad_b_ada: float32 [4608], P('canvas')
- grad_conv_attn: float32 [9, 768], P(None, 'canvas')
- grad_w_qkv: float32 [768, 2304], P('canvas')
- grad_bias_qv: float32 [1536], P('canvas')
- grad_w_out: float32 [768, 768], P('canvas')
- grad_b_out: float32 [768], P('canvas')
- grad_w_up: float32 [768, 3072], P('canvas')
- grad_b_up: float32 [3072], P('canvas')
- grad_conv_ffn: float32 [9, 3072], P(None, 'canvas')
- grad_w_down: float32 [3072, 768], P('canvas')
- grad_b_down: float32 [768], P('canvas')
The draws below stay inside these ranges and needn't reach their ends.
Inputs may be any that keep to these rules, and one draw needn't show every extreme that they name: In each canvas of 32 x 32 tokens each of the four latent ids marks 16 * 16 tokens: either four strips of 32 rows by 8 columns, or two such strips filling one half of the columns beside two 16 x 16 squares filling the other half. Some latent of every canvas covers all rows.
All inputs are finite; a program needn't handle non-finite values.
Results may differ from the reference program's by a relative error of at most 0.02.
The reference program's roundings to bfloat16 on the way count: a program that leaves them out, or rounds other values in their place, can miss the bound.
Values may be sent and summed in bfloat16 or wider, within the bound.
A program may use at most 256 MiB of HBM per device.

```python
import jax
import jax.numpy as jnp
from jax import lax

D = 768
HEADS = 12
HEAD_DIM = 64
FF = 3072
SIDE = 32
CANVASES = 16


def shuffle_labels(label_key):
    return jax.random.permutation(label_key, 4).astype(jnp.int32)


def draw_latent(key, part):
    key = jax.random.fold_in(key, 7)
    layout_key, label_key = jax.random.split(key)
    layout = jax.random.randint(layout_key, (CANVASES, 1), 0, 3)
    positions = jnp.arange(SIDE * SIDE, dtype=jnp.int32)
    row_index = positions // SIDE
    col_index = positions % SIDE
    strip_id = col_index // (SIDE // 4)
    square_id = 2 + (row_index >= SIDE // 2).astype(jnp.int32)
    left_strips = jnp.where(col_index < SIDE // 2, strip_id, square_id)
    right_strips = jnp.where(col_index >= SIDE // 2, strip_id - 2, square_id)
    region = jnp.where(layout == 0, strip_id[None, :], jnp.where(layout == 1, left_strips[None, :], right_strips[None, :]))
    labels = jax.vmap(shuffle_labels)(jax.random.split(label_key, CANVASES))
    return jnp.take_along_axis(labels, region.astype(jnp.int32), axis=1).astype(jnp.int32)


def spiked(entries, own_key, source, target, parts, factor):
    def block_of(axis_at):
        return (jnp.arange(entries.shape[axis_at]) // (entries.shape[axis_at] // parts)).reshape((-1,) + (1,) * (entries.ndim - 1 - axis_at))

    one_side = jax.random.permutation(own_key, parts)[block_of(target)]
    second = (block_of(target) + parts // 2) % parts
    return jnp.where((block_of(source) == one_side) | (block_of(source) == second), factor * entries, entries)


def levels(stream_key, shape, pieces, least, largest):
    def one(dim, parts):
        draws = jax.random.uniform(jax.random.fold_in(jax.random.fold_in(stream_key, 6), dim), (parts,), jnp.float32, least / len(pieces), largest / len(pieces))
        return jnp.repeat(jnp.exp(draws), shape[dim] // parts).reshape((-1,) + (1,) * (len(shape) - dim - 1))

    gain = one(*pieces[0])
    for cut in pieces[1:]:
        gain = gain * one(*cut)
    return gain


def scatter_about(rng, shape, deviation, reach, cuts=(), kind=jnp.bfloat16):
    values = jax.random.normal(rng, shape, jnp.float32) * deviation
    if len(cuts) > 0:
        values = levels(rng, shape, cuts, -0.22, 0.18) * values
    return jnp.clip(values, min=-reach, max=reach).astype(kind)


def heavy_noise(stream_key, extent, scale, reach, shards, heavy, kind=jnp.bfloat16):
    array = scale * jax.random.normal(stream_key, extent, jnp.float32)
    if shards:
        array = array * levels(stream_key, extent, shards, -0.22, 0.18)
    return jnp.clip(spiked(array, jax.random.fold_in(stream_key, 3), *heavy), -reach, reach).astype(kind)


def setup_inputs(seed: int = 0) -> dict:
    key_list = jax.random.split(jax.random.key(seed), 17)
    return {
        "tokens": scatter_about(key_list[0], (CANVASES, SIDE * SIDE, D), 1.0, 6.0, ((0, 8), (1, 4))),
        "latent": draw_latent(jax.random.fold_in(key_list[16], 71), 0),
        "condition": scatter_about(key_list[2], (CANVASES, 4, D), 1.0, 6.0, ((0, 8),), jnp.float32),
        "w_ada": scatter_about(key_list[3], (D, 6 * D), D ** -0.5, 0.21875),
        "b_ada": scatter_about(key_list[4], (6 * D,), 0.3, 1.5),
        "conv_attn": scatter_about(key_list[5], (9, D), 9 ** -0.5, 2.0),
        "w_qkv": scatter_about(key_list[6], (D, 3 * D), D ** -0.5, 0.21875),
        "bias_qv": scatter_about(key_list[7], (2 * D,), 0.3, 1.5),
        "w_out": scatter_about(key_list[8], (D, D), (D // 16) ** -0.5, 0.875),
        "b_out": scatter_about(key_list[9], (D,), 0.3, 1.5),
        "w_up": scatter_about(key_list[10], (D, FF), D ** -0.5, 0.21875),
        "b_up": scatter_about(key_list[11], (FF,), 0.3, 1.5),
        "conv_ffn": scatter_about(key_list[12], (9, FF), 9 ** -0.5, 2.0),
        "w_down": scatter_about(key_list[13], (FF, D), FF ** -0.5, 0.109375),
        "b_down": scatter_about(key_list[14], (D,), 0.3, 1.5),
        "cotangent": heavy_noise(key_list[15], (CANVASES, SIDE * SIDE, D), 1.0, 6.0, ((0, 8), (1, 4)), (0, 2, 8, 2.0)),
    }


EPSILON = 1e-06
NEG_FILL = -1e+30
PRECISE = lax.Precision.HIGHEST

@jax.custom_vjp
def low(v):
    return lax.optimization_barrier(v.astype(jnp.bfloat16)).astype(jnp.float32)

@jax.custom_vjp
def low_back(v):
    return v

def low_keep(v):
    return (low(v), None)

def low_pass(kept, grad):
    return (grad,)

def back_keep(v):
    return (v, None)

def back_low(kept, grad):
    return (low(grad),)
low.defvjp(low_keep, low_pass)
low_back.defvjp(back_keep, back_low)

def layer_norm(values):
    centered = values - lax.optimization_barrier(jnp.mean(values, axis=-1, keepdims=True))
    return centered * lax.rsqrt(lax.optimization_barrier(jnp.mean(centered * centered, axis=-1, keepdims=True)) + EPSILON)

def spatial_conv(field, kernel):
    channels = field.shape[-1]
    canvas_grid = field.reshape(SIDE, SIDE, channels)
    padded = jnp.pad(canvas_grid, ((1, 1), (1, 1), (0, 0)))
    summed = jnp.zeros_like(canvas_grid)
    for tap_row in range(3):
        for tap_col in range(3):
            summed = summed + kernel[3 * tap_row + tap_col] * padded[tap_row:tap_row + SIDE, tap_col:tap_col + SIDE]
    return summed.reshape(SIDE * SIDE, channels)

def unshuffle(field):
    channels = field.shape[-1]
    return field.reshape(SIDE // 2, 2, SIDE // 2, 2, channels).transpose(1, 3, 0, 2, 4).reshape(4, SIDE * SIDE // 4, channels)

def reshuffle(field):
    channels = field.shape[-1]
    return field.reshape(2, 2, SIDE // 2, SIDE // 2, channels).transpose(2, 0, 3, 1, 4).reshape(SIDE * SIDE, channels)

def gelu_tanh(values):
    return jax.nn.gelu(values, approximate=True)

def heads_of(field):
    return unshuffle(field).reshape(4, SIDE * SIDE // 4, HEADS, HEAD_DIM)

def attention(queries, key_rows, value_rows, latent_groups):
    scores = jnp.einsum('gqhe,gkhe->ghqk', heads_of(queries), heads_of(key_rows), precision=PRECISE) * HEAD_DIM ** (-0.5)
    scores = low_back(scores)
    same_latent = latent_groups[:, None, :, None] == latent_groups[:, None, None, :]
    softmax_weights = jax.nn.softmax(jnp.where(same_latent, scores, NEG_FILL), axis=-1)
    mixed_heads = jnp.einsum('ghqk,gkhe->gqhe', softmax_weights, heads_of(value_rows), precision=PRECISE)
    return reshuffle(mixed_heads.reshape(4, SIDE * SIDE // 4, HEADS * HEAD_DIM))

def canvas_block(tokens, latent, condition, w_ada, b_ada, conv_attn, w_qkv, bias_qv, w_out, b_out, w_up, b_up, conv_ffn, w_down, b_down):
    model_width = HEADS * HEAD_DIM
    cond_low = low(jax.nn.silu(condition))
    modulation = jnp.dot(cond_low, w_ada, precision=PRECISE) + b_ada
    onehot = (latent[:, None] == jnp.arange(4)[None, :]).astype(jnp.float32)
    per_token = jnp.dot(onehot, modulation, precision=PRECISE)
    shift_one, scale_one, gate_one, shift_two, scale_two, gate_two = jnp.split(per_token, 6, axis=-1)
    attn_in = low(layer_norm(tokens) * (1.0 + scale_one) + shift_one)
    conv_one = low(low_back(spatial_conv(attn_in, conv_attn)))
    bias_full = jnp.concatenate([bias_qv[:model_width], jnp.zeros((model_width,), jnp.float32), bias_qv[model_width:]])
    projected = jnp.dot(conv_one, w_qkv, precision=PRECISE) + bias_full
    queries = low(low_back(projected[:, :model_width]))
    key_rows = low(low_back(projected[:, model_width:2 * model_width]))
    value_rows = low(low_back(projected[:, 2 * model_width:]))
    latent_groups = unshuffle(latent[:, None])[:, :, 0]
    attended = low(low_back(attention(queries, key_rows, value_rows, latent_groups)))
    attn_out = low_back(jnp.dot(attended, w_out, precision=PRECISE) + b_out)
    middle = tokens + gate_one * attn_out
    ffn_in = low(layer_norm(middle) * (1.0 + scale_two) + shift_two)
    up_rows = low(low_back(jnp.dot(ffn_in, w_up, precision=PRECISE) + b_up))
    conv_two = low_back(spatial_conv(up_rows, conv_ffn))
    activated = low(gelu_tanh(conv_two))
    branch = low_back(jnp.dot(activated, w_down, precision=PRECISE) + b_down)
    return middle + gate_two * branch

def reference(tokens, latent, condition, w_ada, b_ada, conv_attn, w_qkv, bias_qv, w_out, b_out, w_up, b_up, conv_ffn, w_down, b_down, cotangent):
    weights = tuple((weight_arg.astype(jnp.float32) for weight_arg in (w_ada, b_ada, conv_attn, w_qkv, bias_qv, w_out, b_out, w_up, b_up, conv_ffn, w_down, b_down)))

    def canvas_step(totals, inputs_now):
        canvas_tokens, canvas_latent, canvas_cond, canvas_cot = inputs_now

        def forward(token_rows, cond_rows, *params):
            return canvas_block(token_rows, canvas_latent, cond_rows, *params)
        result, pullback = jax.vjp(forward, canvas_tokens.astype(jnp.float32), canvas_cond.astype(jnp.float32), *weights)
        gradients = pullback(canvas_cot.astype(jnp.float32))
        totals = tuple((running + fresh_grad for running, fresh_grad in zip(totals, gradients[2:])))
        return (totals, (result.astype(jnp.bfloat16), gradients[0], gradients[1]))
    initial = tuple((jnp.zeros(weight_arg.shape, jnp.float32) for weight_arg in weights))
    totals, stacked = lax.scan(canvas_step, initial, (tokens, latent, condition, cotangent))
    return (stacked[0], stacked[1], stacked[2], totals[0], totals[1], totals[2], totals[3], totals[4], totals[5], totals[6], totals[7], totals[8], totals[9], totals[10], totals[11])
```

```python
from types import SimpleNamespace

import jax
import jax.numpy as jnp
from jax import lax
from jax.experimental import pallas as pl
from jax.experimental.pallas import tpu as pltpu
from jax.sharding import PartitionSpec as P

HEADS = 12
HEAD_DIM = 64
SIDE = 32


EPSILON = 1e-06
NEG_FILL = -1e30
PRECISE = lax.Precision.HIGHEST
VMEM_LIMIT = 65400 * 2**10


def padded_2(cells, sides, width):
    for axis, dim in sides:
        count = lax.axis_size(axis)
        ends = count - 1
        head = lax.slice_in_dim(cells, 0, width, axis=dim)
        tail = lax.slice_in_dim(cells, cells.shape[dim] - width, cells.shape[dim], axis=dim)
        cells = jnp.concatenate(
            [
                lax.ppermute(tail, axis, [(i, (i + 1) % count) for i in range(ends)]),
                cells,
                lax.ppermute(head, axis, [((i + 1) % count, i) for i in range(ends)]),
            ],
            axis=dim,
        )
    return cells


def passed_along(block, axis, distance):
    devices = range(lax.axis_size(axis))
    route = [((i - distance) % len(devices), i) for i in devices]
    return lax.ppermute(block, axis, route)


def layer_norm(values):
    centered = values - jnp.mean(values, axis=-1, keepdims=True)
    return centered * lax.rsqrt(jnp.mean(centered * centered, axis=-1, keepdims=True) + EPSILON)


def modulate_norm(values, shift, scale_part):
    return layer_norm(values) * (1.0 + scale_part) + shift


def gelu_tanh(values):
    return jax.nn.gelu(values, approximate=True)


def pad_columns(field):
    return jnp.pad(field, ((0, 0), (0, 0), (1, 1), (0, 0)))


def grid_taps(padded, kernel, rows_here, cols_here):
    summed = padded[:, 0:rows_here, 0:cols_here].astype(jnp.float32) * kernel[0]
    for tap_row in range(3):
        for tap_col in range(3):
            if tap_row + tap_col > 0:
                window = padded[
                    :, tap_row : tap_row + rows_here, tap_col : tap_col + cols_here
                ].astype(jnp.float32)
                summed = summed + window * kernel[3 * tap_row + tap_col]
    return summed


def kernel_grad(padded, grad_grid):
    rows_here = grad_grid.shape[1]
    cols_here = grad_grid.shape[2]
    grad_f = grad_grid.astype(jnp.float32)
    tap_sums = []
    for tap_row in range(3):
        for tap_col in range(3):
            window = padded[:, tap_row : tap_row + rows_here, tap_col : tap_col + cols_here].astype(
                jnp.float32
            )
            tap_sums.append(jnp.sum(window * grad_f, axis=(0, 1, 2)))
    return jnp.stack(tap_sums)


def to_groups(field, rows_here):
    canvases = field.shape[0]
    channels = field.shape[-1]
    shaped = field.reshape(canvases, rows_here // 2, 2, SIDE // 2, 2, channels)
    return shaped.transpose(0, 2, 4, 1, 3, 5).reshape(
        canvases, 4, rows_here // 2 * (SIDE // 2), channels
    )


def from_groups(field, rows_here):
    canvases = field.shape[0]
    channels = field.shape[-1]
    shaped = field.reshape(canvases, 2, 2, rows_here // 2, SIDE // 2, channels)
    return shaped.transpose(0, 3, 1, 4, 2, 5).reshape(canvases, rows_here * SIDE, channels)


def block_scores(query_heads, key_piece, query_lat, key_lat):
    canvases = key_piece.shape[0]
    count = key_piece.shape[2]
    key_heads = key_piece.reshape(canvases, 4, count, HEADS, HEAD_DIM)
    scores = jnp.einsum(
        "cgqhe,cgkhe->cghqk", query_heads, key_heads, preferred_element_type=jnp.float32
    ) * HEAD_DIM ** (-0.5)
    same_latent = query_lat[:, :, None, :, None] == key_lat[:, :, None, None, :]
    return (scores, same_latent, key_heads)


def shards(
    tokens,
    latent,
    condition,
    w_ada,
    b_ada,
    conv_attn,
    w_qkv,
    bias_qv,
    w_out,
    b_out,
    w_up,
    b_up,
    conv_ffn,
    w_down,
    b_down,
    cotangent,
):
    canvases = tokens.shape[0]
    local_tokens = tokens.shape[1]
    model_width = tokens.shape[2]
    ffn_width = w_up.shape[1]
    rows_here = local_tokens // SIDE
    group_len = local_tokens // 4
    score_scale = HEAD_DIM ** (-0.5)
    tokens_f = tokens.astype(jnp.float32)
    onehot = (latent[..., None] == jnp.arange(4)).astype(jnp.float32)
    silu_cond, silu_pull = jax.vjp(jax.nn.silu, condition)
    cond_low = silu_cond.astype(jnp.bfloat16)
    modulation = jnp.einsum(
        "ckd,df->ckf", cond_low, w_ada, preferred_element_type=jnp.float32
    ) + b_ada.astype(jnp.float32)
    per_token = jnp.einsum("cnk,ckf->cnf", onehot, modulation, precision=PRECISE)
    shift_one, scale_one, gate_one, shift_two, scale_two, gate_two = jnp.split(
        per_token, 6, axis=-1
    )
    h_one, norm_one_pull = jax.vjp(modulate_norm, tokens_f, shift_one, scale_one)
    attn_in = h_one.astype(jnp.bfloat16).reshape(canvases, rows_here, SIDE, model_width)
    attn_pad = pad_columns(padded_2(attn_in, (("rows", 1),), 1))
    conv_attn_f = conv_attn.astype(jnp.float32)
    conv_low = (
        grid_taps(attn_pad, conv_attn_f, rows_here, SIDE)
        .astype(jnp.bfloat16)
        .reshape(-1, model_width)
    )
    bias_full = jnp.concatenate(
        [bias_qv[:model_width], jnp.zeros((model_width,), jnp.bfloat16), bias_qv[model_width:]]
    ).astype(jnp.float32)
    projected = (jnp.dot(conv_low, w_qkv, preferred_element_type=jnp.float32) + bias_full).astype(
        jnp.bfloat16
    )
    grouped = to_groups(projected.reshape(canvases, local_tokens, 3 * model_width), rows_here)
    queries = grouped[..., :model_width]
    key_rows = grouped[..., model_width : 2 * model_width]
    value_rows = grouped[..., 2 * model_width :]
    lat_groups = to_groups(latent[..., None], rows_here)[..., 0]
    all_lat = lax.all_gather(lat_groups, "rows", axis=2, tiled=True)
    query_heads = queries.reshape(canvases, 4, group_len, HEADS, HEAD_DIM)
    start_best = jnp.full((canvases, 4, HEADS, group_len), NEG_FILL, jnp.float32)
    best = start_best
    key_piece = lax.all_gather(key_rows, "rows", axis=2, tiled=True)
    value_piece = lax.all_gather(value_rows, "rows", axis=2, tiled=True)
    count = key_piece.shape[2]
    fold_scores, fold_same_latent, fold_key_heads = block_scores(
        query_heads, key_piece, lat_groups, all_lat
    )
    masked = jnp.where(fold_same_latent, fold_scores, NEG_FILL)
    newest = jnp.maximum(best, jnp.max(masked, axis=-1))
    weights = jnp.where(fold_same_latent, jnp.exp(masked - newest[..., None]), 0.0)
    fold_value_heads = value_piece.astype(jnp.float32).reshape(canvases, 4, count, HEADS, HEAD_DIM)
    accum = jnp.einsum("cghqk,cgkhe->cghqe", weights, fold_value_heads, precision=PRECISE)
    best, weight_sum, accum = (newest, jnp.sum(weights, axis=-1), accum)
    attn_heads = accum / weight_sum[..., None]
    log_norm = best + jnp.log(weight_sum)
    attended = from_groups(
        attn_heads.transpose(0, 1, 3, 2, 4).reshape(canvases, 4, group_len, model_width), rows_here
    )
    attended_low = attended.astype(jnp.bfloat16).reshape(-1, model_width)
    attn_out = (
        jnp.dot(attended_low, w_out, preferred_element_type=jnp.float32) + b_out.astype(jnp.float32)
    ).reshape(canvases, local_tokens, model_width)
    middle = tokens_f + gate_one * attn_out
    h_two, norm_two_pull = jax.vjp(modulate_norm, middle, shift_two, scale_two)
    ffn_in = h_two.astype(jnp.bfloat16).reshape(-1, model_width)
    up_rows = (
        jnp.dot(ffn_in, w_up, preferred_element_type=jnp.float32) + b_up.astype(jnp.float32)
    ).astype(jnp.bfloat16)
    up_grid = up_rows.reshape(canvases, rows_here, SIDE, ffn_width)
    up_pad = pad_columns(padded_2(up_grid, (("rows", 1),), 1))
    conv_ffn_f = conv_ffn.astype(jnp.float32)
    conv_two = grid_taps(up_pad, conv_ffn_f, rows_here, SIDE)
    activated, gelu_pull = jax.vjp(gelu_tanh, conv_two)
    act_low = activated.astype(jnp.bfloat16).reshape(-1, ffn_width)
    branch = (
        jnp.dot(act_low, w_down, preferred_element_type=jnp.float32) + b_down.astype(jnp.float32)
    ).reshape(canvases, local_tokens, model_width)
    result = (middle + gate_two * branch).astype(jnp.bfloat16)
    out_grad = cotangent.astype(jnp.float32)
    branch_grad = (gate_two * out_grad).astype(jnp.bfloat16).reshape(-1, model_width)
    gate_two_grad = out_grad * branch
    g_b_down = jnp.sum(branch_grad.astype(jnp.float32), axis=0)
    g_w_down = jnp.dot(act_low.T, branch_grad, preferred_element_type=jnp.float32)
    act_grad = jnp.dot(branch_grad, w_down.T, preferred_element_type=jnp.float32).reshape(
        canvases, rows_here, SIDE, ffn_width
    )
    conv_two_grad = gelu_pull(act_grad)[0].astype(jnp.bfloat16)
    conv_two_pad = pad_columns(padded_2(conv_two_grad, (("rows", 1),), 1))
    up_grad = (
        grid_taps(conv_two_pad, conv_ffn_f[::-1], rows_here, SIDE)
        .astype(jnp.bfloat16)
        .reshape(-1, ffn_width)
    )
    g_conv_ffn = kernel_grad(up_pad, conv_two_grad)
    g_b_up = jnp.sum(up_grad.astype(jnp.float32), axis=0)
    g_w_up = jnp.dot(ffn_in.T, up_grad, preferred_element_type=jnp.float32)
    ffn_grad = jnp.dot(up_grad, w_up.T, preferred_element_type=jnp.float32).reshape(
        canvases, local_tokens, model_width
    )
    middle_part, shift_two_grad, scale_two_grad = norm_two_pull(ffn_grad)
    middle_grad = middle_part + out_grad
    gate_one_grad = middle_grad * attn_out
    attn_grad = (gate_one * middle_grad).astype(jnp.bfloat16).reshape(-1, model_width)
    g_b_out = jnp.sum(attn_grad.astype(jnp.float32), axis=0)
    g_w_out = jnp.dot(attended_low.T, attn_grad, preferred_element_type=jnp.float32)
    attended_grad = jnp.dot(attn_grad, w_out.T, preferred_element_type=jnp.float32).astype(
        jnp.bfloat16
    )
    grad_heads = to_groups(
        attended_grad.reshape(canvases, local_tokens, model_width), rows_here
    ).reshape(canvases, 4, group_len, HEADS, HEAD_DIM)
    grad_heads_f = grad_heads.astype(jnp.float32)
    delta = jnp.sum(grad_heads_f.transpose(0, 1, 3, 2, 4) * attn_heads, axis=-1)
    row_count = lax.axis_size("rows")
    here = lax.axis_index("rows")
    carried = jnp.stack([key_rows, value_rows])
    pending = jnp.zeros((2,) + key_rows.shape, jnp.float32)
    query_grad = jnp.zeros((canvases, 4, group_len, HEADS, HEAD_DIM), jnp.float32)
    for turn_index in range(row_count):
        source = (here - turn_index) % row_count
        key_lat = lax.dynamic_slice_in_dim(all_lat, source * group_len, group_len, 2)
        scores, same_latent, key_heads = block_scores(query_heads, carried[0], lat_groups, key_lat)
        value_heads = carried[1].reshape(canvases, 4, group_len, HEADS, HEAD_DIM)
        softmax_weights = jnp.where(same_latent, jnp.exp(scores - log_norm[..., None]), 0.0)
        weight_grad = jnp.einsum(
            "cgqhe,cgkhe->cghqk", grad_heads, value_heads, preferred_element_type=jnp.float32
        )
        score_grad = (softmax_weights * (weight_grad - delta[..., None])).astype(jnp.bfloat16)
        query_grad = query_grad + score_scale * jnp.einsum(
            "cghqk,cgkhe->cgqhe", score_grad, key_heads, preferred_element_type=jnp.float32
        )
        key_part = score_scale * jnp.einsum(
            "cghqk,cgqhe->cgkhe", score_grad, query_heads, preferred_element_type=jnp.float32
        )
        value_part = jnp.einsum(
            "cghqk,cgqhe->cgkhe", softmax_weights, grad_heads_f, precision=PRECISE
        )
        pending = pending + jnp.stack([key_part, value_part]).reshape(pending.shape)
        if turn_index + 1 < row_count:
            carried = passed_along(carried, "rows", 1)
        pending = passed_along(pending.astype(jnp.bfloat16), "rows", 1).astype(pending.dtype)
    query_low = query_grad.reshape(canvases, 4, group_len, model_width).astype(jnp.bfloat16)
    grouped_grad = jnp.concatenate(
        [query_low, pending[0].astype(jnp.bfloat16), pending[1].astype(jnp.bfloat16)], axis=-1
    )
    qkv_grad = from_groups(grouped_grad, rows_here).reshape(-1, 3 * model_width)
    qkv_grad_f = qkv_grad.astype(jnp.float32)
    g_bias_qv = jnp.concatenate(
        [
            jnp.sum(qkv_grad_f[:, :model_width], axis=0),
            jnp.sum(qkv_grad_f[:, 2 * model_width :], axis=0),
        ]
    )
    g_w_qkv = jnp.dot(conv_low.T, qkv_grad, preferred_element_type=jnp.float32)
    conv_one_grad = (
        jnp.dot(qkv_grad, w_qkv.T, preferred_element_type=jnp.float32)
        .astype(jnp.bfloat16)
        .reshape(canvases, rows_here, SIDE, model_width)
    )
    conv_one_pad = pad_columns(padded_2(conv_one_grad, (("rows", 1),), 1))
    attn_in_grad = grid_taps(conv_one_pad, conv_attn_f[::-1], rows_here, SIDE).reshape(
        canvases, local_tokens, model_width
    )
    g_conv_attn = kernel_grad(attn_pad, conv_one_grad)
    token_part, shift_one_grad, scale_one_grad = norm_one_pull(attn_in_grad)
    input_grad = token_part + middle_grad
    token_mod_grad = jnp.concatenate(
        [
            shift_one_grad,
            scale_one_grad,
            gate_one_grad,
            shift_two_grad,
            scale_two_grad,
            gate_two_grad,
        ],
        axis=-1,
    )
    mod_grad = jnp.einsum("cnk,cnf->ckf", onehot, token_mod_grad, precision=PRECISE)
    cond_f = cond_low.astype(jnp.float32)
    summed = (
        lax.psum(g_conv_attn.astype(jnp.bfloat16), "rows").astype(jnp.float32),
        lax.psum(g_w_qkv.astype(jnp.bfloat16), "rows").astype(jnp.float32),
        lax.psum(g_bias_qv.astype(jnp.bfloat16), "rows").astype(jnp.float32),
        lax.psum(g_w_out.astype(jnp.bfloat16), "rows").astype(jnp.float32),
        lax.psum(g_b_out.astype(jnp.bfloat16), "rows").astype(jnp.float32),
        lax.psum(g_w_up.astype(jnp.bfloat16), "rows").astype(jnp.float32),
        lax.psum(g_b_up.astype(jnp.bfloat16), "rows").astype(jnp.float32),
        lax.psum(g_conv_ffn.astype(jnp.bfloat16), "rows").astype(jnp.float32),
        lax.psum(g_w_down.astype(jnp.bfloat16), "rows").astype(jnp.float32),
        lax.psum(g_b_down.astype(jnp.bfloat16), "rows").astype(jnp.float32),
        lax.psum(mod_grad.astype(jnp.bfloat16), "rows").astype(jnp.float32),
    )
    mod_total = summed[10]
    g_w_ada = jnp.einsum("ckd,ckf->df", cond_f, mod_total, precision=PRECISE)
    g_b_ada = jnp.sum(mod_total, axis=(0, 1))
    shares = (
        lax.psum_scatter(
            g_w_ada.astype(jnp.bfloat16), "canvas", scatter_dimension=0, tiled=True
        ).astype(jnp.float32),
        lax.psum_scatter(
            g_b_ada.astype(jnp.bfloat16), "canvas", scatter_dimension=0, tiled=True
        ).astype(jnp.float32),
        lax.psum_scatter(
            summed[0].astype(jnp.bfloat16), "canvas", scatter_dimension=1, tiled=True
        ).astype(jnp.float32),
        lax.psum_scatter(
            summed[1].astype(jnp.bfloat16), "canvas", scatter_dimension=0, tiled=True
        ).astype(jnp.float32),
        lax.psum_scatter(
            summed[2].astype(jnp.bfloat16), "canvas", scatter_dimension=0, tiled=True
        ).astype(jnp.float32),
        lax.psum_scatter(
            summed[3].astype(jnp.bfloat16), "canvas", scatter_dimension=0, tiled=True
        ).astype(jnp.float32),
        lax.psum_scatter(
            summed[4].astype(jnp.bfloat16), "canvas", scatter_dimension=0, tiled=True
        ).astype(jnp.float32),
        lax.psum_scatter(
            summed[5].astype(jnp.bfloat16), "canvas", scatter_dimension=0, tiled=True
        ).astype(jnp.float32),
        lax.psum_scatter(
            summed[6].astype(jnp.bfloat16), "canvas", scatter_dimension=0, tiled=True
        ).astype(jnp.float32),
        lax.psum_scatter(
            summed[7].astype(jnp.bfloat16), "canvas", scatter_dimension=1, tiled=True
        ).astype(jnp.float32),
        lax.psum_scatter(
            summed[8].astype(jnp.bfloat16), "canvas", scatter_dimension=0, tiled=True
        ).astype(jnp.float32),
        lax.psum_scatter(
            summed[9].astype(jnp.bfloat16), "canvas", scatter_dimension=0, tiled=True
        ).astype(jnp.float32),
    )
    cond_grad = silu_pull(
        jnp.einsum("ckf,df->ckd", mod_total, w_ada.astype(jnp.float32), precision=PRECISE)
    )[0]
    return (
        result,
        input_grad,
        cond_grad,
        shares[0],
        shares[1],
        shares[2],
        shares[3],
        shares[4],
        shares[5],
        shares[6],
        shares[7],
        shares[8],
        shares[9],
        shares[10],
        shares[11],
    )

BF = jnp.bfloat16
F32 = jnp.float32
D = 768
FF = 3072
HB = 384
BIG = -1e30


def dot(a, b):
    return jnp.dot(a, b, preferred_element_type=F32)


def dot_t(a, b):
    return lax.dot_general(a, b, (((1,), (1,)), ((), ())), preferred_element_type=F32)


def dot_l(a, b):
    return lax.dot_general(a, b, (((0,), (0,)), ((), ())), preferred_element_type=F32)


def iota(shape, dim):
    return lax.broadcasted_iota(jnp.int32, shape, dim)


def ones_where(mask):
    return jnp.where(mask, 1.0, 0.0).astype(BF)


def taps_of(pr, pc, back):
    found = []
    for i in range(3):
        for j in range(3):
            di, dj = (1 - i, 1 - j) if back else (i - 1, j - 1)
            gr = pr if di == 0 else 1 - pr
            gc = pc if dj == 0 else 1 - pc
            ro = 0 if di == 0 else (pr - 1 if di < 0 else pr)
            co = 0 if dj == 0 else (2 * pc + dj - 1) // 2
            found.append((3 * i + j, 2 * gr + gc, ro, co != 0))
    return found


def shifted(rows, pc):
    n = rows.shape[0]
    col = iota(rows.shape, 0) % 16
    if pc == 1:
        return jnp.where(col == 0, 0.0, pltpu.roll(rows, 1, 0))
    return jnp.where(col == 15, 0.0, pltpu.roll(rows, n - 1, 0))


def norm_parts(v):
    mean = jnp.mean(v, axis=-1, keepdims=True)
    cen = v - mean
    inv = lax.rsqrt(jnp.mean(cen * cen, axis=-1, keepdims=True) + EPSILON)
    return cen * inv, inv


def norm_back(n, nrm, inv):
    m1 = jnp.mean(n, axis=-1, keepdims=True)
    m2 = jnp.mean(n * nrm, axis=-1, keepdims=True)
    return (n - m1 - nrm * m2) * inv


SCRATCH = dict(
    stg_t=((2, 4, 64, D), BF),
    stg_c=((2, 4, 64, D), BF),
    tok=((4, 256, D), BF),
    cot=((4, 256, D), BF),
    latc=((4, 1, 256), jnp.int32),
    lv=((4, 256, 128), F32),
    oh=((4, 256, 128), BF),
    modhl=((32, 6 * D), BF),
    pm=((256, 256), BF),
    ain=((4, 288, D), BF),
    c1t=((D, 1024), BF),
    tmpa=((4, 256, D), BF),
    qkv=((4, 256, 3 * HB), BF),
    att=((4, 256, D), BF),
    fint=((D, 1024), BF),
    bg=((4, 256, D), BF),
    mid=((2, 256, D), F32),
    ub=((4, 288, HB), BF),
    us=((4, 288, HB), BF),
    gb=((4, 288, HB), BF),
    gs=((4, 288, HB), BF),
    gp=((2, 256, D), F32),
    act=((4, 256, 2 * D), BF),
    upg=((4, 256, 2 * D), BF),
    actt=((HB, 1024), BF),
    wup=((D, 2 * D), BF),
    wdn=((2 * D, D), BF),
    wq=((D, 3 * HB), BF),
    wo=((D, D), BF),
    gwd=((4, HB, D), BF),
    gwu=((4, 192, 2 * D), BF),
    gwo=((4, 96, D), BF),
    rd_a=((192, D), BF),
    rd_b=((192, D), BF),
    rd_x=((HB, D), BF),
    rd_y=((HB, D), BF),
    ru_a=((96, 2 * D), BF),
    ru_b=((96, 2 * D), BF),
    ru_x=((192, 2 * D), BF),
    ru_y=((192, 2 * D), BF),
    rq_a=((96, 3 * HB), BF),
    rq_b=((96, 3 * HB), BF),
    rq_x=((192, 3 * HB), BF),
    rq_y=((192, 3 * HB), BF),
    ro_a=((48, D), BF),
    ro_b=((48, D), BF),
    ro_x=((96, D), BF),
    ro_y=((96, D), BF),
    su=((96, 2 * D), BF),
    sq=((96, 3 * HB), BF),
    zd_a=((HB, D), BF),
    zd_b=((HB, D), BF),
    zu_a=((96, FF), BF),
    zu_b=((96, FF), BF),
    zq_a=((96, 3 * D), BF),
    zq_b=((96, 3 * D), BF),
    zo_a=((96, D), BF),
    zo_b=((96, D), BF),
    frcv=((2, 4, 64, D), BF),
    brcv=((2, 4, 64, D), BF),
    oland=((2, 4, 64, D), BF),
    gland=((2, 4, 64, D), BF),
    condc=((16, D), F32),
    clow=((4, 16, D), BF),
    mg1=((16, D), F32),
    mg2=((16, HB), F32),
    mgs1=((16, D), BF),
    mgr1=((16, D), BF),
    mgs2=((16, HB), BF),
    mgr2=((16, HB), BF),
    mga1=((16, 16, D), BF),
    mga2=((16, 16, HB), BF),
    sg1=((16, FF), F32),
    sg1s=((1, 16, FF), BF),
    sg1r=((5, 16, FF), BF),
    sg2=((16, D), F32),
    sg2s=((1, 16, D), BF),
    sg2r=((5, 16, D), BF),
    cgsum=((16, D), F32),
    crcv=((2, 8, D), F32),
)
N_SEMS = 208


def whole_block(
    tok_h, cot_h, lat_h, cond_r, wada_h, par, wqkv_h, wout_h, wup_h, wdn_h,
    o_out, o_gin, o_cond, o_wada, o_bada, o_sg1, o_sg2, o_wqkv, o_wout, o_wup, o_wdn,
    sems, *bufs,
):
    v = SimpleNamespace(**dict(zip(SCRATCH, bufs)))
    stg_t, stg_c, tok, cot, latc, lv, oh = v.stg_t, v.stg_c, v.tok, v.cot, v.latc, v.lv, v.oh
    modhl, pm, ain, c1t, tmpa, qkv, att = v.modhl, v.pm, v.ain, v.c1t, v.tmpa, v.qkv, v.att
    fint, bg, mid, ub, us, gb, gs = v.fint, v.bg, v.mid, v.ub, v.us, v.gb, v.gs
    gp, act, upg, actt, wup, wdn, wq, wo = v.gp, v.act, v.upg, v.actt, v.wup, v.wdn, v.wq, v.wo
    gwd, gwu, gwo, condc, clow = v.gwd, v.gwu, v.gwo, v.condc, v.clow

    c = lax.axis_index("canvas")
    r = lax.axis_index("rows")
    k = c % 2
    x = (c // 2) % 2
    y = c // 4
    col = 2 * y + x
    r1 = r + 1 - 2 * (r % 2)
    r2 = (r + 2) % 4
    r3 = 3 - r
    sib = (y * 4 + x * 2 + 1 - k, r)
    px = (y * 4 + (1 - x) * 2 + k, r)
    py = ((1 - y) * 4 + x * 2 + k, r)
    owner = r // 2
    is_own = k == owner
    owner_c = y * 4 + x * 2 + owner

    count = [0]

    def sem(n=1):
        first = count[0]
        count[0] += n
        return first

    last = []

    def remote(src, dst, ss, rs, dev):
        return pltpu.make_async_remote_copy(
            src_ref=src, dst_ref=dst, send_sem=sems.at[ss], recv_sem=sems.at[rs],
            device_id=dev, device_id_type=pl.DeviceIdType.MESH,
        )

    def local(src, dst, s):
        return pltpu.make_async_copy(src, dst, sems.at[s])

    def swap(src, dst, dev):
        cp = remote(src, dst, sem(), sem(), dev)
        cp.start()
        last.append(cp.wait_send)
        return cp

    barrier = pltpu.get_barrier_semaphore()
    for dev in (sib, px, py, (c, r1), (c, r2), (c, r3), (sib[0], r1), (sib[0], r2), (sib[0], r3)):
        pl.semaphore_signal(barrier, inc=1, device_id=dev, device_id_type=pl.DeviceIdType.MESH)
    s_tok = sem()
    s_cot = sem()
    ld_tok = local(tok_h, act.at[pl.ds(0, 2), :, pl.ds(0, D)], s_tok)
    ld_tok.start()
    ld_cot = local(cot_h, act.at[pl.ds(0, 2), :, pl.ds(D, D)], s_cot)
    ld_cot.start()
    s_wa = sem(2)

    def load_ada(p):
        return local(wada_h.at[:, pl.ds(p * D, D)], wup.at[:, pl.ds((p % 2) * D, D)], s_wa + p % 2)

    load_ada(0).start()
    load_ada(1).start()
    s_w = sem(3)
    ld_wq = [
        local(wqkv_h.at[:, pl.ds(pl.multiple_of(part * D + HB * k, 128), HB)], wq.at[:, pl.ds(part * HB, HB)], s_w + part)
        for part in range(3)
    ]
    for cp in ld_wq:
        cp.start()
    ld_wo = local(wout_h, wo, sem())
    ld_wo.start()
    s_wd = sem(4)
    ld_wd = [
        local(wdn_h.at[pl.ds(pl.multiple_of(HB * (2 * b + k), 128), HB), :], wdn.at[pl.ds(HB * b, HB), :], s_wd + b)
        for b in range(4)
    ]
    for cp in ld_wd:
        cp.start()
    pi = iota((256, 256), 0)
    group, place = pi // 64, pi % 64
    nat = (2 * (place // 16) + group // 2) * 32 + 2 * (place % 16) + group % 2
    pm[...] = ones_where(iota((256, 256), 1) == nat)
    for buf in (ain, ub, us, gb, gs):
        wide = buf.shape[2]
        for g in range(4):
            buf[g, 0:16, :] = jnp.zeros((16, wide), BF)
            buf[g, 272:288, :] = jnp.zeros((16, wide), BF)
    condc[pl.ds(pl.multiple_of(8 * k, 8), 8), :] = cond_r[...]
    pl.semaphore_wait(barrier, 9)

    cond_cp = swap(
        condc.at[pl.ds(pl.multiple_of(8 * k, 8), 8), :], condc.at[pl.ds(pl.multiple_of(8 * k, 8), 8), :], sib
    )
    mine64 = pl.ds(pl.multiple_of(r * 64, 64), 64)
    rt, rl, rc = sem(4), sem(4), sem(4)
    st, sl, sc = sem(2), sem(2), sem(2)

    def give(src, dst, ss, rs, i):
        q = 2 * k + i
        far = remote(src, dst, ss, rs, (c, q))
        near = local(src, dst, rs)

        @pl.when(q != r)
        def _():
            far.start()

        @pl.when(q == r)
        def _():
            near.start()

        def done():
            @pl.when(q != r)
            def _():
                far.wait_send()

        return done

    tok_sent, cot_sent = [], []
    ld_tok.wait()
    for i in range(2):
        stg_t[i] = dot(pm[...], act[i, :, 0:D]).astype(BF).reshape(4, 64, D)
        tok_sent.append(give(stg_t.at[i], tok.at[:, mine64, :], st + i, rt + r, i))
        last.append(give(lat_h.at[i], latc.at[r], sl + i, rl + r, i))
    ld_cot.wait()
    for i in range(2):
        stg_c[i] = dot(pm[...], act[i, :, D : 2 * D]).astype(BF).reshape(4, 64, D)
        cot_sent.append(give(stg_c.at[i], cot.at[:, mine64, :], sc + i, rc + r, i))

    cond_cp.wait_recv()
    cond = condc[...]
    sig = 1.0 / (1.0 + jnp.exp(-cond))
    mine_low = (cond * sig).astype(BF)
    clow[col] = mine_low
    low_x = swap(clow.at[col], clow.at[col], px)
    for p in range(6):
        load_ada(p).wait()
        mod = dot(mine_low, wup[:, (p % 2) * D : (p % 2) * D + D])
        mod = mod + par[14 + p // 4 : 15 + p // 4, (p % 4) * D : (p % 4) * D + D]
        high = mod.astype(BF)
        modhl[0:16, p * D : (p + 1) * D] = high
        modhl[16:32, p * D : (p + 1) * D] = (mod - high.astype(F32)).astype(BF)
        if p + 2 < 6:
            load_ada(p + 2).start()
    s_wu = sem(4)
    ld_wu = [
        local(wup_h.at[:, pl.ds(pl.multiple_of(HB * (2 * b + k), 128), HB)], wup.at[:, pl.ds(HB * b, HB)], s_wu + b)
        for b in range(4)
    ]
    for cp in ld_wu:
        cp.start()

    def piece(o, p):
        return dot(o[:, 0:32], modhl[:, p * D : (p + 1) * D])

    ft, fl, fc = sem(4), sem(4), sem(4)
    order = (r, r1, r2, r3)

    def arrive(buf, of, rs, fs):
        passed = []
        for d in range(4):
            s = order[d]
            place = of(s)
            cp = remote(buf.at[place], buf.at[place], fs + d, rs + s, sib)
            cp.wait_recv()

            @pl.when(is_own)
            def _():
                cp.start()

            def done(cp=cp):
                @pl.when(is_own)
                def _():
                    cp.wait_send()

            passed.append(done)
        return passed

    def slab(s):
        return (slice(None), pl.ds(pl.multiple_of(s * 64, 64), 64), slice(None))

    last.extend(arrive(latc, lambda s: s, rl, fl))
    tok_passed = arrive(tok, slab, rt, ft)

    for s in range(4):
        rows = jnp.broadcast_to(latc[s].astype(F32), (128, 256)).astype(BF)
        ids = dot_t(pm[...], rows)
        for g in range(4):
            lv[g, s * 64 : s * 64 + 64, :] = ids[g * 64 : g * 64 + 64]
    for g in range(4):
        lane = iota((256, 128), 1)
        want = (lane % 16 - 4 * r).astype(F32)
        oh[g] = ones_where((want == lv[g]) & (lane < 32))

    def norm_one(n, _):
        t0 = pl.multiple_of((n % 2) * 128, 128)
        for pc in range(2):
            g = 2 * (n // 2) + pc
            nrm, _inv = norm_parts(tok[g, pl.ds(t0, 128), :].astype(F32))
            o = oh[g, pl.ds(t0, 128), :]
            h = (nrm * (1.0 + piece(o, 1)) + piece(o, 0)).astype(BF)
            ain[g, pl.ds(t0 + 16, 128), :] = h
            sh = shifted(h.astype(F32), pc).astype(BF)
            us[g, pl.ds(t0 + 16, 128), :] = sh[:, 0:HB]
            gs[g, pl.ds(t0 + 16, 128), :] = sh[:, HB:D]
        return 0

    lax.fori_loop(0, 4, norm_one, 0)

    for hh in range(2):
        side = us if hh == 0 else gs

        def conv_one(lt, _, hh=hh, side=side):
            l0 = pl.multiple_of(lt * 128, 128)
            la = pl.multiple_of(hh * HB + lt * 128, 128)
            kr = [par[11 + t // 4 : 12 + t // 4, pl.ds((t % 4) * D + la, 128)] for t in range(9)]
            for g in range(4):
                for h in range(2):
                    acc = None
                    for t, gsrc, ro, moved in taps_of(g // 2, g % 2, False):
                        rows = pl.ds(16 + 16 * ro + 128 * h, 128)
                        src = side[gsrc, rows, pl.ds(l0, 128)] if moved else ain[gsrc, rows, pl.ds(la, 128)]
                        term = src.astype(F32) * kr[t]
                        acc = term if acc is None else acc + term
                    low = acc.astype(BF)
                    tmpa[g, h * 128 : h * 128 + 128, pl.ds(la, 128)] = low
                    c1t[pl.ds(la, 128), g * 256 + h * 128 : g * 256 + h * 128 + 128] = low.astype(F32).T.astype(BF)
            return 0

        lax.fori_loop(0, 3, conv_one, 0)

    for cp in ld_wq:
        cp.wait()
    kcol = pl.multiple_of(HB * k, 128)
    b_q = par[10:11, pl.ds(2 * D + kcol, HB)]
    b_v = par[10:11, pl.ds(3 * D + kcol, HB)]

    def project(g, _):
        got = dot(tmpa[g], wq[...])
        qkv[g, :, 0:HB] = ((got[:, 0:HB] + b_q).astype(BF).astype(F32) * 0.125).astype(BF)
        qkv[g, :, HB : 2 * HB] = got[:, HB : 2 * HB].astype(BF)
        qkv[g, :, 2 * HB : 3 * HB] = (got[:, 2 * HB : 3 * HB] + b_v).astype(BF)
        return 0

    lax.fori_loop(0, 4, project, 0)

    lane1 = iota((1, 128), 1)
    lmf = [jnp.where(lane1 < 64, 1.0, 0.0), jnp.where(lane1 < 64, 0.0, 1.0)]
    lmb = [m.astype(BF) for m in lmf]
    sa, ra = sem(4), sem(4)

    def masks_of(g):
        lane = iota((256, 128), 1)
        same = lane.astype(F32) == lv[g]
        oq = jnp.where(same & (lane < 4), 1.0, 0.0).astype(BF)
        mk = jnp.where(same | (lane >= 4), 0.0, BIG).astype(BF)
        return oq, mk

    def att_copy(g):
        place = att.at[g, :, pl.ds(kcol, HB)]
        return remote(place, place, sa + g, ra + g, sib)

    def attend(g, _):
        oq, mk = masks_of(g)
        for hp in range(3):
            qp = qkv[g, :, hp * 128 : hp * 128 + 128]
            ka = jnp.concatenate([qkv[g, :, HB + hp * 128 : HB + hp * 128 + 128], mk], axis=1)
            vp = qkv[g, :, 2 * HB + hp * 128 : 2 * HB + hp * 128 + 128]
            mixed = None
            for h in range(2):
                s = dot_t(jnp.concatenate([qp * lmb[h], oq], axis=1), ka)
                e = jnp.exp(s - jnp.max(s, axis=1, keepdims=True))
                o = dot(e.astype(BF), vp) * (lmf[h] / jnp.sum(e, axis=1, keepdims=True))
                mixed = o if h == 0 else mixed + o
            att[g, :, pl.ds(pl.multiple_of(kcol + hp * 128, 128), 128)] = mixed.astype(BF)
        att_copy(g).start()
        return 0

    lax.fori_loop(0, 4, attend, 0)
    low_x.wait_recv()
    low_y = swap(clow.at[pl.ds(2 * y, 2)], clow.at[pl.ds(2 * y, 2)], py)
    last.extend(arrive(cot, slab, rc, fc))

    ld_wo.wait()
    kother = pl.multiple_of(HB * (1 - k), 128)

    def norm_two(g, _):
        for h in range(2):
            rows = slice(h * 128, h * 128 + 128)
            a = att[g, rows, :]
            ao = dot(a, wo[...]) + par[10:11, D : 2 * D]
            o = oh[g, rows, :]
            m = tok[g, rows, :].astype(F32) + piece(o, 2) * ao
            nrm, _inv = norm_parts(m)
            f = (nrm * (1.0 + piece(o, 4)) + piece(o, 3)).astype(BF)
            tmpa[g, rows, :] = f
            at = pl.ds(pl.multiple_of(g * 256 + h * 128, 128), 128)
            fint[:, at] = f.astype(F32).T.astype(BF)
            bg[g, rows, :] = (piece(o, 5) * cot[g, rows, :].astype(F32)).astype(BF)
        return 0

    for g in range(4):
        att_copy(g).wait()
    lax.fori_loop(0, 4, norm_two, 0)

    class Scatter:
        def __init__(self, src, a, b, rx, ry):
            self.src, self.a, self.b, self.rx, self.ry = src, a, b, rx, ry
            n = a.shape[0]
            self.n = n
            ss = sem(8)
            wide = a.shape[1]
            ln = pl.ds(0, wide)
            self.ln = slice(0, wide)
            self.ca = remote(src.at[0, pl.ds(0, n), ln], a, ss, ss + 1, px)
            self.cb = remote(src.at[0, pl.ds(n, n), ln], b, ss + 2, ss + 3, py)
            self.cx = remote(src.at[1, :, ln], rx, ss + 4, ss + 5, px)
            self.cy = remote(src.at[2, :, ln], ry, ss + 6, ss + 7, py)

        def s0(self):
            self.ca.start()
            self.cb.start()

        def s1(self):
            self.cb.wait_recv()
            n = self.n
            self.src[1, n : 2 * n, self.ln] = (
                self.src[1, n : 2 * n, self.ln].astype(F32) + self.b[...].astype(F32)
            ).astype(BF)
            self.cx.start()

        def s2(self):
            self.ca.wait_recv()
            n = self.n
            self.src[2, 0:n, self.ln] = (self.src[2, 0:n, self.ln].astype(F32) + self.a[...].astype(F32)).astype(BF)
            self.cy.start()

        def s3(self):
            self.cx.wait_recv()
            self.cy.wait_recv()
            return self.src[3, :, self.ln].astype(F32) + self.rx[...].astype(F32) + self.ry[...].astype(F32)

        def sent(self):
            for cp in (self.ca, self.cb, self.cx, self.cy):
                cp.wait_send()

    inner = (r % 3) != 0

    class Line:
        def __init__(self, out, za, zb):
            self.out, self.za, self.zb = out, za, zb
            ss = sem(6)
            self.up = remote(out, za, ss, ss + 1, (c, r1))
            self.mid = remote(out, zb, ss + 2, ss + 3, (c, r3))
            self.down = remote(out, za, ss + 4, ss + 5, (c, r1))

        def s0(self):
            @pl.when(jnp.logical_not(inner))
            def _():
                self.up.start()

        def s1(self):
            @pl.when(inner)
            def _():
                self.up.wait_recv()
                self.out[...] = (self.out[...].astype(F32) + self.za[...].astype(F32)).astype(BF)
                self.mid.start()

        def s2(self):
            @pl.when(inner)
            def _():
                self.mid.wait()
                self.out[...] = (self.out[...].astype(F32) + self.zb[...].astype(F32)).astype(BF)
                self.down.start()

        def s3(self):
            @pl.when(inner)
            def _():
                self.down.wait_send()

            @pl.when(jnp.logical_not(inner))
            def _():
                self.up.wait_send()
                self.down.wait_recv()
                self.out[...] = self.za[...]

    class Everyone:
        def __init__(self, total, send, recv):
            self.total, self.send, self.recv = total, send, recv
            ss = sem(10)
            devs = (sib, px, py, (c, r1), (c, r2))
            self.cps = [remote(send.at[0], recv.at[i], ss + 2 * i, ss + 2 * i + 1, devs[i]) for i in range(5)]

        def go(self, i):
            self.send[0] = self.total[...].astype(BF)
            self.cps[i].start()

        def end(self, i):
            self.cps[i].wait()
            self.total[...] = self.send[0].astype(F32) + self.recv[i].astype(F32)

    sum_d = Scatter(gwd, v.rd_a, v.rd_b, v.rd_x, v.rd_y)
    sum_u = Scatter(gwu, v.ru_a, v.ru_b, v.ru_x, v.ru_y)
    sum_o = Scatter(gwo, v.ro_a, v.ro_b, v.ro_x, v.ro_y)
    sum_q = Scatter(gwu, v.rq_a, v.rq_b, v.rq_x, v.rq_y)
    line_d = Line(o_wdn, v.zd_a, v.zd_b)
    line_u = Line(o_wup, v.zu_a, v.zu_b)
    line_o = Line(o_wout, v.zo_a, v.zo_b)
    line_q = Line(o_wqkv, v.zq_a, v.zq_b)
    sg1, sg2 = v.sg1, v.sg2
    all1 = Everyone(sg1, v.sg1s, v.sg1r)
    all2 = Everyone(sg2, v.sg2s, v.sg2r)
    sg1[...] = jnp.zeros((16, FF), F32)
    sg2[...] = jnp.zeros((16, D), F32)

    def block_at(pos):
        fx = 1 - pos // 2
        fy = 1 - pos % 2
        bx = x + fx - 2 * x * fx
        by = y + fy - 2 * y * fy
        return 2 * by + bx

    for cp in ld_wd + ld_wu:
        cp.wait()

    def hidden(pos, _):
        b = block_at(pos)
        lo = pl.multiple_of(b * HB, 128)
        wide = pl.multiple_of(HB * (2 * b + k), 128)

        def up(pr, _):
            for pc in range(2):
                g = 2 * pr + pc
                u = (dot(tmpa[g], wup[:, pl.ds(lo, HB)]) + par[9:10, pl.ds(wide, HB)]).astype(BF)
                ub[g, 16:272, :] = u
                us[g, 16:272, :] = shifted(u.astype(F32), pc).astype(BF)
            return 0

        lax.fori_loop(0, 2, up, 0)

        def conv_gelu(lt, _):
            l0 = pl.multiple_of(lt * 128, 128)
            ln = pl.ds(l0, 128)
            kr = [par[t : t + 1, pl.ds(wide + l0, 128)] for t in range(9)]
            for g in range(4):
                for h in range(2):
                    acc = None
                    for t, gsrc, ro, moved in taps_of(g // 2, g % 2, False):
                        src = (us if moved else ub)[gsrc, pl.ds(16 + 16 * ro + 128 * h, 128), ln]
                        term = src.astype(F32) * kr[t]
                        acc = term if acc is None else acc + term
                    sq = acc * acc
                    th = jnp.tanh(0.7978845608028654 * acc * (1.0 + 0.044715 * sq))
                    half = 0.5 + 0.5 * th
                    low = (acc * half).astype(BF)
                    slope = half + half * (1.0 - th) * acc * (0.7978845608028654 + 0.10703222440890037 * sq)
                    rows = slice(h * 128, h * 128 + 128)
                    act[g, rows, pl.ds(lo + l0, 128)] = low
                    gp[g // 2, rows, pl.ds((g % 2) * HB + l0, 128)] = slope
                    actt[ln, g * 256 + h * 128 : g * 256 + h * 128 + 128] = low.astype(F32).T.astype(BF)
            return 0

        lax.fori_loop(0, 3, conv_gelu, 0)

        def down_grad(pr, _):
            for pc in range(2):
                g = 2 * pr + pc
                t = dot_t(bg[g], wdn[pl.ds(lo, HB), :]) * gp[pr, :, pc * HB : pc * HB + HB]
                t = t.astype(BF)
                gb[g, 16:272, :] = t
                gs[g, 16:272, :] = shifted(t.astype(F32), pc).astype(BF)
            return 0

        lax.fori_loop(0, 2, down_grad, 0)

        def conv_back(lt, _):
            l0 = pl.multiple_of(lt * 128, 128)
            ln = pl.ds(l0, 128)
            kr = [par[t : t + 1, pl.ds(wide + l0, 128)] for t in range(9)]
            gk = [jnp.zeros((8, 128), F32) for _ in range(10)]
            for g in range(4):
                for h in range(2):
                    here = ub[g, 16 + 128 * h : 144 + 128 * h, ln].astype(F32)
                    acc = None
                    for t, gsrc, ro, moved in taps_of(g // 2, g % 2, True):
                        src = (gs if moved else gb)[gsrc, pl.ds(16 + 16 * ro + 128 * h, 128), ln].astype(F32)
                        term = src * kr[t]
                        acc = term if acc is None else acc + term
                        gk[t] = gk[t] + jnp.sum((src * here).reshape(16, 8, 128), axis=0)
                    low = acc.astype(BF)
                    upg[g, h * 128 : h * 128 + 128, pl.ds(lo + l0, 128)] = low
                    gk[9] = gk[9] + jnp.sum(low.astype(F32).reshape(16, 8, 128), axis=0)
            for t in range(10):
                sg1[t : t + 1, pl.ds(wide + l0, 128)] = jnp.sum(gk[t], axis=0, keepdims=True)
            return 0

        lax.fori_loop(0, 3, conv_back, 0)

        def grad_down(n, _):
            rows = pl.ds(pl.multiple_of(n * 128, 128), 128)
            gwd[pos, rows, :] = dot(actt[rows, :], bg[...].reshape(1024, D)).astype(BF)
            return 0

        lax.fori_loop(0, 3, grad_down, 0)
        pl.when(pos == 0)(sum_d.s0)
        pl.when(pos == 1)(sum_d.s1)
        pl.when(pos == 2)(sum_d.s2)
        return 0

    lax.fori_loop(0, 4, hidden, 0)

    for done in tok_sent + cot_sent:
        done()

    def give_half(jj, _):
        g = 2 * (1 - k) + jj
        stg_t[jj] = dot_t(upg[g], wup[...]).astype(BF).reshape(4, 64, D)
        return 0

    lax.fori_loop(0, 2, give_half, 0)
    f_cp = remote(stg_t, v.frcv, sem(), sem(), sib)
    f_cp.start()

    def give_branch(jj, _):
        g = 2 * (1 - k) + jj
        stg_c[jj] = dot(act[g], wdn[...]).astype(BF).reshape(4, 64, D)
        return 0

    lax.fori_loop(0, 2, give_branch, 0)
    b_cp = remote(stg_c, v.brcv, sem(), sem(), sib)
    b_cp.start()

    def grad_up(pos, _):
        b = block_at(pos)
        rows = pl.ds(pl.multiple_of(b * 192, 64), 192)

        def part(nt, _):
            ln = pl.ds(pl.multiple_of(nt * HB, 128), HB)
            gwu[pos, :, ln] = dot(fint[rows, :], upg[:, :, ln].reshape(1024, HB)).astype(BF)
            return 0

        lax.fori_loop(0, 4, part, 0)
        pl.when(pos == 0)(sum_u.s0)
        return 0

    lax.fori_loop(0, 4, grad_up, 0)
    f_cp.wait()
    b_cp.wait()

    mg1, mg2 = v.mg1, v.mg2
    mg1[...] = jnp.zeros((16, D), F32)
    mg2[...] = jnp.zeros((16, HB), F32)
    o_rows = jnp.zeros((1, D), F32)

    def place_rows(ids, p):
        lane = iota((128, 128), 1)
        return ones_where((lane - 4 * p).astype(F32) == ids)

    def two_back(n, carry):
        bd, bo = carry
        jj = n // 2
        g = 2 * k + jj
        t0 = pl.multiple_of((n % 2) * 128, 128)
        rows = pl.ds(t0, 128)
        h64 = pl.ds((n % 2) * 2, 2)
        o = oh[g, rows, :]
        gate1 = piece(o, 2)
        ao = dot(att[g, rows, :], wo[...]) + par[10:11, D : 2 * D]
        m = tok[g, rows, :].astype(F32) + gate1 * ao
        nrm, inv = norm_parts(m)
        fg = dot_t(upg[g, rows, :], wup[...]) + v.frcv[jj, h64].reshape(128, D).astype(F32)
        cotf = cot[g, rows, :].astype(F32)
        mg = cotf + norm_back(fg * (1.0 + piece(o, 4)), nrm, inv)
        mid[jj, rows, :] = mg
        ag = (gate1 * mg).astype(BF)
        tmpa[g, rows, :] = ag
        branch = dot(act[g, rows, :], wdn[...]) + v.brcv[jj, h64].reshape(128, D).astype(F32) + par[10:11, 0:D]
        stg_c[jj, h64] = (m + piece(o, 5) * branch).astype(BF).reshape(2, 64, D)
        ids = lv[g, rows, :]
        total = dot_l(place_rows(ids, 0), (mg * ao).astype(BF))
        total = total + dot_l(place_rows(ids, 1), fg.astype(BF))
        total = total + dot_l(place_rows(ids, 2), (fg * nrm).astype(BF))
        total = total + dot_l(place_rows(ids, 3), (cotf * branch).astype(BF))
        mg1[...] += total[0:16]
        bd = bd + jnp.sum(bg[g, rows, :].astype(F32), axis=0, keepdims=True)
        bo = bo + jnp.sum(ag.astype(F32), axis=0, keepdims=True)
        return bd, bo

    bd, bo = lax.fori_loop(0, 4, two_back, (o_rows, o_rows))
    ag_place = tmpa.at[pl.ds(2 * k, 2)]
    ag_cp = swap(ag_place, ag_place, sib)
    sg1[10:11, 0:D] = bd
    sg1[10:11, D : 2 * D] = bo

    def hand_back(src, land, rs):
        ss = sem(4)
        for s in range(4):
            dst = land.at[r % 2, pl.ds(2 * k, 2)]
            at = rs + (r % 2) * 2 + k
            far = remote(src.at[:, s], dst, ss + s, at, (owner_c, s))
            near = local(src.at[:, s], dst, at)
            here = is_own & (r == s)

            @pl.when(jnp.logical_not(here))
            def _(far=far):
                far.start()

            @pl.when(here)
            def _(near=near):
                near.start()

            def done(far=far, here=here):
                @pl.when(jnp.logical_not(here))
                def _():
                    far.wait_send()

            last.append(done)

    def landed(land, rs, out, first):
        for i in range(2):
            for kk in range(2):
                place = land.at[i, pl.ds(2 * kk, 2)]
                local(place, place, rs + 2 * i + kk).wait()
        for i in range(2):
            tok[first + i] = dot_l(pm[...], land[i].reshape(256, D)).astype(BF)
        cp = local(tok.at[pl.ds(first, 2)], out, sem())
        cp.start()
        last.append(cp.wait)

    ro_out, ro_gin = sem(4), sem(4)
    hand_back(stg_c, v.oland, ro_out)
    sum_u.s1()
    sum_u.s2()
    o_wdn[...] = sum_d.s3().astype(BF)
    line_d.s0()
    mgs1, mgr1 = v.mgs1, v.mgr1
    mgs1[...] = mg1[...].astype(BF)
    mg_cp = swap(mgs1, mgr1, sib)
    all1.go(0)

    ag_cp.wait_recv()
    dqkv = act
    kr_rows = pl.ds(kcol, HB)

    def heads_back(g, _):
        oq, mk = masks_of(g)
        for h in range(2):
            at = pl.ds(pl.multiple_of(g * 256 + h * 128, 128), 128)
            fint[:, at] = att[g, h * 128 : h * 128 + 128, :].astype(F32).T.astype(BF)
        act[g, :, 3 * HB : 4 * HB] = dot_t(tmpa[g], wo[kr_rows, :]).astype(BF)
        for hp in range(3):
            qp = qkv[g, :, hp * 128 : hp * 128 + 128]
            kp = qkv[g, :, HB + hp * 128 : HB + hp * 128 + 128]
            vp = qkv[g, :, 2 * HB + hp * 128 : 2 * HB + hp * 128 + 128]
            dop = act[g, :, 3 * HB + hp * 128 : 3 * HB + hp * 128 + 128]
            ka = jnp.concatenate([kp, mk], axis=1)
            dq = dk = dv = None
            for h in range(2):
                s = dot_t(ka, jnp.concatenate([qp * lmb[h], oq], axis=1))
                e = jnp.exp(s - jnp.max(s, axis=0, keepdims=True))
                prob = e * (1.0 / jnp.sum(e, axis=0, keepdims=True))
                dp = dot_t(vp * lmb[h], dop)
                delta = jnp.sum(prob * dp, axis=0, keepdims=True)
                ds = (prob * (dp - delta)).astype(BF)
                dv_h = dot(prob.astype(BF), dop) * lmf[h]
                dk_h = dot(ds, qp) * lmf[h]
                dq_h = dot_l(ds, kp) * (lmf[h] * 0.125)
                dv = dv_h if h == 0 else dv + dv_h
                dk = dk_h if h == 0 else dk + dk_h
                dq = dq_h if h == 0 else dq + dq_h
            dqkv[g, :, hp * 128 : hp * 128 + 128] = dq.astype(BF)
            dqkv[g, :, HB + hp * 128 : HB + hp * 128 + 128] = dk.astype(BF)
            dqkv[g, :, 2 * HB + hp * 128 : 2 * HB + hp * 128 + 128] = dv.astype(BF)
        return 0

    lax.fori_loop(0, 4, heads_back, 0)

    def proj_back(g, _):
        upg[g, :, 0:D] = dot_t(dqkv[g, :, 0 : 3 * HB], wq[...]).astype(BF)
        return 0

    lax.fori_loop(0, 4, proj_back, 0)
    cg_cp = swap(upg.at[:, :, pl.ds(0, D)], bg, sib)

    def grad_out(pos, _):
        rows = pl.ds(pl.multiple_of(96 * (2 * block_at(pos) + k), 32), 96)
        gwo[pos] = dot(fint[rows, :], tmpa[...].reshape(1024, D)).astype(BF)
        pl.when(pos == 0)(sum_o.s0)
        return 0

    lax.fori_loop(0, 4, grad_out, 0)
    total_u = sum_u.s3()
    gwu[3] = total_u.astype(BF)
    half_u = swap(
        gwu.at[3, pl.ds(pl.multiple_of(96 * (1 - k), 32), 96), :], v.su, sib
    )
    mine96 = pl.ds(pl.multiple_of(96 * k, 32), 96)
    for b in range(4):
        o_wup[:, pl.ds(pl.multiple_of(HB * (2 * b + k), 128), HB)] = gwu[3, mine96, b * HB : (b + 1) * HB]
    half_u.wait()
    last.remove(half_u.wait_send)
    for b in range(4):
        o_wup[:, pl.ds(pl.multiple_of(HB * (2 * b + 1 - k), 128), HB)] = v.su[:, b * HB : (b + 1) * HB]
    line_u.s0()
    line_d.s1()
    sum_o.s1()
    sum_o.s2()
    sum_u.sent()
    all1.end(0)
    all1.go(1)

    def grad_qkv(pos, _):
        rows = pl.ds(pl.multiple_of(192 * block_at(pos), 64), 192)

        def part(nt, _):
            ln = pl.ds(pl.multiple_of(nt * HB, 128), HB)
            gwu[pos, :, ln] = dot(c1t[rows, :], dqkv[:, :, ln].reshape(1024, HB)).astype(BF)
            return 0

        lax.fori_loop(0, 3, part, 0)
        pl.when(pos == 0)(sum_q.s0)
        return 0

    lax.fori_loop(0, 4, grad_qkv, 0)
    line_d.s2()
    line_u.s1()
    sg2[9:10, pl.ds(kcol, HB)] = jnp.sum(
        jnp.sum(dqkv[:, :, 0:HB].astype(F32), axis=0), axis=0, keepdims=True
    )
    sg2[10:11, pl.ds(kcol, HB)] = jnp.sum(
        jnp.sum(dqkv[:, :, 2 * HB : 3 * HB].astype(F32), axis=0), axis=0, keepdims=True
    )
    cg_cp.wait_recv()

    def cg_sum(pr, _):
        for pc in range(2):
            g = 2 * pr + pc
            t = (upg[g, :, 0:D].astype(F32) + bg[g].astype(F32)).astype(BF)
            sh = shifted(t.astype(F32), pc).astype(BF)
            ub[g, 16:272, :] = t[:, 0:HB]
            gb[g, 16:272, :] = t[:, HB:D]
            us[g, 16:272, :] = sh[:, 0:HB]
            gs[g, 16:272, :] = sh[:, HB:D]
        return 0

    lax.fori_loop(0, 2, cg_sum, 0)
    for hh in range(2):
        base, side = (ub, us) if hh == 0 else (gb, gs)

        def conv_one_back(lt, _, hh=hh, base=base, side=side):
            l0 = pl.multiple_of(lt * 128, 128)
            la = pl.multiple_of(hh * HB + lt * 128, 128)
            kr = [par[11 + t // 4 : 12 + t // 4, pl.ds((t % 4) * D + la, 128)] for t in range(9)]
            gk = [jnp.zeros((8, 128), F32) for _ in range(9)]
            for pc in range(2):
                for h in range(2):
                    here = ain[2 * k + pc, 16 + 128 * h : 144 + 128 * h, pl.ds(la, 128)].astype(F32)
                    acc = None
                    for t, gsrc, ro, moved in taps_of(k, pc, True):
                        at = pl.ds(pl.multiple_of(16 + 16 * ro + 128 * h, 16), 128)
                        src = (side if moved else base)[gsrc, at, pl.ds(l0, 128)].astype(F32)
                        term = src * kr[t]
                        acc = term if acc is None else acc + term
                        gk[t] = gk[t] + jnp.sum((src * here).reshape(16, 8, 128), axis=0)
                    gp[pc, h * 128 : h * 128 + 128, pl.ds(la, 128)] = acc
            for t in range(9):
                sg2[t : t + 1, pl.ds(la, 128)] = jnp.sum(gk[t], axis=0, keepdims=True)
            return 0

        lax.fori_loop(0, 3, conv_one_back, 0)
    all2.go(0)
    sum_q.s1()
    sum_q.s2()

    def one_back(n, _):
        jj = n // 2
        g = 2 * k + jj
        rows = pl.ds(pl.multiple_of((n % 2) * 128, 128), 128)
        h64 = pl.ds((n % 2) * 2, 2)
        nrm, inv = norm_parts(tok[g, rows, :].astype(F32))
        ig = gp[jj, rows, :]
        gi = mid[jj, rows, :] + norm_back(ig * (1.0 + piece(oh[g, rows, :], 1)), nrm, inv)
        stg_t[jj, h64] = gi.astype(BF).reshape(2, 64, D)
        ids = lv[g, rows, :]
        low = ig.astype(BF)
        scl = (ig * nrm).astype(BF)
        total = dot_l(place_rows(ids, 0), low[:, 0:HB]) + dot_l(place_rows(ids, 1), low[:, HB:D])
        total = total + dot_l(place_rows(ids, 2), scl[:, 0:HB]) + dot_l(place_rows(ids, 3), scl[:, HB:D])
        mg2[...] += total[0:16]
        return 0

    lax.fori_loop(0, 4, one_back, 0)
    hand_back(stg_t, v.gland, ro_gin)
    mgs2, mgr2 = v.mgs2, v.mgr2
    mgs2[...] = mg2[...].astype(BF)
    mg2_cp = swap(mgs2, mgr2, sib)

    o_wout[...] = sum_o.s3().astype(BF)
    line_o.s0()
    mg_cp.wait_recv()
    mga1, mga2 = v.mga1, v.mga2
    slot = 4 * col + r

    class Gather:
        def __init__(self, own, got, everyone):
            self.own, self.got, self.everyone = own, got, everyone
            self.zr, self.zs = sem(4), sem(3)
            self.xy = sem(4)

        def s0(self):
            self.everyone[slot] = (self.own[...].astype(F32) + self.got[...].astype(F32)).astype(BF)
            place = self.everyone.at[slot]
            for d, s in enumerate((r1, r2, r3)):
                cp = remote(place, place, self.zs + d, self.zr + r, (c, s))
                cp.start()
                last.append(cp.wait_send)

        def s1(self):
            for s in (r1, r2, r3):
                place = self.everyone.at[4 * col + s]
                local(place, place, self.zr + s).wait()
            place = self.everyone.at[pl.ds(4 * col, 4)]
            self.cx = remote(place, place, self.xy, self.xy + 1, px)
            self.cx.start()
            last.append(self.cx.wait_send)

        def s2(self):
            self.cx.wait_recv()
            place = self.everyone.at[pl.ds(8 * y, 8)]
            self.cy = remote(place, place, self.xy + 2, self.xy + 3, py)
            self.cy.start()
            last.append(self.cy.wait_send)

        def s3(self):
            self.cy.wait_recv()

    gat1 = Gather(mgs1, mgr1, mga1)
    gat2 = Gather(mgs2, mgr2, mga2)
    gat1.s0()
    all1.end(1)
    all1.go(2)
    mg2_cp.wait_recv()
    gat2.s0()
    all2.end(0)
    all2.go(1)
    gat1.s1()
    line_u.s2()
    line_d.s3()

    def load_again(p):
        return local(wada_h.at[:, pl.ds(p * D, D)], wup.at[:, pl.ds((p % 2) * D, D)], s_wa + p % 2)

    load_again(2).start()
    load_again(3).start()
    line_o.s1()
    gat2.s1()
    all1.end(2)
    all1.go(3)
    all2.end(1)
    all2.go(2)

    def pick(p):
        ri, ci = iota((16, 16), 0), iota((16, 16), 1)
        return ones_where((ri // 4 == r) & (ci == 4 * p + ri % 4))

    my1 = mga1[slot]
    my2 = mga2[slot]
    cg = jnp.zeros((16, D), F32)
    for p in range(2, 6):
        load_again(p).wait()
        lhs = dot(pick(p - 2), my1).astype(BF)
        cg = cg + dot_t(lhs, wup[:, (p % 2) * D : (p % 2) * D + D])
        load_again((p + 2) % 6).start()
    for p in range(2):
        load_again(p).wait()
        for h in range(2):
            lhs = dot(pick(2 * p + h), my2).astype(BF)
            cg = cg + dot_t(lhs, wup[:, p * D + h * HB : p * D + h * HB + HB])
    cond = condc[...]
    sig = 1.0 / (1.0 + jnp.exp(-cond))
    cgsum = v.cgsum
    cgsum[...] = cg * (sig * (1.0 + cond * (1.0 - sig)))
    crcv = v.crcv
    cr, cs = sem(2), sem(4)
    for s in range(4):
        src = cgsum.at[pl.ds(pl.multiple_of(8 * owner, 8), 8), :]
        dst = crcv.at[r % 2]
        far = remote(src, dst, cs + s, cr + r % 2, (c, s))
        near = local(src, dst, cr + r % 2)

        @pl.when(is_own & (r != s))
        def _(far=far):
            far.start()

        @pl.when(is_own & (r == s))
        def _(near=near):
            near.start()

        def done(far=far, s=s):
            @pl.when(is_own & (r != s))
            def _():
                far.wait_send()

        last.append(done)

    total_q = sum_q.s3()
    gwu[3, :, 0 : 3 * HB] = total_q.astype(BF)
    half_q = swap(
        gwu.at[3, pl.ds(pl.multiple_of(96 * (1 - k), 32), 96), pl.ds(0, 3 * HB)], v.sq, sib
    )
    for part in range(3):
        o_wqkv[:, pl.ds(pl.multiple_of(part * D + HB * k, 128), HB)] = gwu[3, mine96, part * HB : (part + 1) * HB]
    half_q.wait_recv()
    for part in range(3):
        o_wqkv[:, pl.ds(pl.multiple_of(part * D + HB * (1 - k), 128), HB)] = v.sq[:, part * HB : (part + 1) * HB]
    line_q.s0()
    line_u.s3()
    gat1.s2()
    line_o.s2()
    all1.end(3)
    all1.go(4)
    all2.end(2)
    all2.go(3)
    gat2.s2()
    line_q.s1()
    for done in tok_passed:
        done()
    landed(v.oland, ro_out, o_out, 0)

    low_y.wait_recv()
    ri, ci = iota((96, D), 0), iota((96, D), 1)
    cond_t = dot_t(ones_where(ci == 96 * c + ri), clow[...].reshape(64, D)).astype(BF)
    ej, en = iota((64, 256), 0), iota((64, 256), 1)
    bn = iota((8, 256), 1)

    def spread(p):
        return dot(cond_t, ones_where((en // 16 == ej // 4) & (en % 16 == 4 * p + ej % 4))).astype(BF)

    all1.end(4)
    o_sg1[...] = sg1[...]
    all2.end(3)
    all2.go(4)
    gat1.s3()
    o_bada[...] = jnp.zeros((8, D), F32)
    every1 = mga1[...].reshape(256, D)

    def ada_out(p):
        cp = local(wdn.at[pl.ds(96 * p, 96), :], o_wada.at[:, pl.ds(p * D, D)], sem())
        cp.start()
        last.append(cp.wait)

    for p in range(4):
        wdn[(p + 2) * 96 : (p + 3) * 96, :] = dot(spread(p), every1).astype(BF)
        ada_out(p + 2)
        o_bada[p + 2 : p + 3, :] = dot(ones_where((bn % 16) // 4 == p), every1)[0:1]
    line_o.s3()
    line_q.s2()
    gat2.s3()
    every2 = mga2[...].reshape(256, HB)
    for p in range(4):
        half = (p % 2) * HB
        wdn[p // 2 * 96 : p // 2 * 96 + 96, half : half + HB] = dot(spread(p), every2).astype(BF)
        o_bada[p // 2 : p // 2 + 1, (p % 2) * HB : (p % 2) * HB + HB] = dot(ones_where((bn % 16) // 4 == p), every2)[0:1]
    ada_out(0)
    ada_out(1)
    all2.end(4)
    o_sg2[...] = sg2[...]
    landed(v.gland, ro_gin, o_gin, 2)
    for i in range(2):
        local(crcv.at[i], crcv.at[i], cr + i).wait()
    o_cond[...] = crcv[0] + crcv[1]
    line_q.s3()
    for done in last:
        done()
    for s in (sum_d, sum_o, sum_q):
        s.sent()
    assert count[0] <= N_SEMS, count[0]


def fast_shards(
    tokens, latent, condition, w_ada, b_ada, conv_attn, w_qkv, bias_qv, w_out, b_out,
    w_up, b_up, conv_ffn, w_down, b_down, cotangent,
):
    f = lambda a: a.astype(F32)
    conv_rows = jnp.pad(f(conv_attn), ((0, 3), (0, 0))).reshape(3, 4 * D)
    ada_rows = jnp.pad(f(b_ada), (0, 2 * D)).reshape(2, 4 * D)
    par = jnp.concatenate(
        [
            f(conv_ffn),
            f(b_up)[None],
            jnp.concatenate([f(b_down), f(b_out), f(bias_qv)])[None],
            conv_rows,
            ada_rows,
        ]
    )
    anyspace = pl.BlockSpec(memory_space=pl.ANY)
    vm = pl.BlockSpec(memory_space=pltpu.VMEM)
    outs = (
        ((2, 256, D), BF),
        ((2, 256, D), BF),
        ((8, D), F32),
        ((96, 6 * D), BF),
        ((8, D), F32),
        ((16, FF), F32),
        ((16, D), F32),
        ((96, 3 * D), BF),
        ((96, D), BF),
        ((96, FF), BF),
        ((HB, D), BF),
    )
    out, gin, gcond, gwada, gbada, sg1, sg2, gwqkv, gwout, gwup, gwdn = pl.pallas_call(
        whole_block,
        out_shape=[jax.ShapeDtypeStruct(s, t) for s, t in outs],
        in_specs=[anyspace, anyspace, vm, vm, anyspace, vm, anyspace, anyspace, anyspace, anyspace],
        out_specs=[anyspace, anyspace, vm, anyspace] + [vm] * (len(outs) - 4),
        scratch_shapes=[pltpu.SemaphoreType.DMA((N_SEMS,))] + [pltpu.VMEM(s, t) for s, t in SCRATCH.values()],
        compiler_params=pltpu.CompilerParams(
            collective_id=0, has_side_effects=True, vmem_limit_bytes=VMEM_LIMIT
        ),
        name="block",
    )(tokens, cotangent, latent.reshape(2, 1, 256), condition.reshape(8, D), w_ada, par, w_qkv, w_out, w_up, w_down)
    c = lax.axis_index("canvas")

    def share(a, dim, n):
        return lax.dynamic_slice_in_dim(a, c * n, n, dim)

    bq = sg2[9:11].reshape(2 * D)
    return (
        out,
        f(gin),
        gcond.reshape(2, 4, D),
        f(gwada),
        share(gbada[0:6].reshape(6 * D), 0, 576),
        share(sg2[0:9], 1, 96),
        f(gwqkv),
        share(bq, 0, 192),
        f(gwout),
        share(sg1[10, D : 2 * D], 0, 96),
        f(gwup),
        share(sg1[9], 0, 384),
        share(sg1[0:9], 1, 384),
        f(gwdn),
        share(sg1[10, 0:D], 0, 96),
    )


def solution(mesh):
    placed = (
        P("canvas", "rows", None),
        P("canvas", "rows"),
        P("canvas", None, None),
        P(),
        P(),
        P(),
        P(),
        P(),
        P(),
        P(),
        P(),
        P(),
        P(),
        P(),
        P(),
        P("canvas", "rows", None),
    )
    fits = mesh.shape["rows"] == 4 and mesh.shape["canvas"] == 8
    return jax.shard_map(
        fast_shards if fits else shards,
        mesh=mesh,
        in_specs=placed,
        out_specs=(
            P("canvas", "rows", None),
            P("canvas", "rows", None),
            P("canvas", None, None),
            P("canvas", None),
            P("canvas"),
            P(None, "canvas"),
            P("canvas", None),
            P("canvas"),
            P("canvas", None),
            P("canvas"),
            P("canvas", None),
            P("canvas"),
            P(None, "canvas"),
            P("canvas", None),
            P("canvas"),
        ),
        check_vma=False,
    )
```

```python
from types import SimpleNamespace

import jax
import jax.numpy as jnp
from jax import lax
from jax.experimental import pallas as pl
from jax.experimental.pallas import tpu as pltpu
from jax.sharding import PartitionSpec as P

HEADS = 12
HEAD_DIM = 64
SIDE = 32


EPSILON = 1e-06
NEG_FILL = -1e30
PRECISE = lax.Precision.HIGHEST
VMEM_LIMIT = 65400 * 2**10


def padded_2(cells, sides, width):
    for axis, dim in sides:
        count = lax.axis_size(axis)
        ends = count - 1
        head = lax.slice_in_dim(cells, 0, width, axis=dim)
        tail = lax.slice_in_dim(cells, cells.shape[dim] - width, cells.shape[dim], axis=dim)
        cells = jnp.concatenate(
            [
                lax.ppermute(tail, axis, [(i, (i + 1) % count) for i in range(ends)]),
                cells,
                lax.ppermute(head, axis, [((i + 1) % count, i) for i in range(ends)]),
            ],
            axis=dim,
        )
    return cells


def passed_along(block, axis, distance):
    devices = range(lax.axis_size(axis))
    route = [((i - distance) % len(devices), i) for i in devices]
    return lax.ppermute(block, axis, route)


def layer_norm(values):
    centered = values - jnp.mean(values, axis=-1, keepdims=True)
    return centered * lax.rsqrt(jnp.mean(centered * centered, axis=-1, keepdims=True) + EPSILON)


def modulate_norm(values, shift, scale_part):
    return layer_norm(values) * (1.0 + scale_part) + shift


def gelu_tanh(values):
    return jax.nn.gelu(values, approximate=True)


def pad_columns(field):
    return jnp.pad(field, ((0, 0), (0, 0), (1, 1), (0, 0)))


def grid_taps(padded, kernel, rows_here, cols_here):
    summed = padded[:, 0:rows_here, 0:cols_here].astype(jnp.float32) * kernel[0]
    for tap_row in range(3):
        for tap_col in range(3):
            if tap_row + tap_col > 0:
                window = padded[
                    :, tap_row : tap_row + rows_here, tap_col : tap_col + cols_here
                ].astype(jnp.float32)
                summed = summed + window * kernel[3 * tap_row + tap_col]
    return summed


def kernel_grad(padded, grad_grid):
    rows_here = grad_grid.shape[1]
    cols_here = grad_grid.shape[2]
    grad_f = grad_grid.astype(jnp.float32)
    tap_sums = []
    for tap_row in range(3):
        for tap_col in range(3):
            window = padded[:, tap_row : tap_row + rows_here, tap_col : tap_col + cols_here].astype(
                jnp.float32
            )
            tap_sums.append(jnp.sum(window * grad_f, axis=(0, 1, 2)))
    return jnp.stack(tap_sums)


def to_groups(field, rows_here):
    canvases = field.shape[0]
    channels = field.shape[-1]
    shaped = field.reshape(canvases, rows_here // 2, 2, SIDE // 2, 2, channels)
    return shaped.transpose(0, 2, 4, 1, 3, 5).reshape(
        canvases, 4, rows_here // 2 * (SIDE // 2), channels
    )


def from_groups(field, rows_here):
    canvases = field.shape[0]
    channels = field.shape[-1]
    shaped = field.reshape(canvases, 2, 2, rows_here // 2, SIDE // 2, channels)
    return shaped.transpose(0, 3, 1, 4, 2, 5).reshape(canvases, rows_here * SIDE, channels)


def block_scores(query_heads, key_piece, query_lat, key_lat):
    canvases = key_piece.shape[0]
    count = key_piece.shape[2]
    key_heads = key_piece.reshape(canvases, 4, count, HEADS, HEAD_DIM)
    scores = jnp.einsum(
        "cgqhe,cgkhe->cghqk", query_heads, key_heads, preferred_element_type=jnp.float32
    ) * HEAD_DIM ** (-0.5)
    same_latent = query_lat[:, :, None, :, None] == key_lat[:, :, None, None, :]
    return (scores, same_latent, key_heads)


def shards(
    tokens,
    latent,
    condition,
    w_ada,
    b_ada,
    conv_attn,
    w_qkv,
    bias_qv,
    w_out,
    b_out,
    w_up,
    b_up,
    conv_ffn,
    w_down,
    b_down,
    cotangent,
):
    canvases = tokens.shape[0]
    local_tokens = tokens.shape[1]
    model_width = tokens.shape[2]
    ffn_width = w_up.shape[1]
    rows_here = local_tokens // SIDE
    group_len = local_tokens // 4
    score_scale = HEAD_DIM ** (-0.5)
    tokens_f = tokens.astype(jnp.float32)
    onehot = (latent[..., None] == jnp.arange(4)).astype(jnp.float32)
    silu_cond, silu_pull = jax.vjp(jax.nn.silu, condition)
    cond_low = silu_cond.astype(jnp.bfloat16)
    modulation = jnp.einsum(
        "ckd,df->ckf", cond_low, w_ada, preferred_element_type=jnp.float32
    ) + b_ada.astype(jnp.float32)
    per_token = jnp.einsum("cnk,ckf->cnf", onehot, modulation, precision=PRECISE)
    shift_one, scale_one, gate_one, shift_two, scale_two, gate_two = jnp.split(
        per_token, 6, axis=-1
    )
    h_one, norm_one_pull = jax.vjp(modulate_norm, tokens_f, shift_one, scale_one)
    attn_in = h_one.astype(jnp.bfloat16).reshape(canvases, rows_here, SIDE, model_width)
    attn_pad = pad_columns(padded_2(attn_in, (("rows", 1),), 1))
    conv_attn_f = conv_attn.astype(jnp.float32)
    conv_low = (
        grid_taps(attn_pad, conv_attn_f, rows_here, SIDE)
        .astype(jnp.bfloat16)
        .reshape(-1, model_width)
    )
    bias_full = jnp.concatenate(
        [bias_qv[:model_width], jnp.zeros((model_width,), jnp.bfloat16), bias_qv[model_width:]]
    ).astype(jnp.float32)
    projected = (jnp.dot(conv_low, w_qkv, preferred_element_type=jnp.float32) + bias_full).astype(
        jnp.bfloat16
    )
    grouped = to_groups(projected.reshape(canvases, local_tokens, 3 * model_width), rows_here)
    queries = grouped[..., :model_width]
    key_rows = grouped[..., model_width : 2 * model_width]
    value_rows = grouped[..., 2 * model_width :]
    lat_groups = to_groups(latent[..., None], rows_here)[..., 0]
    all_lat = lax.all_gather(lat_groups, "rows", axis=2, tiled=True)
    query_heads = queries.reshape(canvases, 4, group_len, HEADS, HEAD_DIM)
    start_best = jnp.full((canvases, 4, HEADS, group_len), NEG_FILL, jnp.float32)
    best = start_best
    key_piece = lax.all_gather(key_rows, "rows", axis=2, tiled=True)
    value_piece = lax.all_gather(value_rows, "rows", axis=2, tiled=True)
    count = key_piece.shape[2]
    fold_scores, fold_same_latent, fold_key_heads = block_scores(
        query_heads, key_piece, lat_groups, all_lat
    )
    masked = jnp.where(fold_same_latent, fold_scores, NEG_FILL)
    newest = jnp.maximum(best, jnp.max(masked, axis=-1))
    weights = jnp.where(fold_same_latent, jnp.exp(masked - newest[..., None]), 0.0)
    fold_value_heads = value_piece.astype(jnp.float32).reshape(canvases, 4, count, HEADS, HEAD_DIM)
    accum = jnp.einsum("cghqk,cgkhe->cghqe", weights, fold_value_heads, precision=PRECISE)
    best, weight_sum, accum = (newest, jnp.sum(weights, axis=-1), accum)
    attn_heads = accum / weight_sum[..., None]
    log_norm = best + jnp.log(weight_sum)
    attended = from_groups(
        attn_heads.transpose(0, 1, 3, 2, 4).reshape(canvases, 4, group_len, model_width), rows_here
    )
    attended_low = attended.astype(jnp.bfloat16).reshape(-1, model_width)
    attn_out = (
        jnp.dot(attended_low, w_out, preferred_element_type=jnp.float32) + b_out.astype(jnp.float32)
    ).reshape(canvases, local_tokens, model_width)
    middle = tokens_f + gate_one * attn_out
    h_two, norm_two_pull = jax.vjp(modulate_norm, middle, shift_two, scale_two)
    ffn_in = h_two.astype(jnp.bfloat16).reshape(-1, model_width)
    up_rows = (
        jnp.dot(ffn_in, w_up, preferred_element_type=jnp.float32) + b_up.astype(jnp.float32)
    ).astype(jnp.bfloat16)
    up_grid = up_rows.reshape(canvases, rows_here, SIDE, ffn_width)
    up_pad = pad_columns(padded_2(up_grid, (("rows", 1),), 1))
    conv_ffn_f = conv_ffn.astype(jnp.float32)
    conv_two = grid_taps(up_pad, conv_ffn_f, rows_here, SIDE)
    activated, gelu_pull = jax.vjp(gelu_tanh, conv_two)
    act_low = activated.astype(jnp.bfloat16).reshape(-1, ffn_width)
    branch = (
        jnp.dot(act_low, w_down, preferred_element_type=jnp.float32) + b_down.astype(jnp.float32)
    ).reshape(canvases, local_tokens, model_width)
    result = (middle + gate_two * branch).astype(jnp.bfloat16)
    out_grad = cotangent.astype(jnp.float32)
    branch_grad = (gate_two * out_grad).astype(jnp.bfloat16).reshape(-1, model_width)
    gate_two_grad = out_grad * branch
    g_b_down = jnp.sum(branch_grad.astype(jnp.float32), axis=0)
    g_w_down = jnp.dot(act_low.T, branch_grad, preferred_element_type=jnp.float32)
    act_grad = jnp.dot(branch_grad, w_down.T, preferred_element_type=jnp.float32).reshape(
        canvases, rows_here, SIDE, ffn_width
    )
    conv_two_grad = gelu_pull(act_grad)[0].astype(jnp.bfloat16)
    conv_two_pad = pad_columns(padded_2(conv_two_grad, (("rows", 1),), 1))
    up_grad = (
        grid_taps(conv_two_pad, conv_ffn_f[::-1], rows_here, SIDE)
        .astype(jnp.bfloat16)
        .reshape(-1, ffn_width)
    )
    g_conv_ffn = kernel_grad(up_pad, conv_two_grad)
    g_b_up = jnp.sum(up_grad.astype(jnp.float32), axis=0)
    g_w_up = jnp.dot(ffn_in.T, up_grad, preferred_element_type=jnp.float32)
    ffn_grad = jnp.dot(up_grad, w_up.T, preferred_element_type=jnp.float32).reshape(
        canvases, local_tokens, model_width
    )
    middle_part, shift_two_grad, scale_two_grad = norm_two_pull(ffn_grad)
    middle_grad = middle_part + out_grad
    gate_one_grad = middle_grad * attn_out
    attn_grad = (gate_one * middle_grad).astype(jnp.bfloat16).reshape(-1, model_width)
    g_b_out = jnp.sum(attn_grad.astype(jnp.float32), axis=0)
    g_w_out = jnp.dot(attended_low.T, attn_grad, preferred_element_type=jnp.float32)
    attended_grad = jnp.dot(attn_grad, w_out.T, preferred_element_type=jnp.float32).astype(
        jnp.bfloat16
    )
    grad_heads = to_groups(
        attended_grad.reshape(canvases, local_tokens, model_width), rows_here
    ).reshape(canvases, 4, group_len, HEADS, HEAD_DIM)
    grad_heads_f = grad_heads.astype(jnp.float32)
    delta = jnp.sum(grad_heads_f.transpose(0, 1, 3, 2, 4) * attn_heads, axis=-1)
    row_count = lax.axis_size("rows")
    here = lax.axis_index("rows")
    carried = jnp.stack([key_rows, value_rows])
    pending = jnp.zeros((2,) + key_rows.shape, jnp.float32)
    query_grad = jnp.zeros((canvases, 4, group_len, HEADS, HEAD_DIM), jnp.float32)
    for turn_index in range(row_count):
        source = (here - turn_index) % row_count
        key_lat = lax.dynamic_slice_in_dim(all_lat, source * group_len, group_len, 2)
        scores, same_latent, key_heads = block_scores(query_heads, carried[0], lat_groups, key_lat)
        value_heads = carried[1].reshape(canvases, 4, group_len, HEADS, HEAD_DIM)
        softmax_weights = jnp.where(same_latent, jnp.exp(scores - log_norm[..., None]), 0.0)
        weight_grad = jnp.einsum(
            "cgqhe,cgkhe->cghqk", grad_heads, value_heads, preferred_element_type=jnp.float32
        )
        score_grad = (softmax_weights * (weight_grad - delta[..., None])).astype(jnp.bfloat16)
        query_grad = query_grad + score_scale * jnp.einsum(
            "cghqk,cgkhe->cgqhe", score_grad, key_heads, preferred_element_type=jnp.float32
        )
        key_part = score_scale * jnp.einsum(
            "cghqk,cgqhe->cgkhe", score_grad, query_heads, preferred_element_type=jnp.float32
        )
        value_part = jnp.einsum(
            "cghqk,cgqhe->cgkhe", softmax_weights, grad_heads_f, precision=PRECISE
        )
        pending = pending + jnp.stack([key_part, value_part]).reshape(pending.shape)
        if turn_index + 1 < row_count:
            carried = passed_along(carried, "rows", 1)
        pending = passed_along(pending.astype(jnp.bfloat16), "rows", 1).astype(pending.dtype)
    query_low = query_grad.reshape(canvases, 4, group_len, model_width).astype(jnp.bfloat16)
    grouped_grad = jnp.concatenate(
        [query_low, pending[0].astype(jnp.bfloat16), pending[1].astype(jnp.bfloat16)], axis=-1
    )
    qkv_grad = from_groups(grouped_grad, rows_here).reshape(-1, 3 * model_width)
    qkv_grad_f = qkv_grad.astype(jnp.float32)
    g_bias_qv = jnp.concatenate(
        [
            jnp.sum(qkv_grad_f[:, :model_width], axis=0),
            jnp.sum(qkv_grad_f[:, 2 * model_width :], axis=0),
        ]
    )
    g_w_qkv = jnp.dot(conv_low.T, qkv_grad, preferred_element_type=jnp.float32)
    conv_one_grad = (
        jnp.dot(qkv_grad, w_qkv.T, preferred_element_type=jnp.float32)
        .astype(jnp.bfloat16)
        .reshape(canvases, rows_here, SIDE, model_width)
    )
    conv_one_pad = pad_columns(padded_2(conv_one_grad, (("rows", 1),), 1))
    attn_in_grad = grid_taps(conv_one_pad, conv_attn_f[::-1], rows_here, SIDE).reshape(
        canvases, local_tokens, model_width
    )
    g_conv_attn = kernel_grad(attn_pad, conv_one_grad)
    token_part, shift_one_grad, scale_one_grad = norm_one_pull(attn_in_grad)
    input_grad = token_part + middle_grad
    token_mod_grad = jnp.concatenate(
        [
            shift_one_grad,
            scale_one_grad,
            gate_one_grad,
            shift_two_grad,
            scale_two_grad,
            gate_two_grad,
        ],
        axis=-1,
    )
    mod_grad = jnp.einsum("cnk,cnf->ckf", onehot, token_mod_grad, precision=PRECISE)
    cond_f = cond_low.astype(jnp.float32)
    summed = (
        lax.psum(g_conv_attn.astype(jnp.bfloat16), "rows").astype(jnp.float32),
        lax.psum(g_w_qkv.astype(jnp.bfloat16), "rows").astype(jnp.float32),
        lax.psum(g_bias_qv.astype(jnp.bfloat16), "rows").astype(jnp.float32),
        lax.psum(g_w_out.astype(jnp.bfloat16), "rows").astype(jnp.float32),
        lax.psum(g_b_out.astype(jnp.bfloat16), "rows").astype(jnp.float32),
        lax.psum(g_w_up.astype(jnp.bfloat16), "rows").astype(jnp.float32),
        lax.psum(g_b_up.astype(jnp.bfloat16), "rows").astype(jnp.float32),
        lax.psum(g_conv_ffn.astype(jnp.bfloat16), "rows").astype(jnp.float32),
        lax.psum(g_w_down.astype(jnp.bfloat16), "rows").astype(jnp.float32),
        lax.psum(g_b_down.astype(jnp.bfloat16), "rows").astype(jnp.float32),
        lax.psum(mod_grad.astype(jnp.bfloat16), "rows").astype(jnp.float32),
    )
    mod_total = summed[10]
    g_w_ada = jnp.einsum("ckd,ckf->df", cond_f, mod_total, precision=PRECISE)
    g_b_ada = jnp.sum(mod_total, axis=(0, 1))
    shares = (
        lax.psum_scatter(
            g_w_ada.astype(jnp.bfloat16), "canvas", scatter_dimension=0, tiled=True
        ).astype(jnp.float32),
        lax.psum_scatter(
            g_b_ada.astype(jnp.bfloat16), "canvas", scatter_dimension=0, tiled=True
        ).astype(jnp.float32),
        lax.psum_scatter(
            summed[0].astype(jnp.bfloat16), "canvas", scatter_dimension=1, tiled=True
        ).astype(jnp.float32),
        lax.psum_scatter(
            summed[1].astype(jnp.bfloat16), "canvas", scatter_dimension=0, tiled=True
        ).astype(jnp.float32),
        lax.psum_scatter(
            summed[2].astype(jnp.bfloat16), "canvas", scatter_dimension=0, tiled=True
        ).astype(jnp.float32),
        lax.psum_scatter(
            summed[3].astype(jnp.bfloat16), "canvas", scatter_dimension=0, tiled=True
        ).astype(jnp.float32),
        lax.psum_scatter(
            summed[4].astype(jnp.bfloat16), "canvas", scatter_dimension=0, tiled=True
        ).astype(jnp.float32),
        lax.psum_scatter(
            summed[5].astype(jnp.bfloat16), "canvas", scatter_dimension=0, tiled=True
        ).astype(jnp.float32),
        lax.psum_scatter(
            summed[6].astype(jnp.bfloat16), "canvas", scatter_dimension=0, tiled=True
        ).astype(jnp.float32),
        lax.psum_scatter(
            summed[7].astype(jnp.bfloat16), "canvas", scatter_dimension=1, tiled=True
        ).astype(jnp.float32),
        lax.psum_scatter(
            summed[8].astype(jnp.bfloat16), "canvas", scatter_dimension=0, tiled=True
        ).astype(jnp.float32),
        lax.psum_scatter(
            summed[9].astype(jnp.bfloat16), "canvas", scatter_dimension=0, tiled=True
        ).astype(jnp.float32),
    )
    cond_grad = silu_pull(
        jnp.einsum("ckf,df->ckd", mod_total, w_ada.astype(jnp.float32), precision=PRECISE)
    )[0]
    return (
        result,
        input_grad,
        cond_grad,
        shares[0],
        shares[1],
        shares[2],
        shares[3],
        shares[4],
        shares[5],
        shares[6],
        shares[7],
        shares[8],
        shares[9],
        shares[10],
        shares[11],
    )

BF = jnp.bfloat16
F32 = jnp.float32
D = 768
FF = 3072
HB = 384
BIG = -1e30


def dot(a, b):
    return jnp.dot(a, b, preferred_element_type=F32)


def dot_t(a, b):
    return lax.dot_general(a, b, (((1,), (1,)), ((), ())), preferred_element_type=F32)


def dot_l(a, b):
    return lax.dot_general(a, b, (((0,), (0,)), ((), ())), preferred_element_type=F32)


def iota(shape, dim):
    return lax.broadcasted_iota(jnp.int32, shape, dim)


def ones_where(mask):
    return jnp.where(mask, 1.0, 0.0).astype(BF)


def taps_of(pr, pc, back):
    found = []
    for i in range(3):
        for j in range(3):
            di, dj = (1 - i, 1 - j) if back else (i - 1, j - 1)
            gr = pr if di == 0 else 1 - pr
            gc = pc if dj == 0 else 1 - pc
            ro = 0 if di == 0 else (pr - 1 if di < 0 else pr)
            co = 0 if dj == 0 else (2 * pc + dj - 1) // 2
            found.append((3 * i + j, 2 * gr + gc, ro, co != 0))
    return found


def shifted(rows, pc):
    n = rows.shape[0]
    col = iota(rows.shape, 0) % 16
    if pc == 1:
        return jnp.where(col == 0, 0.0, pltpu.roll(rows, 1, 0))
    return jnp.where(col == 15, 0.0, pltpu.roll(rows, n - 1, 0))


def conv_sum(load, kr, taps):
    total = None
    for t, gsrc, ro, moved in taps:
        term = load(gsrc, ro, moved).astype(F32) * kr[t]
        total = term if total is None else total + term
    return total


def conv_both(load, here, kr, gk, taps):
    total = None
    for t, gsrc, ro, moved in taps:
        src = load(gsrc, ro, moved).astype(F32)
        term = src * kr[t]
        total = term if total is None else total + term
        gk[t] = gk[t] + fold_rows(src * here)
    return total


def fold_rows(rows):
    return jnp.sum(rows.reshape(rows.shape[0] // 8, 8, 128), axis=0)


def norm_parts(v):
    mean = jnp.mean(v, axis=-1, keepdims=True)
    cen = v - mean
    inv = lax.rsqrt(jnp.mean(cen * cen, axis=-1, keepdims=True) + EPSILON)
    return cen * inv, inv


def norm_back(n, nrm, inv):
    m1 = jnp.mean(n, axis=-1, keepdims=True)
    m2 = jnp.mean(n * nrm, axis=-1, keepdims=True)
    return (n - m1 - nrm * m2) * inv


SCRATCH = dict(
    stg_t=((2, 4, 64, D), BF),
    stg_c=((2, 4, 64, D), BF),
    tok=((4, 256, D), BF),
    cot=((4, 256, D), BF),
    latc=((4, 1, 256), jnp.int32),
    lv=((4, 256, 128), F32),
    oh=((4, 256, 128), BF),
    modhl=((32, 6 * D), BF),
    pm=((256, 256), BF),
    ain=((4, 288, D), BF),
    c1t=((D, 1024), BF),
    tmpa=((4, 256, D), BF),
    qkv=((4, 256, 3 * HB), BF),
    att=((4, 256, D), BF),
    fint=((D, 1024), BF),
    bg=((4, 256, D), BF),
    mid=((2, 256, D), F32),
    ub=((4, 288, HB), BF),
    us=((4, 288, HB), BF),
    gb=((4, 288, HB), BF),
    gs=((4, 288, HB), BF),
    gp=((2, 256, D), F32),
    act=((4, 256, 2 * D), BF),
    upg=((4, 256, 2 * D), BF),
    upr=((4, 256, 2 * D), BF),
    actt=((HB, 1024), BF),
    wup=((D, 2 * D), BF),
    wdn=((2 * D, D), BF),
    wq=((D, 3 * HB), BF),
    wo=((D, D), BF),
    gwd=((4, HB, D), BF),
    gwo=((4, 96, D), BF),
    rd_a=((192, D), BF),
    rd_b=((192, D), BF),
    rd_x=((HB, D), BF),
    rd_y=((HB, D), BF),
    ru_a=((96, 2 * D), BF),
    ru_b=((96, 2 * D), BF),
    ru_x=((192, 2 * D), BF),
    ru_y=((192, 2 * D), BF),
    rq_a=((96, 3 * HB), BF),
    rq_b=((96, 3 * HB), BF),
    rq_x=((192, 3 * HB), BF),
    rq_y=((192, 3 * HB), BF),
    ro_a=((48, D), BF),
    ro_b=((48, D), BF),
    ro_x=((96, D), BF),
    ro_y=((96, D), BF),
    su=((96, 2 * D), BF),
    sq=((96, 3 * HB), BF),
    zd_a=((HB, D), BF),
    zd_b=((HB, D), BF),
    zu_a=((96, FF), BF),
    zu_b=((96, FF), BF),
    zq_a=((96, 3 * D), BF),
    zq_b=((96, 3 * D), BF),
    zo_a=((96, D), BF),
    zo_b=((96, D), BF),
    frcv=((2, 4, 64, D), BF),
    brcv=((2, 4, 64, D), BF),
    oland=((2, 4, 64, D), BF),
    gland=((2, 4, 64, D), BF),
    condc=((16, D), F32),
    clow=((4, 16, D), BF),
    mg1=((16, D), F32),
    mg2=((16, HB), F32),
    mgs1=((16, D), BF),
    mgr1=((16, D), BF),
    mgs2=((16, HB), BF),
    mgr2=((16, HB), BF),
    mga1=((16, 16, D), BF),
    mga2=((16, 16, HB), BF),
    sg1=((16, FF), F32),
    sg1s=((1, 16, FF), BF),
    sg1r=((5, 16, FF), BF),
    sg2=((16, D), F32),
    sg2s=((1, 16, D), BF),
    sg2r=((5, 16, D), BF),
    cgsum=((16, D), F32),
    crcv=((2, 8, D), F32),
    lat_own=((2, 1, 256), jnp.int32),
    cond_own=((8, D), F32),
    par=((16, FF), F32),
)
N_SEMS = 240


def whole_block(
    tok_h, cot_h, lat_in, cond_in, wada_h, wqkv_h, wout_h, wup_h, wdn_h,
    p_bada, p_conv1, p_bqv, p_bout, p_bup, p_conv2, p_bdn,
    o_out, o_gin, o_cond, o_wada, o_bada, o_sg1, o_sg2, o_wqkv, o_wout, o_wup, o_wdn,
    sems, *bufs,
):
    v = SimpleNamespace(**dict(zip(SCRATCH, bufs)))
    stg_t, stg_c, tok, cot, latc, lv, oh = v.stg_t, v.stg_c, v.tok, v.cot, v.latc, v.lv, v.oh
    modhl, pm, ain, c1t, tmpa, qkv, att = v.modhl, v.pm, v.ain, v.c1t, v.tmpa, v.qkv, v.att
    fint, bg, mid, ub, us, gb, gs = v.fint, v.bg, v.mid, v.ub, v.us, v.gb, v.gs
    gp, act, upg, actt, wup, wdn, wq, wo = v.gp, v.act, v.upg, v.actt, v.wup, v.wdn, v.wq, v.wo
    upr = v.upr
    gwd, gwo, condc, clow = v.gwd, v.gwo, v.condc, v.clow

    c = lax.axis_index("canvas")
    r = lax.axis_index("rows")
    k = c % 2
    x = (c // 2) % 2
    y = c // 4
    col = 2 * y + x
    r1 = r + 1 - 2 * (r % 2)
    r2 = (r + 2) % 4
    r3 = 3 - r
    sib = (y * 4 + x * 2 + 1 - k, r)
    px = (y * 4 + (1 - x) * 2 + k, r)
    py = ((1 - y) * 4 + x * 2 + k, r)
    owner = r // 2
    is_own = k == owner
    owner_c = y * 4 + x * 2 + owner

    count = [0]

    def sem(n=1):
        first = count[0]
        count[0] += n
        return first

    last = []

    def remote(src, dst, ss, rs, dev):
        return pltpu.make_async_remote_copy(
            src_ref=src, dst_ref=dst, send_sem=sems.at[ss], recv_sem=sems.at[rs],
            device_id=dev, device_id_type=pl.DeviceIdType.MESH,
        )

    def local(src, dst, s):
        return pltpu.make_async_copy(src, dst, sems.at[s])

    def swap(src, dst, dev):
        cp = remote(src, dst, sem(), sem(), dev)
        cp.start()
        last.append(cp.wait_send)
        return cp

    barrier = pltpu.get_barrier_semaphore()
    for dev in (sib, px, py, (c, r1), (c, r2), (c, r3), (sib[0], r1), (sib[0], r2), (sib[0], r3)):
        pl.semaphore_signal(barrier, inc=1, device_id=dev, device_id_type=pl.DeviceIdType.MESH)
    s_tok = sem()
    s_cot = sem()
    ld_tok = local(tok_h, act.at[pl.ds(0, 2), :, pl.ds(0, D)], s_tok)
    ld_tok.start()
    ld_cot = local(cot_h, act.at[pl.ds(0, 2), :, pl.ds(D, D)], s_cot)
    ld_cot.start()
    s_wa = sem(2)

    def load_ada(p):
        return local(wada_h.at[:, pl.ds(p * D, D)], wup.at[:, pl.ds((p % 2) * D, D)], s_wa + p % 2)

    load_ada(0).start()
    load_ada(1).start()
    s_w = sem(3)
    ld_wq = [
        local(wqkv_h.at[:, pl.ds(pl.multiple_of(part * D + HB * k, 128), HB)], wq.at[:, pl.ds(part * HB, HB)], s_w + part)
        for part in range(3)
    ]
    for cp in ld_wq:
        cp.start()
    ld_wo = local(wout_h, wo, sem())
    ld_wo.start()
    s_wd = sem(4)
    ld_wd = [
        local(wdn_h.at[pl.ds(pl.multiple_of(HB * (2 * b + k), 128), HB), :], wdn.at[pl.ds(HB * b, HB), :], s_wd + b)
        for b in range(4)
    ]
    for cp in ld_wd:
        cp.start()
    pi = iota((256, 256), 0)
    group, place = pi // 64, pi % 64
    nat = (2 * (place // 16) + group // 2) * 32 + 2 * (place % 16) + group % 2
    pm[...] = ones_where(iota((256, 256), 1) == nat)
    for buf in (ain, ub, us, gb, gs):
        wide = buf.shape[2]
        for g in range(4):
            buf[g, 0:16, :] = jnp.zeros((16, wide), BF)
            buf[g, 272:288, :] = jnp.zeros((16, wide), BF)
    lat_h, par = v.lat_own, v.par
    for i in range(2):
        lat_h[i] = lat_in[i : i + 1, :]
        v.cond_own[4 * i : 4 * i + 4, :] = cond_in[i]
    condc[pl.ds(pl.multiple_of(8 * k, 8), 8), :] = v.cond_own[...]
    par[0:9, :] = p_conv2[...].astype(F32)

    def row_of(ref):
        return ref[...].astype(F32).reshape(1, ref.shape[0])

    par[9:10, :] = row_of(p_bup)
    par[10:11, 0:D] = row_of(p_bdn)
    par[10:11, D : 2 * D] = row_of(p_bout)
    par[10:11, 2 * D : 4 * D] = row_of(p_bqv)
    taps1 = p_conv1[...].astype(F32)
    for t in range(9):
        par[11 + t // 4 : 12 + t // 4, (t % 4) * D : (t % 4) * D + D] = taps1[t : t + 1]
    ada = row_of(p_bada)
    par[14:15, :] = ada[:, 0 : 4 * D]
    par[15:16, 0 : 2 * D] = ada[:, 4 * D : 6 * D]
    pl.semaphore_wait(barrier, 9)

    cond_cp = swap(
        condc.at[pl.ds(pl.multiple_of(8 * k, 8), 8), :], condc.at[pl.ds(pl.multiple_of(8 * k, 8), 8), :], sib
    )
    mine64 = pl.ds(pl.multiple_of(r * 64, 64), 64)
    rt, rl, rc = sem(4), sem(4), sem(4)
    st, sl, sc = sem(2), sem(2), sem(2)

    def give(src, dst, ss, rs, i):
        q = 2 * k + i
        far = remote(src, dst, ss, rs, (c, q))
        near = local(src, dst, rs)

        @pl.when(q != r)
        def _():
            far.start()

        @pl.when(q == r)
        def _():
            near.start()

        def done():
            @pl.when(q != r)
            def _():
                far.wait_send()

        return done

    tok_sent, cot_sent = [], []
    ld_tok.wait()
    for i in range(2):
        stg_t[i] = dot(pm[...], act[i, :, 0:D]).astype(BF).reshape(4, 64, D)
        tok_sent.append(give(stg_t.at[i], tok.at[:, mine64, :], st + i, rt + r, i))
        last.append(give(lat_h.at[i], latc.at[r], sl + i, rl + r, i))

    ld_cot.wait()
    for i in range(2):
        stg_c[i] = dot(pm[...], act[i, :, D : 2 * D]).astype(BF).reshape(4, 64, D)

    cond_cp.wait_recv()
    cond = condc[...]
    sig = 1.0 / (1.0 + jnp.exp(-cond))
    mine_low = (cond * sig).astype(BF)
    clow[col] = mine_low
    low_x = swap(clow.at[col], clow.at[col], px)
    for p in range(6):
        load_ada(p).wait()
        mod = dot(mine_low, wup[:, (p % 2) * D : (p % 2) * D + D])
        mod = mod + par[14 + p // 4 : 15 + p // 4, (p % 4) * D : (p % 4) * D + D]
        high = mod.astype(BF)
        modhl[0:16, p * D : (p + 1) * D] = high
        modhl[16:32, p * D : (p + 1) * D] = (mod - high.astype(F32)).astype(BF)
        if p + 2 < 6:
            load_ada(p + 2).start()
    s_wu = sem(4)
    ld_wu = [
        local(wup_h.at[:, pl.ds(pl.multiple_of(HB * (2 * b + k), 128), HB)], wup.at[:, pl.ds(HB * b, HB)], s_wu + b)
        for b in range(4)
    ]
    for cp in ld_wu:
        cp.start()

    def piece(o, p):
        return dot(o[:, 0:32], modhl[:, p * D : (p + 1) * D])

    ft, fl, fc = sem(4), sem(4), sem(4)
    order = (r, r1, r2, r3)

    def arrive(buf, of, rs, fs):
        passed = []
        for d in range(4):
            s = order[d]
            place = of(s)
            cp = remote(buf.at[place], buf.at[place], fs + d, rs + s, sib)
            cp.wait_recv()

            @pl.when(is_own)
            def _():
                cp.start()

            def done(cp=cp):
                @pl.when(is_own)
                def _():
                    cp.wait_send()

            passed.append(done)
        return passed

    def slab(s):
        return (slice(None), pl.ds(pl.multiple_of(s * 64, 64), 64), slice(None))

    last.extend(arrive(latc, lambda s: s, rl, fl))
    tok_passed = arrive(tok, slab, rt, ft)
    for i in range(2):
        cot_sent.append(give(stg_c.at[i], cot.at[:, mine64, :], sc + i, rc + r, i))

    for s in range(4):
        rows = jnp.broadcast_to(latc[s].astype(F32), (128, 256)).astype(BF)
        ids = dot_t(pm[...], rows)
        for g in range(4):
            lv[g, s * 64 : s * 64 + 64, :] = ids[g * 64 : g * 64 + 64]
    for g in range(4):
        lane = iota((256, 128), 1)
        want = (lane % 16 - 4 * r).astype(F32)
        oh[g] = ones_where((want == lv[g]) & (lane < 32))

    def norm_one(n, _):
        t0 = pl.multiple_of((n % 2) * 128, 128)
        for pc in range(2):
            g = 2 * (n // 2) + pc
            nrm, _inv = norm_parts(tok[g, pl.ds(t0, 128), :].astype(F32))
            o = oh[g, pl.ds(t0, 128), :]
            h = (nrm * (1.0 + piece(o, 1)) + piece(o, 0)).astype(BF)
            ain[g, pl.ds(t0 + 16, 128), :] = h
            sh = shifted(h.astype(F32), pc).astype(BF)
            us[g, pl.ds(t0 + 16, 128), :] = sh[:, 0:HB]
            gs[g, pl.ds(t0 + 16, 128), :] = sh[:, HB:D]
        return 0

    lax.fori_loop(0, 4, norm_one, 0)

    for hh in range(2):
        side = us if hh == 0 else gs

        def conv_one(lt, _, hh=hh, side=side):
            l0 = pl.multiple_of(lt * 128, 128)
            la = pl.multiple_of(hh * HB + lt * 128, 128)
            kr = [par[11 + t // 4 : 12 + t // 4, pl.ds((t % 4) * D + la, 128)] for t in range(9)]
            for g in range(4):
                for h in range(2):

                    def load(gsrc, ro, moved):
                        rows = pl.ds(16 + 16 * ro + 128 * h, 128)
                        return side[gsrc, rows, pl.ds(l0, 128)] if moved else ain[gsrc, rows, pl.ds(la, 128)]

                    low = conv_sum(load, kr, taps_of(g // 2, g % 2, False)).astype(BF)
                    tmpa[g, h * 128 : h * 128 + 128, pl.ds(la, 128)] = low
                    c1t[pl.ds(la, 128), g * 256 + h * 128 : g * 256 + h * 128 + 128] = low.astype(F32).T.astype(BF)
            return 0

        lax.fori_loop(0, 3, conv_one, 0)

    for cp in ld_wq:
        cp.wait()
    kcol = pl.multiple_of(HB * k, 128)
    b_q = par[10:11, pl.ds(2 * D + kcol, HB)]
    b_v = par[10:11, pl.ds(3 * D + kcol, HB)]

    def project(n, _):
        two = pl.ds(2 * n, 2)
        rows = tmpa[two].reshape(512, D)
        got = dot(rows, wq[:, 0:HB]) + b_q
        qkv[two, :, 0:HB] = (got.astype(BF).astype(F32) * 0.125).astype(BF).reshape(2, 256, HB)
        qkv[two, :, HB : 2 * HB] = dot(rows, wq[:, HB : 2 * HB]).astype(BF).reshape(2, 256, HB)
        got = dot(rows, wq[:, 2 * HB : 3 * HB]) + b_v
        qkv[two, :, 2 * HB : 3 * HB] = got.astype(BF).reshape(2, 256, HB)
        return 0

    lax.fori_loop(0, 2, project, 0)

    lane1 = iota((1, 128), 1)
    lmf = [jnp.where(lane1 < 64, 1.0, 0.0), jnp.where(lane1 < 64, 0.0, 1.0)]
    lmb = [m.astype(BF) for m in lmf]
    sa, ra = sem(4), sem(4)

    def masks_of(g):
        lane = iota((256, 128), 1)
        same = lane.astype(F32) == lv[g]
        oq = jnp.where(same & (lane < 4), 1.0, 0.0).astype(BF)
        mk = jnp.where(same | (lane >= 4), 0.0, BIG).astype(BF)
        return oq, mk

    def att_copy(g):
        place = att.at[g, :, pl.ds(kcol, HB)]
        return remote(place, place, sa + g, ra + g, sib)

    def attend(g, _):
        oq, mk = masks_of(g)
        oq2 = jnp.concatenate([oq, oq], axis=0)
        for hp in range(3):
            qp = qkv[g, :, hp * 128 : hp * 128 + 128]
            ka = jnp.concatenate([qkv[g, :, HB + hp * 128 : HB + hp * 128 + 128], mk], axis=1)
            vp = qkv[g, :, 2 * HB + hp * 128 : 2 * HB + hp * 128 + 128]
            qa = jnp.concatenate([qp * lmb[0], qp * lmb[1]], axis=0)
            s = dot_t(jnp.concatenate([qa, oq2], axis=1), ka)
            e = jnp.exp(s - jnp.max(s, axis=1, keepdims=True))
            o = dot(e.astype(BF), vp) * (1.0 / jnp.sum(e, axis=1, keepdims=True))
            mixed = o[0:256] * lmf[0] + o[256:512] * lmf[1]
            att[g, :, pl.ds(pl.multiple_of(kcol + hp * 128, 128), 128)] = mixed.astype(BF)
        att_copy(g).start()
        return 0

    lax.fori_loop(0, 4, attend, 0)
    low_x.wait_recv()
    low_y = swap(clow.at[pl.ds(2 * y, 2)], clow.at[pl.ds(2 * y, 2)], py)
    last.extend(arrive(cot, slab, rc, fc))

    ld_wo.wait()
    kother = pl.multiple_of(HB * (1 - k), 128)

    def norm_two(g, _):
        for h in range(2):
            rows = slice(h * 128, h * 128 + 128)
            a = att[g, rows, :]
            ao = dot(a, wo[...]) + par[10:11, D : 2 * D]
            o = oh[g, rows, :]
            m = tok[g, rows, :].astype(F32) + piece(o, 2) * ao
            nrm, _inv = norm_parts(m)
            f = (nrm * (1.0 + piece(o, 4)) + piece(o, 3)).astype(BF)
            tmpa[g, rows, :] = f
            at = pl.ds(pl.multiple_of(g * 256 + h * 128, 128), 128)
            fint[:, at] = f.astype(F32).T.astype(BF)
            bg[g, rows, :] = (piece(o, 5) * cot[g, rows, :].astype(F32)).astype(BF)
        return 0

    for g in range(4):
        att_copy(g).wait()
    lax.fori_loop(0, 4, norm_two, 0)

    class Scatter:
        def __init__(self, src, a, b, rx, ry):
            self.src, self.a, self.b, self.rx, self.ry = src, a, b, rx, ry
            n = a.shape[0]
            self.n = n
            ss = sem(8)
            self.ca = remote(src(0, 0, n), a, ss, ss + 1, px)
            self.cb = remote(src(0, n, n), b, ss + 2, ss + 3, py)
            self.cx = remote(src(1, 0, 2 * n), rx, ss + 4, ss + 5, px)
            self.cy = remote(src(2, 0, 2 * n), ry, ss + 6, ss + 7, py)

        def s0(self):
            self.ca.start()
            self.cb.start()

        def s1(self):
            self.cb.wait_recv()
            part = self.src(1, self.n, self.n)
            part[...] = (part[...].astype(F32) + self.b[...].astype(F32)).astype(BF)
            self.cx.start()

        def s2(self):
            self.ca.wait_recv()
            part = self.src(2, 0, self.n)
            part[...] = (part[...].astype(F32) + self.a[...].astype(F32)).astype(BF)
            self.cy.start()

        def s3(self):
            self.cx.wait_recv()
            self.cy.wait_recv()
            part = self.src(3, 0, 2 * self.n)
            return part[...].astype(F32) + self.rx[...].astype(F32) + self.ry[...].astype(F32)

        def sent(self):
            for cp in (self.ca, self.cb, self.cx, self.cy):
                cp.wait_send()

    inner = (r % 3) != 0

    class Line:
        def __init__(self, out, za, zb, cuts):
            n = out.shape[0] // cuts
            self.parts = []
            for i in range(cuts):
                rows = pl.ds(i * n, n)
                o, a, b = out.at[rows], za.at[rows], zb.at[rows]
                ss = sem(6)
                up = remote(o, a, ss, ss + 1, (c, r1))
                mid = remote(o, b, ss + 2, ss + 3, (c, r3))
                down = remote(o, a, ss + 4, ss + 5, (c, r1))
                self.parts.append((o, a, b, up, mid, down))

        def s0(self):
            @pl.when(jnp.logical_not(inner))
            def _():
                for part in self.parts:
                    part[3].start()

        def s1(self):
            @pl.when(inner)
            def _():
                for o, a, _b, up, mid, _down in self.parts:
                    up.wait_recv()
                    o[...] = (o[...].astype(F32) + a[...].astype(F32)).astype(BF)
                    mid.start()

        def s2(self):
            @pl.when(inner)
            def _():
                for o, _a, b, _up, mid, down in self.parts:
                    mid.wait()
                    o[...] = (o[...].astype(F32) + b[...].astype(F32)).astype(BF)
                    down.start()

        def s3(self):
            @pl.when(inner)
            def _():
                for part in self.parts:
                    part[5].wait_send()

            @pl.when(jnp.logical_not(inner))
            def _():
                for o, a, _b, up, _mid, down in self.parts:
                    up.wait_send()
                    down.wait_recv()
                    o[...] = a[...]

    class Gather:
        def __init__(self, own, got, everyone):
            self.own, self.got, self.everyone = own, got, everyone
            self.zr, self.zs = sem(4), sem(3)
            self.xy = sem(4)

        def s0(self):
            self.everyone[slot] = (self.own[...].astype(F32) + self.got[...].astype(F32)).astype(BF)
            place = self.everyone.at[slot]
            for d, s in enumerate((r1, r2, r3)):
                cp = remote(place, place, self.zs + d, self.zr + r, (c, s))
                cp.start()
                last.append(cp.wait_send)

        def s1(self):
            for s in (r1, r2, r3):
                place = self.everyone.at[4 * col + s]
                local(place, place, self.zr + s).wait()
            place = self.everyone.at[pl.ds(4 * col, 4)]
            self.cx = remote(place, place, self.xy, self.xy + 1, px)
            self.cx.start()
            last.append(self.cx.wait_send)

        def s2(self):
            self.cx.wait_recv()
            place = self.everyone.at[pl.ds(8 * y, 8)]
            self.cy = remote(place, place, self.xy + 2, self.xy + 3, py)
            self.cy.start()
            last.append(self.cy.wait_send)

        def s3(self):
            self.cy.wait_recv()

    class Everyone:
        def __init__(self, total, send, recv):
            self.total, self.send, self.recv = total, send, recv
            ss = sem(6)
            devs = (sib, px, py)
            self.cps = [remote(send.at[0], recv.at[i], ss + 2 * i, ss + 2 * i + 1, devs[i]) for i in range(3)]

        def go(self, i):
            self.send[0] = self.total[...].astype(BF)
            self.cps[i].start()

        def end(self, i):
            self.cps[i].wait()
            self.total[...] = self.send[0].astype(F32) + self.recv[i].astype(F32)

        def plane(self):
            self.end(2)
            self.send[0] = self.total[...].astype(BF)

    mga1, mga2 = v.mga1, v.mga2
    mgs1, mgr1, mgs2, mgr2 = v.mgs1, v.mgr1, v.mgs2, v.mgr2
    slot = 4 * col + r
    gat1 = Gather(mgs1, mgr1, mga1)
    gat2 = Gather(mgs2, mgr2, mga2)
    sum_d = Scatter(lambda p, r0, n: gwd.at[p, pl.ds(r0, n)], v.rd_a, v.rd_b, v.rd_x, v.rd_y)
    sum_u = Scatter(lambda p, r0, n: upr.at[p, pl.ds(r0, n)], v.ru_a, v.ru_b, v.ru_x, v.ru_y)
    sum_o = Scatter(lambda p, r0, n: gwo.at[p, pl.ds(r0, n)], v.ro_a, v.ro_b, v.ro_x, v.ro_y)
    sum_q = Scatter(lambda p, r0, n: wup.at[pl.ds(192 * p + r0, n), pl.ds(0, 3 * HB)], v.rq_a, v.rq_b, v.rq_x, v.rq_y)
    line_d = Line(o_wdn, v.zd_a, v.zd_b, 2)
    line_u = Line(o_wup, v.zu_a, v.zu_b, 2)
    line_o = Line(o_wout, v.zo_a, v.zo_b, 1)
    line_q = Line(o_wqkv, v.zq_a, v.zq_b, 2)
    sg1, sg2 = v.sg1, v.sg2
    all1 = Everyone(sg1, v.sg1s, v.sg1r)
    all2 = Everyone(sg2, v.sg2s, v.sg2r)
    line_a = Line(v.sg1s.at[0], v.sg1r.at[3], v.sg1r.at[4], 1)
    line_b = Line(v.sg2s.at[0], v.sg2r.at[3], v.sg2r.at[4], 1)
    sg1[...] = jnp.zeros((16, FF), F32)
    sg2[...] = jnp.zeros((16, D), F32)

    def block_at(pos):
        fx = 1 - pos // 2
        fy = 1 - pos % 2
        bx = x + fx - 2 * x * fx
        by = y + fy - 2 * y * fy
        return 2 * by + bx

    for cp in ld_wd + ld_wu:
        cp.wait()

    def hidden(pos, _):
        b = block_at(pos)
        lo = pl.multiple_of(b * HB, 128)
        wide = pl.multiple_of(HB * (2 * b + k), 128)

        def up(pr, _):
            both = dot(tmpa[pl.ds(2 * pr, 2)].reshape(512, D), wup[:, pl.ds(lo, HB)])
            for pc in range(2):
                g = 2 * pr + pc
                u = (both[pc * 256 : pc * 256 + 256] + par[9:10, pl.ds(wide, HB)]).astype(BF)
                ub[g, 16:272, :] = u
                upr[g, :, pl.ds(lo, HB)] = u
                us[g, 16:272, :] = shifted(u.astype(F32), pc).astype(BF)
            return 0

        lax.fori_loop(0, 2, up, 0)

        def conv_gelu(lt, _):
            l0 = pl.multiple_of(lt * 128, 128)
            ln = pl.ds(l0, 128)
            kr = [par[t : t + 1, pl.ds(wide + l0, 128)] for t in range(9)]
            for g in range(4):
                for h in range(2):

                    def load(gsrc, ro, moved):
                        return (us if moved else ub)[gsrc, pl.ds(16 + 16 * ro + 128 * h, 128), ln]

                    acc = conv_sum(load, kr, taps_of(g // 2, g % 2, False))
                    sq = acc * acc
                    th = jnp.tanh(0.7978845608028654 * acc * (1.0 + 0.044715 * sq))
                    half = 0.5 + 0.5 * th
                    low = (acc * half).astype(BF)
                    slope = half + half * (1.0 - th) * acc * (0.7978845608028654 + 0.10703222440890037 * sq)
                    rows = slice(h * 128, h * 128 + 128)
                    act[g, rows, pl.ds(lo + l0, 128)] = low
                    upg[g, rows, pl.ds(lo + l0, 128)] = slope.astype(BF)
                    actt[ln, g * 256 + h * 128 : g * 256 + h * 128 + 128] = low.astype(F32).T.astype(BF)
            return 0

        lax.fori_loop(0, 3, conv_gelu, 0)

        def grad_down(n, _):
            ln = pl.ds(pl.multiple_of(n * 256, 128), 256)
            gwd[pos, :, ln] = dot(actt[...], bg[:, :, ln].reshape(1024, 256)).astype(BF)
            return 0

        lax.fori_loop(0, 3, grad_down, 0)
        pl.when(pos == 0)(sum_d.s0)

        @pl.when(pos == 2)
        def _():
            sum_d.s1()
            sum_d.s2()

        return 0

    lax.fori_loop(0, 4, hidden, 0)

    for done in tok_sent + cot_sent:
        done()
    other2 = pl.ds(2 * (1 - k), 2)
    mine2 = pl.ds(2 * k, 2)

    def half_f(which, n):
        return dot_t(upg[which].reshape(512, 2 * D), wup[n * HB : n * HB + HB, :])

    def half_b(which, n):
        return dot(act[which].reshape(512, 2 * D), wdn[:, n * HB : n * HB + HB])

    for n in range(2):
        cols = slice(n * HB, n * HB + HB)
        stg_c[:, :, :, cols] = half_b(other2, n).astype(BF).reshape(2, 4, 64, HB)
    b_cp = remote(stg_c, v.brcv, sem(), sem(), sib)
    b_cp.start()
    for n in range(2):
        cols = slice(n * HB, n * HB + HB)
        mid[:, :, cols] = half_b(mine2, n).reshape(2, 256, HB)

    def down_total():
        o_wdn[...] = sum_d.s3().astype(BF)
        line_d.s0()

    mg1, mg2 = v.mg1, v.mg2
    mg1[...] = jnp.zeros((16, D), F32)
    mg2[...] = jnp.zeros((16, HB), F32)
    o_rows = jnp.zeros((1, D), F32)

    def place_rows(ids, p):
        lane = iota((128, 128), 1)
        return ones_where((lane - 4 * p).astype(F32) == ids)

    def hand_back(src, land, rs):
        ss = sem(4)
        for s in range(4):
            dst = land.at[r % 2, pl.ds(2 * k, 2)]
            at = rs + (r % 2) * 2 + k
            far = remote(src.at[:, s], dst, ss + s, at, (owner_c, s))
            near = local(src.at[:, s], dst, at)
            here = is_own & (r == s)

            @pl.when(jnp.logical_not(here))
            def _(far=far):
                far.start()

            @pl.when(here)
            def _(near=near):
                near.start()

            def done(far=far, here=here):
                @pl.when(jnp.logical_not(here))
                def _():
                    far.wait_send()

            last.append(done)

    def landed(land, rs, out, first):
        for i in range(2):
            for kk in range(2):
                place = land.at[i, pl.ds(2 * kk, 2)]
                local(place, place, rs + 2 * i + kk).wait()
        for i in range(2):
            tok[first + i] = dot_l(pm[...], land[i].reshape(256, D)).astype(BF)
        cp = local(tok.at[pl.ds(first, 2)], out, sem())
        cp.start()
        last.append(cp.wait)

    ro_out, ro_gin = sem(4), sem(4)

    b_cp.wait()

    def out_half(n, bd):
        jj = n // 2
        g = 2 * k + jj
        rows = pl.ds(pl.multiple_of((n % 2) * 128, 128), 128)
        h64 = pl.ds((n % 2) * 2, 2)
        o = oh[g, rows, :]
        ao = dot(att[g, rows, :], wo[...]) + par[10:11, D : 2 * D]
        m = tok[g, rows, :].astype(F32) + piece(o, 2) * ao
        gp[jj, rows, :] = m
        branch = mid[jj, rows, :] + v.brcv[jj, h64].reshape(128, D).astype(F32) + par[10:11, 0:D]
        stg_c[jj, h64] = (m + piece(o, 5) * branch).astype(BF).reshape(2, 64, D)
        low = (cot[g, rows, :].astype(F32) * branch).astype(BF)
        mg1[...] += dot_l(place_rows(lv[g, rows, :], 3), low)[0:16]
        return bd + jnp.sum(bg[g, rows, :].astype(F32), axis=0, keepdims=True)

    sg1[10:11, 0:D] = lax.fori_loop(0, 4, out_half, o_rows)
    hand_back(stg_c, v.oland, ro_out)
    def hidden_back(pos, _):
        b = block_at(pos)
        lo = pl.multiple_of(b * HB, 128)
        wide = pl.multiple_of(HB * (2 * b + k), 128)
        pl.when(pos == 2)(down_total)

        def down_grad(pr, _):
            both = dot_t(bg[pl.ds(2 * pr, 2)].reshape(512, D), wdn[pl.ds(lo, HB), :])
            for pc in range(2):
                g = 2 * pr + pc
                t = both[pc * 256 : pc * 256 + 256] * upg[g, :, pl.ds(lo, HB)].astype(F32)
                t = t.astype(BF)
                gb[g, 16:272, :] = t
                gs[g, 16:272, :] = shifted(t.astype(F32), pc).astype(BF)
            return 0

        lax.fori_loop(0, 2, down_grad, 0)

        def conv_back(lt, _):
            l0 = pl.multiple_of(lt * 128, 128)
            ln = pl.ds(l0, 128)
            kr = [par[t : t + 1, pl.ds(wide + l0, 128)] for t in range(9)]
            gk = [jnp.zeros((8, 128), F32) for _ in range(10)]
            for g in range(4):
                for h in range(2):
                    here = upr[g, h * 128 : h * 128 + 128, pl.ds(lo + l0, 128)].astype(F32)

                    def load(gsrc, ro, moved):
                        return (gs if moved else gb)[gsrc, pl.ds(16 + 16 * ro + 128 * h, 128), ln]

                    acc = conv_both(load, here, kr, gk, taps_of(g // 2, g % 2, True))
                    low = acc.astype(BF)
                    upg[g, h * 128 : h * 128 + 128, pl.ds(lo + l0, 128)] = low
                    gk[9] = gk[9] + fold_rows(low.astype(F32))
            for t in range(10):
                sg1[t : t + 1, pl.ds(wide + l0, 128)] = jnp.sum(gk[t], axis=0, keepdims=True)
            return 0

        lax.fori_loop(0, 3, conv_back, 0)

        return 0

    lax.fori_loop(0, 4, hidden_back, 0)

    for n in range(2):
        cols = slice(n * HB, n * HB + HB)
        stg_t[:, :, :, cols] = half_f(other2, n).astype(BF).reshape(2, 4, 64, HB)
    f_cp = remote(stg_t, v.frcv, sem(), sem(), sib)
    f_cp.start()
    for n in range(2):
        cols = slice(n * HB, n * HB + HB)
        mid[:, :, cols] = half_f(mine2, n).reshape(2, 256, HB)

    def pos_of(b):
        bx, by = b % 2, b // 2
        fx = (bx - x) * (bx - x)
        fy = (by - y) * (by - y)
        return 2 * (1 - fx) + 1 - fy

    def grad_up(nt, _):
        ln = pl.ds(pl.multiple_of(nt * 256, 128), 256)
        got = dot(fint[...], upg[:, :, ln].reshape(1024, 256)).astype(BF)
        for b in range(4):
            upr[pos_of(b), 0:192, ln] = got[b * 192 : b * 192 + 192]
        return 0

    lax.fori_loop(0, 6, grad_up, 0)
    sum_u.s0()
    line_d.s1()
    f_cp.wait()

    def two_back(n, bo):
        jj = n // 2
        g = 2 * k + jj
        rows = pl.ds(pl.multiple_of((n % 2) * 128, 128), 128)
        h64 = pl.ds((n % 2) * 2, 2)
        o = oh[g, rows, :]
        gate1 = piece(o, 2)
        nrm, inv = norm_parts(gp[jj, rows, :])
        fg = mid[jj, rows, :] + v.frcv[jj, h64].reshape(128, D).astype(F32)
        mg = cot[g, rows, :].astype(F32) + norm_back(fg * (1.0 + piece(o, 4)), nrm, inv)
        mid[jj, rows, :] = mg
        ag = (gate1 * mg).astype(BF)
        tmpa[g, rows, :] = ag
        ids = lv[g, rows, :]
        ao = dot(att[g, rows, :], wo[...]) + par[10:11, D : 2 * D]
        total = dot_l(place_rows(ids, 0), (mg * ao).astype(BF))
        total = total + dot_l(place_rows(ids, 1), fg.astype(BF))
        total = total + dot_l(place_rows(ids, 2), (fg * nrm).astype(BF))
        mg1[...] += total[0:16]
        return bo + jnp.sum(ag.astype(F32), axis=0, keepdims=True)

    sg1[10:11, D : 2 * D] = lax.fori_loop(0, 4, two_back, o_rows)
    ag_place = tmpa.at[pl.ds(2 * k, 2)]
    ag_cp = swap(ag_place, ag_place, sib)

    sum_u.s1()
    sum_u.s2()
    mgs1[...] = mg1[...].astype(BF)
    mg_cp = swap(mgs1, mgr1, sib)
    all1.go(0)

    ag_cp.wait_recv()
    mg_cp.wait_recv()
    gat1.s0()
    dqkv = act
    kr_rows = pl.ds(kcol, HB)

    def heads_back(g, _):
        pl.when(g == 2)(line_d.s2)
        oq, mk = masks_of(g)
        mk2 = jnp.concatenate([mk, mk], axis=0)
        for h in range(2):
            at = pl.ds(pl.multiple_of(g * 256 + h * 128, 128), 128)
            fint[:, at] = att[g, h * 128 : h * 128 + 128, :].astype(F32).T.astype(BF)
        act[g, :, 3 * HB : 4 * HB] = dot_t(tmpa[g], wo[kr_rows, :]).astype(BF)
        for hp in range(3):
            qp = qkv[g, :, hp * 128 : hp * 128 + 128]
            kp = qkv[g, :, HB + hp * 128 : HB + hp * 128 + 128]
            vp = qkv[g, :, 2 * HB + hp * 128 : 2 * HB + hp * 128 + 128]
            dop = act[g, :, 3 * HB + hp * 128 : 3 * HB + hp * 128 + 128]
            k2 = jnp.concatenate([kp * lmb[0], kp * lmb[1]], axis=0)
            v2 = jnp.concatenate([vp * lmb[0], vp * lmb[1]], axis=0)
            s = dot_t(jnp.concatenate([k2, mk2], axis=1), jnp.concatenate([qp, oq], axis=1))
            dp = dot_t(v2, dop)
            probs, dss = [], []
            for h in range(2):
                sh = s[h * 256 : h * 256 + 256]
                dph = dp[h * 256 : h * 256 + 256]
                e = jnp.exp(sh - jnp.max(sh, axis=0, keepdims=True))
                prob = e * (1.0 / jnp.sum(e, axis=0, keepdims=True))
                delta = jnp.sum(prob * dph, axis=0, keepdims=True)
                probs.append(prob.astype(BF))
                dss.append((prob * (dph - delta)).astype(BF))
            ds2 = jnp.concatenate(dss, axis=0)
            dv2 = dot(jnp.concatenate(probs, axis=0), dop)
            dk2 = dot(ds2, qp)
            dq = dot_l(ds2, k2) * 0.125
            dv = dv2[0:256] * lmf[0] + dv2[256:512] * lmf[1]
            dk = dk2[0:256] * lmf[0] + dk2[256:512] * lmf[1]
            dqkv[g, :, hp * 128 : hp * 128 + 128] = dq.astype(BF)
            dqkv[g, :, HB + hp * 128 : HB + hp * 128 + 128] = dk.astype(BF)
            dqkv[g, :, 2 * HB + hp * 128 : 2 * HB + hp * 128 + 128] = dv.astype(BF)
        return 0

    lax.fori_loop(0, 4, heads_back, 0)
    all1.end(0)
    all1.go(1)

    def proj_back(g, _):
        upg[g, :, 0:D] = dot_t(dqkv[g, :, 0 : 3 * HB], wq[...]).astype(BF)
        return 0

    lax.fori_loop(0, 4, proj_back, 0)
    cg_cp = swap(upg.at[:, :, pl.ds(0, D)], bg, sib)

    def grad_qkv(nt, _):
        ln = pl.ds(pl.multiple_of(nt * HB, 128), HB)
        got = dot(c1t[...], dqkv[:, :, ln].reshape(1024, HB)).astype(BF)
        for b in range(4):
            wup[pl.ds(pl.multiple_of(192 * pos_of(b), 64), 192), ln] = got[b * 192 : b * 192 + 192]
        return 0

    lax.fori_loop(0, 3, grad_qkv, 0)
    sum_q.s0()
    all1.end(1)
    all1.go(2)
    gat1.s1()
    sg2[9:10, pl.ds(kcol, HB)] = jnp.sum(
        jnp.sum(dqkv[:, :, 0:HB].astype(F32), axis=0), axis=0, keepdims=True
    )
    sg2[10:11, pl.ds(kcol, HB)] = jnp.sum(
        jnp.sum(dqkv[:, :, 2 * HB : 3 * HB].astype(F32), axis=0), axis=0, keepdims=True
    )
    def grad_out(pos, _):
        rows = pl.ds(pl.multiple_of(96 * (2 * block_at(pos) + k), 32), 96)
        gwo[pos] = dot(fint[rows, :], tmpa[...].reshape(1024, D)).astype(BF)
        pl.when(pos == 0)(sum_o.s0)
        return 0

    lax.fori_loop(0, 4, grad_out, 0)
    total_u = sum_u.s3()
    upr[3, 0:192, :] = total_u.astype(BF)
    half_u = swap(
        upr.at[3, pl.ds(pl.multiple_of(96 * (1 - k), 32), 96), :], v.su, sib
    )
    mine96 = pl.ds(pl.multiple_of(96 * k, 32), 96)
    for b in range(4):
        o_wup[:, pl.ds(pl.multiple_of(HB * (2 * b + k), 128), HB)] = upr[3, mine96, b * HB : (b + 1) * HB]
    half_u.wait()
    last.remove(half_u.wait_send)
    for b in range(4):
        o_wup[:, pl.ds(pl.multiple_of(HB * (2 * b + 1 - k), 128), HB)] = v.su[:, b * HB : (b + 1) * HB]
    line_u.s0()
    all1.plane()
    line_a.s0()
    cg_cp.wait_recv()

    def cg_sum(pr, _):
        for pc in range(2):
            g = 2 * pr + pc
            t = (upg[g, :, 0:D].astype(F32) + bg[g].astype(F32)).astype(BF)
            sh = shifted(t.astype(F32), pc).astype(BF)
            ub[g, 16:272, :] = t[:, 0:HB]
            gb[g, 16:272, :] = t[:, HB:D]
            us[g, 16:272, :] = sh[:, 0:HB]
            gs[g, 16:272, :] = sh[:, HB:D]
        return 0

    lax.fori_loop(0, 2, cg_sum, 0)
    sum_q.s1()
    sum_q.s2()
    gat1.s2()
    for hh in range(2):
        base, side = (ub, us) if hh == 0 else (gb, gs)

        def conv_one_back(lt, _, hh=hh, base=base, side=side):
            l0 = pl.multiple_of(lt * 128, 128)
            la = pl.multiple_of(hh * HB + lt * 128, 128)
            kr = [par[11 + t // 4 : 12 + t // 4, pl.ds((t % 4) * D + la, 128)] for t in range(9)]
            gk = [jnp.zeros((8, 128), F32) for _ in range(9)]
            for pc in range(2):
                for h in range(2):
                    here = ain[2 * k + pc, 16 + 128 * h : 144 + 128 * h, pl.ds(la, 128)].astype(F32)

                    def load(gsrc, ro, moved):
                        at = pl.ds(pl.multiple_of(16 + 16 * ro + 128 * h, 16), 128)
                        return (side if moved else base)[gsrc, at, pl.ds(l0, 128)]

                    acc = conv_both(load, here, kr, gk, taps_of(k, pc, True))
                    gp[pc, h * 128 : h * 128 + 128, pl.ds(la, 128)] = acc
            for t in range(9):
                sg2[t : t + 1, pl.ds(la, 128)] = jnp.sum(gk[t], axis=0, keepdims=True)
            return 0

        lax.fori_loop(0, 3, conv_one_back, 0)
    all2.go(0)
    line_u.s1()

    def one_back(n, _):
        jj = n // 2
        g = 2 * k + jj
        rows = pl.ds(pl.multiple_of((n % 2) * 128, 128), 128)
        h64 = pl.ds((n % 2) * 2, 2)
        nrm, inv = norm_parts(tok[g, rows, :].astype(F32))
        ig = gp[jj, rows, :]
        gi = mid[jj, rows, :] + norm_back(ig * (1.0 + piece(oh[g, rows, :], 1)), nrm, inv)
        stg_t[jj, h64] = gi.astype(BF).reshape(2, 64, D)
        ids = lv[g, rows, :]
        low = ig.astype(BF)
        scl = (ig * nrm).astype(BF)
        total = dot_l(place_rows(ids, 0), low[:, 0:HB]) + dot_l(place_rows(ids, 1), low[:, HB:D])
        total = total + dot_l(place_rows(ids, 2), scl[:, 0:HB]) + dot_l(place_rows(ids, 3), scl[:, HB:D])
        mg2[...] += total[0:16]
        return 0

    lax.fori_loop(0, 4, one_back, 0)
    mgs2[...] = mg2[...].astype(BF)
    mg2_cp = swap(mgs2, mgr2, sib)

    sum_o.s1()
    sum_o.s2()
    all2.end(0)
    all2.go(1)
    line_a.s1()
    mg2_cp.wait_recv()
    gat2.s0()
    hand_back(stg_t, v.gland, ro_gin)

    def load_again(p):
        return local(wada_h.at[:, pl.ds(p * D, D)], wdn.at[pl.ds((p % 2) * D, D), :], s_wa + p % 2)

    load_again(2).start()
    load_again(3).start()

    def pick(p):
        ri, ci = iota((16, 16), 0), iota((16, 16), 1)
        return ones_where((ri // 4 == r) & (ci == 4 * p + ri % 4))

    my1 = mga1[slot]
    my2 = mga2[slot]
    cg = jnp.zeros((16, D), F32)
    for p in range(2, 6):
        load_again(p).wait()
        lhs = dot(pick(p - 2), my1).astype(BF)
        cg = cg + dot_t(lhs, wdn[(p % 2) * D : (p % 2) * D + D, :])
        load_again((p + 2) % 6).start()
    for p in range(2):
        load_again(p).wait()
        for h in range(2):
            lhs = dot(pick(2 * p + h), my2).astype(BF)
            cg = cg + dot_t(lhs, wdn[p * D : p * D + D, h * HB : h * HB + HB])
    cond = condc[...]
    sig = 1.0 / (1.0 + jnp.exp(-cond))
    cgsum = v.cgsum
    cgsum[...] = cg * (sig * (1.0 + cond * (1.0 - sig)))
    crcv = v.crcv
    cr, cs = sem(2), sem(4)
    for s in range(4):
        src = cgsum.at[pl.ds(pl.multiple_of(8 * owner, 8), 8), :]
        dst = crcv.at[r % 2]
        far = remote(src, dst, cs + s, cr + r % 2, (c, s))
        near = local(src, dst, cr + r % 2)

        @pl.when(is_own & (r != s))
        def _(far=far):
            far.start()

        @pl.when(is_own & (r == s))
        def _(near=near):
            near.start()

        def done(far=far, s=s):
            @pl.when(is_own & (r != s))
            def _():
                far.wait_send()

        last.append(done)

    total_q = sum_q.s3()
    wup[576:768, 0 : 3 * HB] = total_q.astype(BF)
    half_q = swap(
        wup.at[pl.ds(pl.multiple_of(576 + 96 * (1 - k), 32), 96), pl.ds(0, 3 * HB)], v.sq, sib
    )
    for part in range(3):
        o_wqkv[:, pl.ds(pl.multiple_of(part * D + HB * k, 128), HB)] = wup[
            pl.ds(pl.multiple_of(576 + 96 * k, 32), 96), part * HB : (part + 1) * HB
        ]
    half_q.wait_recv()
    for part in range(3):
        o_wqkv[:, pl.ds(pl.multiple_of(part * D + HB * (1 - k), 128), HB)] = v.sq[:, part * HB : (part + 1) * HB]
    line_q.s0()
    all2.end(1)
    all2.go(2)
    line_u.s2()
    o_wout[...] = sum_o.s3().astype(BF)
    line_o.s0()
    all2.plane()
    line_b.s0()
    gat2.s1()
    line_q.s1()
    line_o.s1()
    line_a.s2()
    gat2.s2()
    line_b.s1()
    for done in tok_passed:
        done()
    landed(v.oland, ro_out, o_out, 0)

    low_y.wait_recv()
    ri, ci = iota((96, D), 0), iota((96, D), 1)
    cond_t = dot_t(ones_where(ci == 96 * c + ri), clow[...].reshape(64, D)).astype(BF)
    ej, en = iota((64, 256), 0), iota((64, 256), 1)
    bn = iota((8, 256), 1)

    def spread(p):
        return dot(cond_t, ones_where((en // 16 == ej // 4) & (en % 16 == 4 * p + ej % 4))).astype(BF)

    gat1.s3()
    o_bada[...] = jnp.zeros((8, 6 * D), F32)
    every1 = mga1[...].reshape(256, D)

    def ada_out(p):
        cp = local(wdn.at[pl.ds(96 * p, 96), :], o_wada.at[:, pl.ds(p * D, D)], sem())
        cp.start()
        last.append(cp.wait)

    for p in range(4):
        wdn[(p + 2) * 96 : (p + 3) * 96, :] = dot(spread(p), every1).astype(BF)
        ada_out(p + 2)
        o_bada[0:1, (p + 2) * D : (p + 3) * D] = dot(ones_where((bn % 16) // 4 == p), every1)[0:1]
    line_q.s2()
    line_o.s2()
    gat2.s3()
    every2 = mga2[...].reshape(256, HB)
    for p in range(4):
        half = (p % 2) * HB
        wdn[p // 2 * 96 : p // 2 * 96 + 96, half : half + HB] = dot(spread(p), every2).astype(BF)
        o_bada[0:1, p * HB : (p + 1) * HB] = dot(ones_where((bn % 16) // 4 == p), every2)[0:1]
    ada_out(0)
    ada_out(1)
    line_b.s2()
    line_d.s3()
    line_u.s3()
    landed(v.gland, ro_gin, o_gin, 2)
    for i in range(2):
        local(crcv.at[i], crcv.at[i], cr + i).wait()
    both = crcv[0] + crcv[1]
    for i in range(2):
        o_cond[i] = both[4 * i : 4 * i + 4]
    line_a.s3()
    o_sg1[...] = v.sg1s[0].astype(F32)
    line_b.s3()
    o_sg2[...] = v.sg2s[0].astype(F32)
    line_o.s3()
    line_q.s3()
    for done in last:
        done()
    for s in (sum_d, sum_u, sum_o, sum_q):
        s.sent()
    assert count[0] <= N_SEMS, count[0]


def finish(
    out, gin, gcond, wada, bada_h, sg1_h, sg2_h, wqkv, wout, wup, wdn,
    f_out, f_gin, f_gcond, f_wada, f_bada, f_conv1, f_wqkv, f_bqv, f_wout, f_bout, f_wup, f_bup, f_conv2, f_wdn,
    f_bdn, sems, *bufs,
):
    c = lax.axis_index("canvas")
    bada, sg1, sg2, narrow, wide = bufs[0], bufs[1], bufs[2], bufs[3:9], bufs[9:15]
    small = ((sg1_h, sg1), (sg2_h, sg2), (bada_h, bada))
    large = ((wada, f_wada), (gin, f_gin), (wup, f_wup), (wdn, f_wdn), (wqkv, f_wqkv), (wout, f_wout))
    ins = [pltpu.make_async_copy(src, buf, sems.at[i]) for i, ((src, _), buf) in enumerate(zip(large, narrow))]
    ins += [pltpu.make_async_copy(src, buf, sems.at[6 + i]) for i, (src, buf) in enumerate(small)]
    outs = [pltpu.make_async_copy(buf, dst, sems.at[9 + i]) for i, ((_, dst), buf) in enumerate(zip(large, wide))]
    ins.append(pltpu.make_async_copy(out, bufs[15], sems.at[15]))
    ins.append(pltpu.make_async_copy(gcond, f_gcond, sems.at[16]))
    outs.append(pltpu.make_async_copy(bufs[15], f_out, sems.at[15]))
    for cp in ins:
        cp.start()
    for i in range(6):
        ins[i].wait()
        wide[i][...] = narrow[i][...].astype(F32)
        outs[i].start()
    for cp in ins[6:]:
        cp.wait()
    outs[6].start()

    def cut(rows, n):
        wide = rows.shape[1]
        return pltpu.roll(rows, lax.rem(wide - c * n, wide), 1)[:, 0:n]

    f_bada[...] = cut(bada[...], 576)[0:1]
    f_conv1[...] = cut(sg2[...], 96)[0:9]
    both = jnp.concatenate([sg2[8:16, :], sg2[8:16, :]], axis=1)
    f_bqv[...] = cut(jnp.where(iota((8, 2 * D), 1) < D, both, pltpu.roll(both, 7, 0)), 192)[1:2]
    f_bout[...] = cut(sg1[8:16, D : 2 * D], 96)[2:3]
    f_bdn[...] = cut(sg1[8:16, 0:D], 96)[2:3]
    ln = pl.ds(pl.multiple_of(c * HB, 128), HB)
    f_bup[...] = sg1[9:10, ln]
    f_conv2[...] = sg1[0:9, ln]
    for cp in outs:
        cp.wait()


def fast_shards(
    tokens, latent, condition, w_ada, b_ada, conv_attn, w_qkv, bias_qv, w_out, b_out,
    w_up, b_up, conv_ffn, w_down, b_down, cotangent,
):
    anyspace = pl.BlockSpec(memory_space=pl.ANY)
    vm = pl.BlockSpec(memory_space=pltpu.VMEM)
    outs = (
        ((2, 256, D), BF),
        ((2, 256, D), BF),
        ((2, 4, D), F32),
        ((96, 6 * D), BF),
        ((8, 6 * D), F32),
        ((16, FF), F32),
        ((16, D), F32),
        ((96, 3 * D), BF),
        ((96, D), BF),
        ((96, FF), BF),
        ((HB, D), BF),
    )
    got = pl.pallas_call(
        whole_block,
        out_shape=[jax.ShapeDtypeStruct(s, t) for s, t in outs],
        in_specs=[anyspace, anyspace, vm, vm] + [anyspace] * 5 + [vm] * 7,
        out_specs=[anyspace, anyspace, vm, anyspace] + [vm] * (len(outs) - 4),
        scratch_shapes=[pltpu.SemaphoreType.DMA((N_SEMS,))] + [pltpu.VMEM(s, t) for s, t in SCRATCH.values()],
        compiler_params=pltpu.CompilerParams(
            collective_id=0, has_side_effects=True, vmem_limit_bytes=VMEM_LIMIT
        ),
        name="block",
    )(
        tokens, cotangent, latent, condition, w_ada, w_qkv, w_out, w_up, w_down,
        b_ada, conv_attn, bias_qv, b_out, b_up, conv_ffn, b_down,
    )
    big = ((96, 6 * D), (2, 256, D), (96, FF), (HB, D), (96, 3 * D), (96, D))
    shapes = (
        (2, 256, D), (2, 256, D), (2, 4, D), (96, 6 * D), (1, 576), (9, 96), (96, 3 * D), (1, 192), (96, D), (1, 96),
        (96, FF), (1, HB), (9, HB), (HB, D), (1, 96),
    )
    out, gin, gcond, wada, bada, conv1, wqkv, bqv, wout, bout, wup, bup, conv2, wdn, bdn = pl.pallas_call(
        finish,
        out_shape=[jax.ShapeDtypeStruct(s, F32 if i else BF) for i, s in enumerate(shapes)],
        in_specs=[anyspace] * 11,
        out_specs=[anyspace if i in (0, 1, 3, 6, 8, 10, 13) else vm for i in range(len(shapes))],
        scratch_shapes=[pltpu.SemaphoreType.DMA((17,))]
        + [pltpu.VMEM(s, F32) for s in ((8, 6 * D), (16, FF), (16, D))]
        + [pltpu.VMEM(s, BF) for s in big]
        + [pltpu.VMEM(s, F32) for s in big]
        + [pltpu.VMEM((2, 256, D), BF)],
        compiler_params=pltpu.CompilerParams(vmem_limit_bytes=VMEM_LIMIT),
        name="finish",
    )(*got)
    flat = lambda a: a.reshape(a.shape[1])
    return (
        out, gin, gcond, wada, flat(bada), conv1, wqkv, flat(bqv), wout, flat(bout),
        wup, flat(bup), conv2, wdn, flat(bdn),
    )


def solution(mesh):
    placed = (
        P("canvas", "rows", None),
        P("canvas", "rows"),
        P("canvas", None, None),
        P(),
        P(),
        P(),
        P(),
        P(),
        P(),
        P(),
        P(),
        P(),
        P(),
        P(),
        P(),
        P("canvas", "rows", None),
    )
    fits = mesh.shape["rows"] == 4 and mesh.shape["canvas"] == 8
    return jax.shard_map(
        fast_shards if fits else shards,
        mesh=mesh,
        in_specs=placed,
        out_specs=(
            P("canvas", "rows", None),
            P("canvas", "rows", None),
            P("canvas", None, None),
            P("canvas", None),
            P("canvas"),
            P(None, "canvas"),
            P("canvas", None),
            P("canvas"),
            P("canvas", None),
            P("canvas"),
            P("canvas", None),
            P("canvas"),
            P(None, "canvas"),
            P("canvas", None),
            P("canvas"),
        ),
        check_vma=False,
    )
```

```python
from types import SimpleNamespace

import jax
import jax.numpy as jnp
from jax import lax
from jax.experimental import pallas as pl
from jax.experimental.pallas import tpu as pltpu
from jax.sharding import PartitionSpec as P

HEADS = 12
HEAD_DIM = 64
SIDE = 32


EPSILON = 1e-06
NEG_FILL = -1e30
PRECISE = lax.Precision.HIGHEST
VMEM_LIMIT = 65400 * 2**10


def padded_2(cells, sides, width):
    for axis, dim in sides:
        count = lax.axis_size(axis)
        ends = count - 1
        head = lax.slice_in_dim(cells, 0, width, axis=dim)
        tail = lax.slice_in_dim(cells, cells.shape[dim] - width, cells.shape[dim], axis=dim)
        cells = jnp.concatenate(
            [
                lax.ppermute(tail, axis, [(i, (i + 1) % count) for i in range(ends)]),
                cells,
                lax.ppermute(head, axis, [((i + 1) % count, i) for i in range(ends)]),
            ],
            axis=dim,
        )
    return cells


def passed_along(block, axis, distance):
    devices = range(lax.axis_size(axis))
    route = [((i - distance) % len(devices), i) for i in devices]
    return lax.ppermute(block, axis, route)


def layer_norm(values):
    centered = values - jnp.mean(values, axis=-1, keepdims=True)
    return centered * lax.rsqrt(jnp.mean(centered * centered, axis=-1, keepdims=True) + EPSILON)


def modulate_norm(values, shift, scale_part):
    return layer_norm(values) * (1.0 + scale_part) + shift


def gelu_tanh(values):
    return jax.nn.gelu(values, approximate=True)


def pad_columns(field):
    return jnp.pad(field, ((0, 0), (0, 0), (1, 1), (0, 0)))


def grid_taps(padded, kernel, rows_here, cols_here):
    summed = padded[:, 0:rows_here, 0:cols_here].astype(jnp.float32) * kernel[0]
    for tap_row in range(3):
        for tap_col in range(3):
            if tap_row + tap_col > 0:
                window = padded[
                    :, tap_row : tap_row + rows_here, tap_col : tap_col + cols_here
                ].astype(jnp.float32)
                summed = summed + window * kernel[3 * tap_row + tap_col]
    return summed


def kernel_grad(padded, grad_grid):
    rows_here = grad_grid.shape[1]
    cols_here = grad_grid.shape[2]
    grad_f = grad_grid.astype(jnp.float32)
    tap_sums = []
    for tap_row in range(3):
        for tap_col in range(3):
            window = padded[:, tap_row : tap_row + rows_here, tap_col : tap_col + cols_here].astype(
                jnp.float32
            )
            tap_sums.append(jnp.sum(window * grad_f, axis=(0, 1, 2)))
    return jnp.stack(tap_sums)


def to_groups(field, rows_here):
    canvases = field.shape[0]
    channels = field.shape[-1]
    shaped = field.reshape(canvases, rows_here // 2, 2, SIDE // 2, 2, channels)
    return shaped.transpose(0, 2, 4, 1, 3, 5).reshape(
        canvases, 4, rows_here // 2 * (SIDE // 2), channels
    )


def from_groups(field, rows_here):
    canvases = field.shape[0]
    channels = field.shape[-1]
    shaped = field.reshape(canvases, 2, 2, rows_here // 2, SIDE // 2, channels)
    return shaped.transpose(0, 3, 1, 4, 2, 5).reshape(canvases, rows_here * SIDE, channels)


def block_scores(query_heads, key_piece, query_lat, key_lat):
    canvases = key_piece.shape[0]
    count = key_piece.shape[2]
    key_heads = key_piece.reshape(canvases, 4, count, HEADS, HEAD_DIM)
    scores = jnp.einsum(
        "cgqhe,cgkhe->cghqk", query_heads, key_heads, preferred_element_type=jnp.float32
    ) * HEAD_DIM ** (-0.5)
    same_latent = query_lat[:, :, None, :, None] == key_lat[:, :, None, None, :]
    return (scores, same_latent, key_heads)


def shards(
    tokens,
    latent,
    condition,
    w_ada,
    b_ada,
    conv_attn,
    w_qkv,
    bias_qv,
    w_out,
    b_out,
    w_up,
    b_up,
    conv_ffn,
    w_down,
    b_down,
    cotangent,
):
    canvases = tokens.shape[0]
    local_tokens = tokens.shape[1]
    model_width = tokens.shape[2]
    ffn_width = w_up.shape[1]
    rows_here = local_tokens // SIDE
    group_len = local_tokens // 4
    score_scale = HEAD_DIM ** (-0.5)
    tokens_f = tokens.astype(jnp.float32)
    onehot = (latent[..., None] == jnp.arange(4)).astype(jnp.float32)
    silu_cond, silu_pull = jax.vjp(jax.nn.silu, condition)
    cond_low = silu_cond.astype(jnp.bfloat16)
    modulation = jnp.einsum(
        "ckd,df->ckf", cond_low, w_ada, preferred_element_type=jnp.float32
    ) + b_ada.astype(jnp.float32)
    per_token = jnp.einsum("cnk,ckf->cnf", onehot, modulation, precision=PRECISE)
    shift_one, scale_one, gate_one, shift_two, scale_two, gate_two = jnp.split(
        per_token, 6, axis=-1
    )
    h_one, norm_one_pull = jax.vjp(modulate_norm, tokens_f, shift_one, scale_one)
    attn_in = h_one.astype(jnp.bfloat16).reshape(canvases, rows_here, SIDE, model_width)
    attn_pad = pad_columns(padded_2(attn_in, (("rows", 1),), 1))
    conv_attn_f = conv_attn.astype(jnp.float32)
    conv_low = (
        grid_taps(attn_pad, conv_attn_f, rows_here, SIDE)
        .astype(jnp.bfloat16)
        .reshape(-1, model_width)
    )
    bias_full = jnp.concatenate(
        [bias_qv[:model_width], jnp.zeros((model_width,), jnp.bfloat16), bias_qv[model_width:]]
    ).astype(jnp.float32)
    projected = (jnp.dot(conv_low, w_qkv, preferred_element_type=jnp.float32) + bias_full).astype(
        jnp.bfloat16
    )
    grouped = to_groups(projected.reshape(canvases, local_tokens, 3 * model_width), rows_here)
    queries = grouped[..., :model_width]
    key_rows = grouped[..., model_width : 2 * model_width]
    value_rows = grouped[..., 2 * model_width :]
    lat_groups = to_groups(latent[..., None], rows_here)[..., 0]
    all_lat = lax.all_gather(lat_groups, "rows", axis=2, tiled=True)
    query_heads = queries.reshape(canvases, 4, group_len, HEADS, HEAD_DIM)
    start_best = jnp.full((canvases, 4, HEADS, group_len), NEG_FILL, jnp.float32)
    best = start_best
    key_piece = lax.all_gather(key_rows, "rows", axis=2, tiled=True)
    value_piece = lax.all_gather(value_rows, "rows", axis=2, tiled=True)
    count = key_piece.shape[2]
    fold_scores, fold_same_latent, fold_key_heads = block_scores(
        query_heads, key_piece, lat_groups, all_lat
    )
    masked = jnp.where(fold_same_latent, fold_scores, NEG_FILL)
    newest = jnp.maximum(best, jnp.max(masked, axis=-1))
    weights = jnp.where(fold_same_latent, jnp.exp(masked - newest[..., None]), 0.0)
    fold_value_heads = value_piece.astype(jnp.float32).reshape(canvases, 4, count, HEADS, HEAD_DIM)
    accum = jnp.einsum("cghqk,cgkhe->cghqe", weights, fold_value_heads, precision=PRECISE)
    best, weight_sum, accum = (newest, jnp.sum(weights, axis=-1), accum)
    attn_heads = accum / weight_sum[..., None]
    log_norm = best + jnp.log(weight_sum)
    attended = from_groups(
        attn_heads.transpose(0, 1, 3, 2, 4).reshape(canvases, 4, group_len, model_width), rows_here
    )
    attended_low = attended.astype(jnp.bfloat16).reshape(-1, model_width)
    attn_out = (
        jnp.dot(attended_low, w_out, preferred_element_type=jnp.float32) + b_out.astype(jnp.float32)
    ).reshape(canvases, local_tokens, model_width)
    middle = tokens_f + gate_one * attn_out
    h_two, norm_two_pull = jax.vjp(modulate_norm, middle, shift_two, scale_two)
    ffn_in = h_two.astype(jnp.bfloat16).reshape(-1, model_width)
    up_rows = (
        jnp.dot(ffn_in, w_up, preferred_element_type=jnp.float32) + b_up.astype(jnp.float32)
    ).astype(jnp.bfloat16)
    up_grid = up_rows.reshape(canvases, rows_here, SIDE, ffn_width)
    up_pad = pad_columns(padded_2(up_grid, (("rows", 1),), 1))
    conv_ffn_f = conv_ffn.astype(jnp.float32)
    conv_two = grid_taps(up_pad, conv_ffn_f, rows_here, SIDE)
    activated, gelu_pull = jax.vjp(gelu_tanh, conv_two)
    act_low = activated.astype(jnp.bfloat16).reshape(-1, ffn_width)
    branch = (
        jnp.dot(act_low, w_down, preferred_element_type=jnp.float32) + b_down.astype(jnp.float32)
    ).reshape(canvases, local_tokens, model_width)
    result = (middle + gate_two * branch).astype(jnp.bfloat16)
    out_grad = cotangent.astype(jnp.float32)
    branch_grad = (gate_two * out_grad).astype(jnp.bfloat16).reshape(-1, model_width)
    gate_two_grad = out_grad * branch
    g_b_down = jnp.sum(branch_grad.astype(jnp.float32), axis=0)
    g_w_down = jnp.dot(act_low.T, branch_grad, preferred_element_type=jnp.float32)
    act_grad = jnp.dot(branch_grad, w_down.T, preferred_element_type=jnp.float32).reshape(
        canvases, rows_here, SIDE, ffn_width
    )
    conv_two_grad = gelu_pull(act_grad)[0].astype(jnp.bfloat16)
    conv_two_pad = pad_columns(padded_2(conv_two_grad, (("rows", 1),), 1))
    up_grad = (
        grid_taps(conv_two_pad, conv_ffn_f[::-1], rows_here, SIDE)
        .astype(jnp.bfloat16)
        .reshape(-1, ffn_width)
    )
    g_conv_ffn = kernel_grad(up_pad, conv_two_grad)
    g_b_up = jnp.sum(up_grad.astype(jnp.float32), axis=0)
    g_w_up = jnp.dot(ffn_in.T, up_grad, preferred_element_type=jnp.float32)
    ffn_grad = jnp.dot(up_grad, w_up.T, preferred_element_type=jnp.float32).reshape(
        canvases, local_tokens, model_width
    )
    middle_part, shift_two_grad, scale_two_grad = norm_two_pull(ffn_grad)
    middle_grad = middle_part + out_grad
    gate_one_grad = middle_grad * attn_out
    attn_grad = (gate_one * middle_grad).astype(jnp.bfloat16).reshape(-1, model_width)
    g_b_out = jnp.sum(attn_grad.astype(jnp.float32), axis=0)
    g_w_out = jnp.dot(attended_low.T, attn_grad, preferred_element_type=jnp.float32)
    attended_grad = jnp.dot(attn_grad, w_out.T, preferred_element_type=jnp.float32).astype(
        jnp.bfloat16
    )
    grad_heads = to_groups(
        attended_grad.reshape(canvases, local_tokens, model_width), rows_here
    ).reshape(canvases, 4, group_len, HEADS, HEAD_DIM)
    grad_heads_f = grad_heads.astype(jnp.float32)
    delta = jnp.sum(grad_heads_f.transpose(0, 1, 3, 2, 4) * attn_heads, axis=-1)
    row_count = lax.axis_size("rows")
    here = lax.axis_index("rows")
    carried = jnp.stack([key_rows, value_rows])
    pending = jnp.zeros((2,) + key_rows.shape, jnp.float32)
    query_grad = jnp.zeros((canvases, 4, group_len, HEADS, HEAD_DIM), jnp.float32)
    for turn_index in range(row_count):
        source = (here - turn_index) % row_count
        key_lat = lax.dynamic_slice_in_dim(all_lat, source * group_len, group_len, 2)
        scores, same_latent, key_heads = block_scores(query_heads, carried[0], lat_groups, key_lat)
        value_heads = carried[1].reshape(canvases, 4, group_len, HEADS, HEAD_DIM)
        softmax_weights = jnp.where(same_latent, jnp.exp(scores - log_norm[..., None]), 0.0)
        weight_grad = jnp.einsum(
            "cgqhe,cgkhe->cghqk", grad_heads, value_heads, preferred_element_type=jnp.float32
        )
        score_grad = (softmax_weights * (weight_grad - delta[..., None])).astype(jnp.bfloat16)
        query_grad = query_grad + score_scale * jnp.einsum(
            "cghqk,cgkhe->cgqhe", score_grad, key_heads, preferred_element_type=jnp.float32
        )
        key_part = score_scale * jnp.einsum(
            "cghqk,cgqhe->cgkhe", score_grad, query_heads, preferred_element_type=jnp.float32
        )
        value_part = jnp.einsum(
            "cghqk,cgqhe->cgkhe", softmax_weights, grad_heads_f, precision=PRECISE
        )
        pending = pending + jnp.stack([key_part, value_part]).reshape(pending.shape)
        if turn_index + 1 < row_count:
            carried = passed_along(carried, "rows", 1)
        pending = passed_along(pending.astype(jnp.bfloat16), "rows", 1).astype(pending.dtype)
    query_low = query_grad.reshape(canvases, 4, group_len, model_width).astype(jnp.bfloat16)
    grouped_grad = jnp.concatenate(
        [query_low, pending[0].astype(jnp.bfloat16), pending[1].astype(jnp.bfloat16)], axis=-1
    )
    qkv_grad = from_groups(grouped_grad, rows_here).reshape(-1, 3 * model_width)
    qkv_grad_f = qkv_grad.astype(jnp.float32)
    g_bias_qv = jnp.concatenate(
        [
            jnp.sum(qkv_grad_f[:, :model_width], axis=0),
            jnp.sum(qkv_grad_f[:, 2 * model_width :], axis=0),
        ]
    )
    g_w_qkv = jnp.dot(conv_low.T, qkv_grad, preferred_element_type=jnp.float32)
    conv_one_grad = (
        jnp.dot(qkv_grad, w_qkv.T, preferred_element_type=jnp.float32)
        .astype(jnp.bfloat16)
        .reshape(canvases, rows_here, SIDE, model_width)
    )
    conv_one_pad = pad_columns(padded_2(conv_one_grad, (("rows", 1),), 1))
    attn_in_grad = grid_taps(conv_one_pad, conv_attn_f[::-1], rows_here, SIDE).reshape(
        canvases, local_tokens, model_width
    )
    g_conv_attn = kernel_grad(attn_pad, conv_one_grad)
    token_part, shift_one_grad, scale_one_grad = norm_one_pull(attn_in_grad)
    input_grad = token_part + middle_grad
    token_mod_grad = jnp.concatenate(
        [
            shift_one_grad,
            scale_one_grad,
            gate_one_grad,
            shift_two_grad,
            scale_two_grad,
            gate_two_grad,
        ],
        axis=-1,
    )
    mod_grad = jnp.einsum("cnk,cnf->ckf", onehot, token_mod_grad, precision=PRECISE)
    cond_f = cond_low.astype(jnp.float32)
    summed = (
        lax.psum(g_conv_attn.astype(jnp.bfloat16), "rows").astype(jnp.float32),
        lax.psum(g_w_qkv.astype(jnp.bfloat16), "rows").astype(jnp.float32),
        lax.psum(g_bias_qv.astype(jnp.bfloat16), "rows").astype(jnp.float32),
        lax.psum(g_w_out.astype(jnp.bfloat16), "rows").astype(jnp.float32),
        lax.psum(g_b_out.astype(jnp.bfloat16), "rows").astype(jnp.float32),
        lax.psum(g_w_up.astype(jnp.bfloat16), "rows").astype(jnp.float32),
        lax.psum(g_b_up.astype(jnp.bfloat16), "rows").astype(jnp.float32),
        lax.psum(g_conv_ffn.astype(jnp.bfloat16), "rows").astype(jnp.float32),
        lax.psum(g_w_down.astype(jnp.bfloat16), "rows").astype(jnp.float32),
        lax.psum(g_b_down.astype(jnp.bfloat16), "rows").astype(jnp.float32),
        lax.psum(mod_grad.astype(jnp.bfloat16), "rows").astype(jnp.float32),
    )
    mod_total = summed[10]
    g_w_ada = jnp.einsum("ckd,ckf->df", cond_f, mod_total, precision=PRECISE)
    g_b_ada = jnp.sum(mod_total, axis=(0, 1))
    shares = (
        lax.psum_scatter(
            g_w_ada.astype(jnp.bfloat16), "canvas", scatter_dimension=0, tiled=True
        ).astype(jnp.float32),
        lax.psum_scatter(
            g_b_ada.astype(jnp.bfloat16), "canvas", scatter_dimension=0, tiled=True
        ).astype(jnp.float32),
        lax.psum_scatter(
            summed[0].astype(jnp.bfloat16), "canvas", scatter_dimension=1, tiled=True
        ).astype(jnp.float32),
        lax.psum_scatter(
            summed[1].astype(jnp.bfloat16), "canvas", scatter_dimension=0, tiled=True
        ).astype(jnp.float32),
        lax.psum_scatter(
            summed[2].astype(jnp.bfloat16), "canvas", scatter_dimension=0, tiled=True
        ).astype(jnp.float32),
        lax.psum_scatter(
            summed[3].astype(jnp.bfloat16), "canvas", scatter_dimension=0, tiled=True
        ).astype(jnp.float32),
        lax.psum_scatter(
            summed[4].astype(jnp.bfloat16), "canvas", scatter_dimension=0, tiled=True
        ).astype(jnp.float32),
        lax.psum_scatter(
            summed[5].astype(jnp.bfloat16), "canvas", scatter_dimension=0, tiled=True
        ).astype(jnp.float32),
        lax.psum_scatter(
            summed[6].astype(jnp.bfloat16), "canvas", scatter_dimension=0, tiled=True
        ).astype(jnp.float32),
        lax.psum_scatter(
            summed[7].astype(jnp.bfloat16), "canvas", scatter_dimension=1, tiled=True
        ).astype(jnp.float32),
        lax.psum_scatter(
            summed[8].astype(jnp.bfloat16), "canvas", scatter_dimension=0, tiled=True
        ).astype(jnp.float32),
        lax.psum_scatter(
            summed[9].astype(jnp.bfloat16), "canvas", scatter_dimension=0, tiled=True
        ).astype(jnp.float32),
    )
    cond_grad = silu_pull(
        jnp.einsum("ckf,df->ckd", mod_total, w_ada.astype(jnp.float32), precision=PRECISE)
    )[0]
    return (
        result,
        input_grad,
        cond_grad,
        shares[0],
        shares[1],
        shares[2],
        shares[3],
        shares[4],
        shares[5],
        shares[6],
        shares[7],
        shares[8],
        shares[9],
        shares[10],
        shares[11],
    )

BF = jnp.bfloat16
F32 = jnp.float32
D = 768
FF = 3072
HB = 384
BIG = -1e30


def dot(a, b):
    return jnp.dot(a, b, preferred_element_type=F32)


def dot_t(a, b):
    return lax.dot_general(a, b, (((1,), (1,)), ((), ())), preferred_element_type=F32)


def dot_l(a, b):
    return lax.dot_general(a, b, (((0,), (0,)), ((), ())), preferred_element_type=F32)


def iota(shape, dim):
    return lax.broadcasted_iota(jnp.int32, shape, dim)


def ones_where(mask):
    return jnp.where(mask, 1.0, 0.0).astype(BF)


def taps_of(pr, pc, back):
    found = []
    for i in range(3):
        for j in range(3):
            di, dj = (1 - i, 1 - j) if back else (i - 1, j - 1)
            gr = pr if di == 0 else 1 - pr
            gc = pc if dj == 0 else 1 - pc
            ro = 0 if di == 0 else (pr - 1 if di < 0 else pr)
            co = 0 if dj == 0 else (2 * pc + dj - 1) // 2
            found.append((3 * i + j, 2 * gr + gc, ro, co != 0))
    return found


def shifted(rows, pc):
    n = rows.shape[0]
    col = iota(rows.shape, 0) % 16
    if pc == 1:
        return jnp.where(col == 0, 0.0, pltpu.roll(rows, 1, 0))
    return jnp.where(col == 15, 0.0, pltpu.roll(rows, n - 1, 0))


def conv_sum(load, kr, taps):
    total = None
    for t, gsrc, ro, moved in taps:
        term = load(gsrc, ro, moved).astype(F32) * kr[t]
        total = term if total is None else total + term
    return total


def conv_both(load, here, kr, gk, taps):
    total = None
    for t, gsrc, ro, moved in taps:
        src = load(gsrc, ro, moved).astype(F32)
        term = src * kr[t]
        total = term if total is None else total + term
        gk[t] = gk[t] + fold_rows(src * here)
    return total


def fold_rows(rows):
    return jnp.sum(rows.reshape(rows.shape[0] // 8, 8, 128), axis=0)


def norm_parts(v):
    mean = jnp.mean(v, axis=-1, keepdims=True)
    cen = v - mean
    inv = lax.rsqrt(jnp.mean(cen * cen, axis=-1, keepdims=True) + EPSILON)
    return cen * inv, inv


def norm_back(n, nrm, inv):
    m1 = jnp.mean(n, axis=-1, keepdims=True)
    m2 = jnp.mean(n * nrm, axis=-1, keepdims=True)
    return (n - m1 - nrm * m2) * inv


SCRATCH = dict(
    stg_t=((2, 4, 64, D), BF),
    stg_c=((2, 4, 64, D), BF),
    tok=((4, 256, D), BF),
    cot=((4, 256, D), BF),
    latc=((4, 1, 256), jnp.int32),
    lv=((4, 256, 128), F32),
    oh=((4, 256, 128), BF),
    modhl=((32, 6 * D), BF),
    pm=((256, 256), BF),
    ain=((4, 288, D), BF),
    c1t=((D, 1024), BF),
    tmpa=((4, 256, D), BF),
    qkv=((4, 256, 3 * HB), BF),
    att=((4, 256, D), BF),
    fint=((D, 1024), BF),
    bg=((4, 256, D), BF),
    mid=((2, 256, D), F32),
    ub=((4, 288, HB), BF),
    us=((4, 288, HB), BF),
    gb=((4, 288, HB), BF),
    gs=((4, 288, HB), BF),
    gp=((2, 256, D), F32),
    act=((4, 256, 2 * D), BF),
    upg=((4, 256, 2 * D), BF),
    upr=((4, 256, 2 * D), BF),
    actt=((HB, 1024), BF),
    wup=((D, 2 * D), BF),
    wdn=((2 * D, D), BF),
    wq=((D, 3 * HB), BF),
    wo=((D, D), BF),
    gwd=((4, HB, D), BF),
    gwo=((4, 96, D), BF),
    rd_a=((192, D), BF),
    rd_b=((192, D), BF),
    rd_x=((HB, D), BF),
    rd_y=((HB, D), BF),
    ru_a=((96, 2 * D), BF),
    ru_b=((96, 2 * D), BF),
    ru_x=((192, 2 * D), BF),
    ru_y=((192, 2 * D), BF),
    rq_a=((96, 3 * HB), BF),
    rq_b=((96, 3 * HB), BF),
    rq_x=((192, 3 * HB), BF),
    rq_y=((192, 3 * HB), BF),
    ro_a=((48, D), BF),
    ro_b=((48, D), BF),
    ro_x=((96, D), BF),
    ro_y=((96, D), BF),
    su=((96, 2 * D), BF),
    sq=((96, 3 * HB), BF),
    zd_a=((HB, D), BF),
    zd_b=((HB, D), BF),
    zu_a=((96, FF), BF),
    zu_b=((96, FF), BF),
    zq_a=((96, 3 * D), BF),
    zq_b=((96, 3 * D), BF),
    zo_a=((96, D), BF),
    zo_b=((96, D), BF),
    frcv=((2, 4, 64, D), BF),
    brcv=((2, 4, 64, D), BF),
    oland=((2, 4, 64, D), BF),
    gland=((2, 4, 64, D), BF),
    condc=((16, D), F32),
    clow=((4, 16, D), BF),
    mg1=((16, D), F32),
    mg2=((16, HB), F32),
    mgs1=((16, D), BF),
    mgr1=((16, D), BF),
    mgs2=((16, HB), BF),
    mgr2=((16, HB), BF),
    mga1=((16, 16, D), BF),
    mga2=((16, 16, HB), BF),
    sg1=((16, FF), F32),
    sg1s=((1, 16, FF), BF),
    sg1r=((5, 16, FF), BF),
    sg2=((16, D), F32),
    sg2s=((1, 16, D), BF),
    sg2r=((5, 16, D), BF),
    cgsum=((16, D), F32),
    crcv=((2, 8, D), F32),
    lat_own=((2, 1, 256), jnp.int32),
    cond_own=((8, D), F32),
    par=((16, FF), F32),
)
N_SEMS = 340


def whole_block(
    tok_h, cot_h, lat_in, cond_in, wada_h, wqkv_h, wout_h, wup_h, wdn_h,
    p_bada, p_conv1, p_bqv, p_bout, p_bup, p_conv2, p_bdn,
    o_out, o_gin, o_cond, o_wada, o_bada, o_sg1, o_sg2, o_wqkv, o_wout, o_wup, o_wdn,
    sems, *bufs,
):
    v = SimpleNamespace(**dict(zip(SCRATCH, bufs)))
    stg_t, stg_c, tok, cot, latc, lv, oh = v.stg_t, v.stg_c, v.tok, v.cot, v.latc, v.lv, v.oh
    modhl, pm, ain, c1t, tmpa, qkv, att = v.modhl, v.pm, v.ain, v.c1t, v.tmpa, v.qkv, v.att
    fint, bg, mid, ub, us, gb, gs = v.fint, v.bg, v.mid, v.ub, v.us, v.gb, v.gs
    gp, act, upg, actt, wup, wdn, wq, wo = v.gp, v.act, v.upg, v.actt, v.wup, v.wdn, v.wq, v.wo
    upr = v.upr
    gwd, gwo, condc, clow = v.gwd, v.gwo, v.condc, v.clow

    c = lax.axis_index("canvas")
    r = lax.axis_index("rows")
    k = c % 2
    x = (c // 2) % 2
    y = c // 4
    col = 2 * y + x
    r1 = r + 1 - 2 * (r % 2)
    r2 = (r + 2) % 4
    r3 = 3 - r
    sib = (y * 4 + x * 2 + 1 - k, r)
    px = (y * 4 + (1 - x) * 2 + k, r)
    py = ((1 - y) * 4 + x * 2 + k, r)
    owner = r // 2
    is_own = k == owner
    owner_c = y * 4 + x * 2 + owner

    count = [0]

    def sem(n=1):
        first = count[0]
        count[0] += n
        return first

    last = []

    def remote(src, dst, ss, rs, dev):
        return pltpu.make_async_remote_copy(
            src_ref=src, dst_ref=dst, send_sem=sems.at[ss], recv_sem=sems.at[rs],
            device_id=dev, device_id_type=pl.DeviceIdType.MESH,
        )

    def local(src, dst, s):
        return pltpu.make_async_copy(src, dst, sems.at[s])

    def swap(src, dst, dev):
        cp = remote(src, dst, sem(), sem(), dev)
        cp.start()
        last.append(cp.wait_send)
        return cp

    barrier = pltpu.get_barrier_semaphore()
    for dev in (sib, px, py, (c, r1), (c, r2), (c, r3), (sib[0], r1), (sib[0], r2), (sib[0], r3)):
        pl.semaphore_signal(barrier, inc=1, device_id=dev, device_id_type=pl.DeviceIdType.MESH)
    s_tok = sem()
    s_cot = sem()
    ld_tok = local(tok_h, act.at[pl.ds(0, 2), :, pl.ds(0, D)], s_tok)
    ld_tok.start()
    ld_cot = local(cot_h, act.at[pl.ds(0, 2), :, pl.ds(D, D)], s_cot)
    ld_cot.start()
    s_wa = sem(2)

    def load_ada(p):
        return local(wada_h.at[:, pl.ds(p * D, D)], wup.at[:, pl.ds((p % 2) * D, D)], s_wa + p % 2)

    load_ada(0).start()
    load_ada(1).start()
    s_w = sem(3)
    ld_wq = [
        local(wqkv_h.at[:, pl.ds(pl.multiple_of(part * D + HB * k, 128), HB)], wq.at[:, pl.ds(part * HB, HB)], s_w + part)
        for part in range(3)
    ]
    for cp in ld_wq:
        cp.start()
    ld_wo = local(wout_h, wo, sem())
    ld_wo.start()
    s_wd = sem(4)
    ld_wd = [
        local(wdn_h.at[pl.ds(pl.multiple_of(HB * (2 * b + k), 128), HB), :], wdn.at[pl.ds(HB * b, HB), :], s_wd + b)
        for b in range(4)
    ]
    for cp in ld_wd:
        cp.start()
    pi = iota((256, 256), 0)
    group, place = pi // 64, pi % 64
    nat = (2 * (place // 16) + group // 2) * 32 + 2 * (place % 16) + group % 2
    pm[...] = ones_where(iota((256, 256), 1) == nat)
    for buf in (ain, ub, us, gb, gs):
        wide = buf.shape[2]
        for g in range(4):
            buf[g, 0:16, :] = jnp.zeros((16, wide), BF)
            buf[g, 272:288, :] = jnp.zeros((16, wide), BF)
    lat_h, par = v.lat_own, v.par
    for i in range(2):
        lat_h[i] = lat_in[i : i + 1, :]
        v.cond_own[4 * i : 4 * i + 4, :] = cond_in[i]
    condc[pl.ds(pl.multiple_of(8 * k, 8), 8), :] = v.cond_own[...]
    par[0:9, :] = p_conv2[...].astype(F32)

    def row_of(ref):
        return ref[...].astype(F32).reshape(1, ref.shape[0])

    par[9:10, :] = row_of(p_bup)
    par[10:11, 0:D] = row_of(p_bdn)
    par[10:11, D : 2 * D] = row_of(p_bout)
    par[10:11, 2 * D : 4 * D] = row_of(p_bqv)
    taps1 = p_conv1[...].astype(F32)
    for t in range(9):
        par[11 + t // 4 : 12 + t // 4, (t % 4) * D : (t % 4) * D + D] = taps1[t : t + 1]
    ada = row_of(p_bada)
    par[14:15, :] = ada[:, 0 : 4 * D]
    par[15:16, 0 : 2 * D] = ada[:, 4 * D : 6 * D]
    pl.semaphore_wait(barrier, 9)

    cond_cp = swap(
        condc.at[pl.ds(pl.multiple_of(8 * k, 8), 8), :], condc.at[pl.ds(pl.multiple_of(8 * k, 8), 8), :], sib
    )
    mine64 = pl.ds(pl.multiple_of(r * 64, 64), 64)
    rt, rl, rc = sem(4), sem(4), sem(4)
    st, sl, sc = sem(2), sem(2), sem(2)

    def give(src, dst, ss, rs, i):
        q = 2 * k + i
        far = remote(src, dst, ss, rs, (c, q))
        near = local(src, dst, rs)

        @pl.when(q != r)
        def _():
            far.start()

        @pl.when(q == r)
        def _():
            near.start()

        def done():
            @pl.when(q != r)
            def _():
                far.wait_send()

        return done

    tok_sent, cot_sent = [], []
    ld_tok.wait()
    for i in range(2):
        stg_t[i] = dot(pm[...], act[i, :, 0:D]).astype(BF).reshape(4, 64, D)
        tok_sent.append(give(stg_t.at[i], tok.at[:, mine64, :], st + i, rt + r, i))
        last.append(give(lat_h.at[i], latc.at[r], sl + i, rl + r, i))

    ld_cot.wait()
    for i in range(2):
        stg_c[i] = dot(pm[...], act[i, :, D : 2 * D]).astype(BF).reshape(4, 64, D)

    cond_cp.wait_recv()
    cond = condc[...]
    sig = 1.0 / (1.0 + jnp.exp(-cond))
    mine_low = (cond * sig).astype(BF)
    clow[col] = mine_low
    low_x = swap(clow.at[col], clow.at[col], px)
    for p in range(6):
        load_ada(p).wait()
        mod = dot(mine_low, wup[:, (p % 2) * D : (p % 2) * D + D])
        mod = mod + par[14 + p // 4 : 15 + p // 4, (p % 4) * D : (p % 4) * D + D]
        high = mod.astype(BF)
        modhl[0:16, p * D : (p + 1) * D] = high
        modhl[16:32, p * D : (p + 1) * D] = (mod - high.astype(F32)).astype(BF)
        if p + 2 < 6:
            load_ada(p + 2).start()
    s_wu = sem(4)
    ld_wu = [
        local(wup_h.at[:, pl.ds(pl.multiple_of(HB * (2 * b + k), 128), HB)], wup.at[:, pl.ds(HB * b, HB)], s_wu + b)
        for b in range(4)
    ]
    for cp in ld_wu:
        cp.start()

    def piece(o, p):
        return dot(o[:, 0:32], modhl[:, p * D : (p + 1) * D])

    ft, fl, fc = sem(4), sem(4), sem(4)
    order = (r, r1, r2, r3)

    def arrive(buf, of, rs, fs, then=None):
        passed = []
        for d in range(4):
            s = order[d]
            place = of(s)
            cp = remote(buf.at[place], buf.at[place], fs + d, rs + s, sib)
            cp.wait_recv()

            @pl.when(is_own)
            def _():
                cp.start()

            def done(cp=cp):
                @pl.when(is_own)
                def _():
                    cp.wait_send()

            passed.append(done)
            if then is not None:
                then(s)
        return passed

    def slab(s):
        return (slice(None), pl.ds(pl.multiple_of(s * 64, 64), 64), slice(None))

    last.extend(arrive(latc, lambda s: s, rl, fl))
    def norm_one(s):
        rows = jnp.broadcast_to(latc[s].astype(F32), (128, 256)).astype(BF)
        ids = dot_t(pm[...], rows)
        lane = iota((256, 128), 1)
        want = (lane % 16 - 4 * r).astype(F32)
        o = ones_where((want == ids) & (lane < 32))
        at = pl.ds(pl.multiple_of(s * 64, 64), 64)
        lv[:, at, :] = ids.reshape(4, 64, 128)
        oh[:, at, :] = o.reshape(4, 64, 128)
        nrm, _inv = norm_parts(tok[:, at, :].reshape(256, D).astype(F32))
        h = (nrm * (1.0 + piece(o, 1)) + piece(o, 0)).astype(BF)
        padded = pl.ds(pl.multiple_of(s * 64 + 16, 16), 64)
        ain[:, padded, :] = h.reshape(4, 64, D)
        for g in range(4):
            sh = shifted(h[g * 64 : g * 64 + 64].astype(F32), g % 2).astype(BF)
            us[g, padded, :] = sh[:, 0:HB]
            gs[g, padded, :] = sh[:, HB:D]

    tok_passed = arrive(tok, slab, rt, ft, norm_one)
    for i in range(2):
        cot_sent.append(give(stg_c.at[i], cot.at[:, mine64, :], sc + i, rc + r, i))

    for hh in range(2):
        side = us if hh == 0 else gs

        def conv_one(lt, _, hh=hh, side=side):
            l0 = pl.multiple_of(lt * 128, 128)
            la = pl.multiple_of(hh * HB + lt * 128, 128)
            kr = [par[11 + t // 4 : 12 + t // 4, pl.ds((t % 4) * D + la, 128)] for t in range(9)]
            for g in range(4):
                for h in range(2):

                    def load(gsrc, ro, moved):
                        rows = pl.ds(16 + 16 * ro + 128 * h, 128)
                        return side[gsrc, rows, pl.ds(l0, 128)] if moved else ain[gsrc, rows, pl.ds(la, 128)]

                    low = conv_sum(load, kr, taps_of(g // 2, g % 2, False)).astype(BF)
                    tmpa[g, h * 128 : h * 128 + 128, pl.ds(la, 128)] = low
                    c1t[pl.ds(la, 128), g * 256 + h * 128 : g * 256 + h * 128 + 128] = low.astype(F32).T.astype(BF)
            return 0

        lax.fori_loop(0, 3, conv_one, 0)

    for cp in ld_wq:
        cp.wait()
    kcol = pl.multiple_of(HB * k, 128)
    b_q = par[10:11, pl.ds(2 * D + kcol, HB)]
    b_v = par[10:11, pl.ds(3 * D + kcol, HB)]

    def project(n, _):
        two = pl.ds(2 * n, 2)
        rows = tmpa[two].reshape(512, D)
        got = dot(rows, wq[:, 0:HB]) + b_q
        qkv[two, :, 0:HB] = (got.astype(BF).astype(F32) * 0.125).astype(BF).reshape(2, 256, HB)
        qkv[two, :, HB : 2 * HB] = dot(rows, wq[:, HB : 2 * HB]).astype(BF).reshape(2, 256, HB)
        got = dot(rows, wq[:, 2 * HB : 3 * HB]) + b_v
        qkv[two, :, 2 * HB : 3 * HB] = got.astype(BF).reshape(2, 256, HB)
        return 0

    lax.fori_loop(0, 2, project, 0)

    lane1 = iota((1, 128), 1)
    lmf = [jnp.where(lane1 < 64, 1.0, 0.0), jnp.where(lane1 < 64, 0.0, 1.0)]
    lmb = [m.astype(BF) for m in lmf]
    sa, ra = sem(4), sem(4)

    def masks_of(g):
        lane = iota((256, 128), 1)
        same = lane.astype(F32) == lv[g]
        oq = jnp.where(same & (lane < 4), 1.0, 0.0).astype(BF)
        mk = jnp.where(same | (lane >= 4), 0.0, BIG).astype(BF)
        return oq, mk

    def att_copy(g):
        place = att.at[g, :, pl.ds(kcol, HB)]
        return remote(place, place, sa + g, ra + g, sib)

    def attend(g, _):
        oq, mk = masks_of(g)
        oq2 = jnp.concatenate([oq, oq], axis=0)
        for hp in range(3):
            qp = qkv[g, :, hp * 128 : hp * 128 + 128]
            ka = jnp.concatenate([qkv[g, :, HB + hp * 128 : HB + hp * 128 + 128], mk], axis=1)
            vp = qkv[g, :, 2 * HB + hp * 128 : 2 * HB + hp * 128 + 128]
            qa = jnp.concatenate([qp * lmb[0], qp * lmb[1]], axis=0)
            s = dot_t(jnp.concatenate([qa, oq2], axis=1), ka)
            e = jnp.exp(s - jnp.max(s, axis=1, keepdims=True))
            o = dot(e.astype(BF), vp) * (1.0 / jnp.sum(e, axis=1, keepdims=True))
            mixed = o[0:256] * lmf[0] + o[256:512] * lmf[1]
            att[g, :, pl.ds(pl.multiple_of(kcol + hp * 128, 128), 128)] = mixed.astype(BF)
        att_copy(g).start()
        return 0

    lax.fori_loop(0, 4, attend, 0)
    low_x.wait_recv()
    low_y = swap(clow.at[pl.ds(2 * y, 2)], clow.at[pl.ds(2 * y, 2)], py)

    ld_wo.wait()
    kother = pl.multiple_of(HB * (1 - k), 128)

    def norm_two(g, _):
        for h in range(2):
            rows = slice(h * 128, h * 128 + 128)
            a = att[g, rows, :]
            ao = dot(a, wo[...]) + par[10:11, D : 2 * D]
            o = oh[g, rows, :]
            m = tok[g, rows, :].astype(F32) + piece(o, 2) * ao
            nrm, _inv = norm_parts(m)
            f = (nrm * (1.0 + piece(o, 4)) + piece(o, 3)).astype(BF)
            tmpa[g, rows, :] = f
            at = pl.ds(pl.multiple_of(g * 256 + h * 128, 128), 128)
            fint[:, at] = f.astype(F32).T.astype(BF)
        return 0

    for g in range(4):
        att_copy(g).wait()
    lax.fori_loop(0, 4, norm_two, 0)
    last.extend(arrive(cot, slab, rc, fc))

    def gate_cot(g, _):
        bg[g] = (piece(oh[g], 5) * cot[g].astype(F32)).astype(BF)
        return 0

    lax.fori_loop(0, 4, gate_cot, 0)

    class Scatter:
        def __init__(self, src, a, b, rx, ry):
            self.src, self.a, self.b, self.rx, self.ry = src, a, b, rx, ry
            n = a.shape[0]
            self.n = n
            ss = sem(8)
            self.ca = remote(src(0, 0, n), a, ss, ss + 1, px)
            self.cb = remote(src(0, n, n), b, ss + 2, ss + 3, py)
            self.cx = remote(src(1, 0, 2 * n), rx, ss + 4, ss + 5, px)
            self.cy = remote(src(2, 0, 2 * n), ry, ss + 6, ss + 7, py)

        def s0(self):
            self.ca.start()
            self.cb.start()

        def s1(self):
            self.cb.wait_recv()
            part = self.src(1, self.n, self.n)
            part[...] = (part[...].astype(F32) + self.b[...].astype(F32)).astype(BF)
            self.cx.start()

        def s2(self):
            self.ca.wait_recv()
            part = self.src(2, 0, self.n)
            part[...] = (part[...].astype(F32) + self.a[...].astype(F32)).astype(BF)
            self.cy.start()

        def s3(self):
            self.cx.wait_recv()
            self.cy.wait_recv()
            part = self.src(3, 0, 2 * self.n)
            return part[...].astype(F32) + self.rx[...].astype(F32) + self.ry[...].astype(F32)

        def sent(self):
            for cp in (self.ca, self.cb, self.cx, self.cy):
                cp.wait_send()

    inner = (r % 3) != 0

    class Line:
        def __init__(self, pieces):
            self.parts = []
            for o, a, b in pieces:
                ss = sem(6)
                up = remote(o, a, ss, ss + 1, (c, r1))
                mid = remote(o, b, ss + 2, ss + 3, (c, r3))
                down = remote(o, a, ss + 4, ss + 5, (c, r1))
                self.parts.append((o, a, b, up, mid, down))

        def s0(self, which=None):
            @pl.when(jnp.logical_not(inner))
            def _():
                for i, part in enumerate(self.parts):
                    if which is None or which == i:
                        part[3].start()

        def s1(self):
            @pl.when(inner)
            def _():
                for o, a, _b, up, mid, _down in self.parts:
                    up.wait_recv()
                    o[...] = (o[...].astype(F32) + a[...].astype(F32)).astype(BF)
                    mid.start()

        def s2(self):
            @pl.when(inner)
            def _():
                for o, _a, b, _up, mid, down in self.parts:
                    mid.wait()
                    o[...] = (o[...].astype(F32) + b[...].astype(F32)).astype(BF)
                    down.start()

        def s3(self):
            @pl.when(inner)
            def _():
                for part in self.parts:
                    part[5].wait_send()

            @pl.when(jnp.logical_not(inner))
            def _():
                for o, a, _b, up, _mid, down in self.parts:
                    up.wait_send()
                    down.wait_recv()
                    o[...] = a[...]

    class Gather:
        def __init__(self, own, got, everyone):
            self.own, self.got, self.everyone = own, got, everyone
            self.zr, self.zs = sem(4), sem(3)
            self.xy = sem(4)

        def s0(self):
            self.everyone[slot] = (self.own[...].astype(F32) + self.got[...].astype(F32)).astype(BF)
            place = self.everyone.at[slot]
            for d, s in enumerate((r1, r2, r3)):
                cp = remote(place, place, self.zs + d, self.zr + r, (c, s))
                cp.start()
                last.append(cp.wait_send)

        def s1(self):
            for s in (r1, r2, r3):
                place = self.everyone.at[4 * col + s]
                local(place, place, self.zr + s).wait()
            place = self.everyone.at[pl.ds(4 * col, 4)]
            self.cx = remote(place, place, self.xy, self.xy + 1, px)
            self.cx.start()
            last.append(self.cx.wait_send)

        def s2(self):
            self.cx.wait_recv()
            place = self.everyone.at[pl.ds(8 * y, 8)]
            self.cy = remote(place, place, self.xy + 2, self.xy + 3, py)
            self.cy.start()
            last.append(self.cy.wait_send)

        def s3(self):
            self.cy.wait_recv()

    def by_rows(out, za, zb, cuts):
        n = out.shape[0] // cuts
        rows = [pl.ds(i * n, n) for i in range(cuts)]
        return Line([(out.at[at], za.at[at], zb.at[at]) for at in rows])

    class Columns:
        def __init__(self, src, a, b, rx, ry, su, out, za, zb):
            self.src, self.a, self.b, self.rx, self.ry, self.su, self.out = src, a, b, rx, ry, su, out
            count = su.shape[1] // HB
            self.lanes = [pl.ds(t * HB, HB) for t in range(count)]
            self.cps = []
            for ln in self.lanes:
                ss = sem(10)
                self.cps.append(
                    (
                        remote(src(0, 0, 96, ln), a.at[:, ln], ss, ss + 1, px),
                        remote(src(0, 96, 96, ln), b.at[:, ln], ss + 2, ss + 3, py),
                        remote(src(1, 0, 192, ln), rx.at[:, ln], ss + 4, ss + 5, px),
                        remote(src(2, 0, 192, ln), ry.at[:, ln], ss + 6, ss + 7, py),
                        remote(
                            src(3, pl.multiple_of(96 * (1 - k), 32), 96, ln), su.at[:, ln], ss + 8, ss + 9, sib
                        ),
                    )
                )
            both = [pl.ds(t * D, D) for t in range(count)]
            self.line = Line([(out.at[:, at], za.at[:, at], zb.at[:, at]) for at in both])

        def s0(self, t):
            self.cps[t][0].start()
            self.cps[t][1].start()

        def s1(self, t):
            ca, cb, cx, cy, _ = self.cps[t]
            ln = self.lanes[t]
            cb.wait_recv()
            part = self.src(1, 96, 96, ln)
            part[...] = (part[...].astype(F32) + self.b[:, ln].astype(F32)).astype(BF)
            cx.start()
            ca.wait_recv()
            part = self.src(2, 0, 96, ln)
            part[...] = (part[...].astype(F32) + self.a[:, ln].astype(F32)).astype(BF)
            cy.start()

        def s3(self, t):
            ln = self.lanes[t]
            self.cps[t][2].wait_recv()
            self.cps[t][3].wait_recv()
            part = self.src(3, 0, 192, ln)
            part[...] = (part[...].astype(F32) + self.rx[:, ln].astype(F32) + self.ry[:, ln].astype(F32)).astype(BF)
            self.cps[t][4].start()
            mine = self.src(3, pl.multiple_of(96 * k, 32), 96, ln)
            self.out[:, pl.ds(pl.multiple_of(t * D + HB * k, 128), HB)] = mine[...]

        def s4(self, t):
            self.cps[t][4].wait()
            self.out[:, pl.ds(pl.multiple_of(t * D + HB * (1 - k), 128), HB)] = self.su[:, self.lanes[t]]
            self.line.s0(t)

        def sent(self):
            for cps in self.cps:
                for cp in cps[0:4]:
                    cp.wait_send()

    class Everyone:
        def __init__(self, total, send, recv):
            self.total, self.send, self.recv = total, send, recv
            ss = sem(6)
            devs = (sib, px, py)
            self.cps = [remote(send.at[0], recv.at[i], ss + 2 * i, ss + 2 * i + 1, devs[i]) for i in range(3)]

        def go(self, i):
            self.send[0] = self.total[...].astype(BF)
            self.cps[i].start()

        def end(self, i):
            self.cps[i].wait()
            self.total[...] = self.send[0].astype(F32) + self.recv[i].astype(F32)

        def plane(self):
            self.end(2)
            self.send[0] = self.total[...].astype(BF)

    mga1, mga2 = v.mga1, v.mga2
    mgs1, mgr1, mgs2, mgr2 = v.mgs1, v.mgr1, v.mgs2, v.mgr2
    slot = 4 * col + r
    gat1 = Gather(mgs1, mgr1, mga1)
    gat2 = Gather(mgs2, mgr2, mga2)
    sum_d = Scatter(lambda p, r0, n: gwd.at[p, pl.ds(r0, n)], v.rd_a, v.rd_b, v.rd_x, v.rd_y)
    sum_u = Columns(
        lambda p, r0, n, ln: upr.at[p, pl.ds(r0, n), ln],
        v.ru_a, v.ru_b, v.ru_x, v.ru_y, v.su, o_wup, v.zu_a, v.zu_b,
    )
    sum_q = Columns(
        lambda p, r0, n, ln: wup.at[pl.ds(192 * p + r0, n), ln],
        v.rq_a, v.rq_b, v.rq_x, v.rq_y, v.sq, o_wqkv, v.zq_a, v.zq_b,
    )
    sum_o = Scatter(lambda p, r0, n: gwo.at[p, pl.ds(r0, n)], v.ro_a, v.ro_b, v.ro_x, v.ro_y)
    line_d = by_rows(o_wdn, v.zd_a, v.zd_b, 4)
    line_u = sum_u.line
    line_o = by_rows(o_wout, v.zo_a, v.zo_b, 1)
    line_q = sum_q.line
    sg1, sg2 = v.sg1, v.sg2
    all1 = Everyone(sg1, v.sg1s, v.sg1r)
    all2 = Everyone(sg2, v.sg2s, v.sg2r)
    line_a = Line([(v.sg1s.at[0], v.sg1r.at[3], v.sg1r.at[4])])
    line_b = Line([(v.sg2s.at[0], v.sg2r.at[3], v.sg2r.at[4])])
    sg1[...] = jnp.zeros((16, FF), F32)
    sg2[...] = jnp.zeros((16, D), F32)

    def block_at(pos):
        fx = 1 - pos // 2
        fy = 1 - pos % 2
        bx = x + fx - 2 * x * fx
        by = y + fy - 2 * y * fy
        return 2 * by + bx

    for cp in ld_wd + ld_wu:
        cp.wait()

    def hidden(pos, _):
        b = block_at(pos)
        lo = pl.multiple_of(b * HB, 128)
        wide = pl.multiple_of(HB * (2 * b + k), 128)

        def up(pr, _):
            both = dot(tmpa[pl.ds(2 * pr, 2)].reshape(512, D), wup[:, pl.ds(lo, HB)])
            for pc in range(2):
                g = 2 * pr + pc
                u = (both[pc * 256 : pc * 256 + 256] + par[9:10, pl.ds(wide, HB)]).astype(BF)
                ub[g, 16:272, :] = u
                upr[g, :, pl.ds(lo, HB)] = u
                us[g, 16:272, :] = shifted(u.astype(F32), pc).astype(BF)
            return 0

        lax.fori_loop(0, 2, up, 0)

        def conv_gelu(lt, _):
            l0 = pl.multiple_of(lt * 128, 128)
            ln = pl.ds(l0, 128)
            kr = [par[t : t + 1, pl.ds(wide + l0, 128)] for t in range(9)]
            for g in range(4):
                for h in range(2):

                    def load(gsrc, ro, moved):
                        return (us if moved else ub)[gsrc, pl.ds(16 + 16 * ro + 128 * h, 128), ln]

                    acc = conv_sum(load, kr, taps_of(g // 2, g % 2, False))
                    sq = acc * acc
                    th = jnp.tanh(0.7978845608028654 * acc * (1.0 + 0.044715 * sq))
                    half = 0.5 + 0.5 * th
                    low = (acc * half).astype(BF)
                    slope = half + half * (1.0 - th) * acc * (0.7978845608028654 + 0.10703222440890037 * sq)
                    rows = slice(h * 128, h * 128 + 128)
                    act[g, rows, pl.ds(lo + l0, 128)] = low
                    upg[g, rows, pl.ds(lo + l0, 128)] = slope.astype(BF)
                    actt[ln, g * 256 + h * 128 : g * 256 + h * 128 + 128] = low.astype(F32).T.astype(BF)
            return 0

        lax.fori_loop(0, 3, conv_gelu, 0)

        def grad_down(n, _):
            ln = pl.ds(pl.multiple_of(n * 256, 128), 256)
            gwd[pos, :, ln] = dot(actt[...], bg[:, :, ln].reshape(1024, 256)).astype(BF)
            return 0

        lax.fori_loop(0, 3, grad_down, 0)
        pl.when(pos == 0)(sum_d.s0)

        @pl.when(pos == 2)
        def _():
            sum_d.s1()
            sum_d.s2()

        return 0

    lax.fori_loop(0, 4, hidden, 0)

    for done in tok_sent + cot_sent:
        done()
    other2 = pl.ds(2 * (1 - k), 2)
    mine2 = pl.ds(2 * k, 2)

    def half_f(which, n):
        return dot_t(upg[which].reshape(512, 2 * D), wup[n * HB : n * HB + HB, :])

    def half_b(which, n):
        return dot(act[which].reshape(512, 2 * D), wdn[:, n * HB : n * HB + HB])

    for n in range(2):
        cols = slice(n * HB, n * HB + HB)
        stg_c[:, :, :, cols] = half_b(other2, n).astype(BF).reshape(2, 4, 64, HB)
    b_cp = remote(stg_c, v.brcv, sem(), sem(), sib)
    b_cp.start()
    for n in range(2):
        cols = slice(n * HB, n * HB + HB)
        mid[:, :, cols] = half_b(mine2, n).reshape(2, 256, HB)

    def down_total():
        o_wdn[...] = sum_d.s3().astype(BF)
        line_d.s0()

    mg1, mg2 = v.mg1, v.mg2
    mg1[...] = jnp.zeros((16, D), F32)
    mg2[...] = jnp.zeros((16, HB), F32)
    o_rows = jnp.zeros((1, D), F32)

    def place_rows(ids, p):
        lane = iota((128, 128), 1)
        return ones_where((lane - 4 * p).astype(F32) == ids)

    def hand_back(src, land, rs, slabs):
        for s in slabs:
            ss = sem()
            dst = land.at[r % 2, pl.ds(2 * k, 2)]
            at = rs + (r % 2) * 2 + k
            far = remote(src.at[:, s], dst, ss, at, (owner_c, s))
            near = local(src.at[:, s], dst, at)
            here = is_own & (r == s)

            @pl.when(jnp.logical_not(here))
            def _(far=far):
                far.start()

            @pl.when(here)
            def _(near=near):
                near.start()

            def done(far=far, here=here):
                @pl.when(jnp.logical_not(here))
                def _():
                    far.wait_send()

            last.append(done)

    def landed(land, rs, out, first):
        for i in range(2):
            for kk in range(2):
                place = land.at[i, pl.ds(2 * kk, 2)]
                local(place, place, rs + 2 * i + kk).wait()
        for i in range(2):
            tok[first + i] = dot_l(pm[...], land[i].reshape(256, D)).astype(BF)
        cp = local(tok.at[pl.ds(first, 2)], out, sem())
        cp.start()
        last.append(cp.wait)

    ro_out, ro_gin = sem(4), sem(4)

    b_cp.wait()

    def out_half(n, bd):
        jj = n // 2
        g = 2 * k + jj
        rows = pl.ds(pl.multiple_of((n % 2) * 128, 128), 128)
        h64 = pl.ds((n % 2) * 2, 2)
        o = oh[g, rows, :]
        ao = dot(att[g, rows, :], wo[...]) + par[10:11, D : 2 * D]
        m = tok[g, rows, :].astype(F32) + piece(o, 2) * ao
        gp[jj, rows, :] = m
        branch = mid[jj, rows, :] + v.brcv[jj, h64].reshape(128, D).astype(F32) + par[10:11, 0:D]
        v.brcv[jj, h64] = ao.astype(BF).reshape(2, 64, D)
        stg_c[jj, h64] = (m + piece(o, 5) * branch).astype(BF).reshape(2, 64, D)
        low = (cot[g, rows, :].astype(F32) * branch).astype(BF)
        mg1[...] += dot_l(place_rows(lv[g, rows, :], 3), low)[0:16]
        return bd + jnp.sum(bg[g, rows, :].astype(F32), axis=0, keepdims=True)

    sg1[10:11, 0:D] = lax.fori_loop(0, 4, out_half, o_rows)
    hand_back(stg_c, v.oland, ro_out, range(4))
    def pos_of(b):
        bx, by = b % 2, b // 2
        fx = (bx - x) * (bx - x)
        fy = (by - y) * (by - y)
        return 2 * (1 - fx) + 1 - fy

    def hidden_back(b, _):
        lo = pl.multiple_of(b * HB, 128)
        wide = pl.multiple_of(HB * (2 * b + k), 128)
        pl.when(b == 2)(down_total)

        def down_grad(pr, _):
            both = dot_t(bg[pl.ds(2 * pr, 2)].reshape(512, D), wdn[pl.ds(lo, HB), :])
            for pc in range(2):
                g = 2 * pr + pc
                t = both[pc * 256 : pc * 256 + 256] * upg[g, :, pl.ds(lo, HB)].astype(F32)
                t = t.astype(BF)
                gb[g, 16:272, :] = t
                gs[g, 16:272, :] = shifted(t.astype(F32), pc).astype(BF)
            return 0

        lax.fori_loop(0, 2, down_grad, 0)

        def conv_back(lt, _):
            l0 = pl.multiple_of(lt * 128, 128)
            ln = pl.ds(l0, 128)
            kr = [par[t : t + 1, pl.ds(wide + l0, 128)] for t in range(9)]
            gk = [jnp.zeros((8, 128), F32) for _ in range(10)]
            for g in range(4):
                for h in range(2):
                    here = upr[g, h * 128 : h * 128 + 128, pl.ds(lo + l0, 128)].astype(F32)

                    def load(gsrc, ro, moved):
                        return (gs if moved else gb)[gsrc, pl.ds(16 + 16 * ro + 128 * h, 128), ln]

                    acc = conv_both(load, here, kr, gk, taps_of(g // 2, g % 2, True))
                    low = acc.astype(BF)
                    upg[g, h * 128 : h * 128 + 128, pl.ds(lo + l0, 128)] = low
                    gk[9] = gk[9] + fold_rows(low.astype(F32))
            for t in range(10):
                sg1[t : t + 1, pl.ds(wide + l0, 128)] = jnp.sum(gk[t], axis=0, keepdims=True)
            return 0

        lax.fori_loop(0, 3, conv_back, 0)
        got = dot(fint[...], upg[:, :, pl.ds(lo, HB)].reshape(1024, HB)).astype(BF)
        for rb in range(4):
            upr[pos_of(rb), 0:192, pl.ds(lo, HB)] = got[rb * 192 : rb * 192 + 192]
        for t in range(4):

            @pl.when(b == t)
            def _(t=t):
                sum_u.s0(t)
                if t >= 1:
                    sum_u.s1(t - 1)
                if t >= 3:
                    sum_u.s3(t - 3)

        return 0

    lax.fori_loop(0, 4, hidden_back, 0)

    for n in range(2):
        cols = slice(n * HB, n * HB + HB)
        stg_t[:, :, :, cols] = half_f(other2, n).astype(BF).reshape(2, 4, 64, HB)
    f_cp = remote(stg_t, v.frcv, sem(), sem(), sib)
    f_cp.start()
    sum_u.s3(1)
    sum_u.s4(0)
    for n in range(2):
        cols = slice(n * HB, n * HB + HB)
        mid[:, :, cols] = half_f(mine2, n).reshape(2, 256, HB)

    sum_u.s1(3)
    sum_u.s4(1)
    f_cp.wait()

    def two_back(n, bo):
        pl.when(n == 3)(line_d.s1)
        jj = n // 2
        g = 2 * k + jj
        rows = pl.ds(pl.multiple_of((n % 2) * 128, 128), 128)
        h64 = pl.ds((n % 2) * 2, 2)
        o = oh[g, rows, :]
        gate1 = piece(o, 2)
        nrm, inv = norm_parts(gp[jj, rows, :])
        fg = mid[jj, rows, :] + v.frcv[jj, h64].reshape(128, D).astype(F32)
        mg = cot[g, rows, :].astype(F32) + norm_back(fg * (1.0 + piece(o, 4)), nrm, inv)
        mid[jj, rows, :] = mg
        ag = (gate1 * mg).astype(BF)
        tmpa[g, rows, :] = ag
        ids = lv[g, rows, :]
        ao = v.brcv[jj, h64].reshape(128, D).astype(F32)
        total = dot_l(place_rows(ids, 0), (mg * ao).astype(BF))
        total = total + dot_l(place_rows(ids, 1), fg.astype(BF))
        total = total + dot_l(place_rows(ids, 2), (fg * nrm).astype(BF))
        mg1[...] += total[0:16]
        return bo + jnp.sum(ag.astype(F32), axis=0, keepdims=True)

    sg1[10:11, D : 2 * D] = lax.fori_loop(0, 4, two_back, o_rows)
    ag_place = tmpa.at[pl.ds(2 * k, 2)]
    ag_cp = swap(ag_place, ag_place, sib)

    sum_u.s3(2)
    sum_u.s3(3)
    sum_u.s4(2)
    mgs1[...] = mg1[...].astype(BF)
    mg_cp = swap(mgs1, mgr1, sib)
    all1.go(0)

    ag_cp.wait_recv()
    mg_cp.wait_recv()
    sum_u.s4(3)
    gat1.s0()
    dqkv = act
    kr_rows = pl.ds(kcol, HB)

    def heads_back(g, _):
        pl.when(g == 3)(line_d.s2)
        oq, mk = masks_of(g)
        mk2 = jnp.concatenate([mk, mk], axis=0)
        for h in range(2):
            at = pl.ds(pl.multiple_of(g * 256 + h * 128, 128), 128)
            fint[:, at] = att[g, h * 128 : h * 128 + 128, :].astype(F32).T.astype(BF)
        act[g, :, 3 * HB : 4 * HB] = dot_t(tmpa[g], wo[kr_rows, :]).astype(BF)
        for hp in range(3):
            qp = qkv[g, :, hp * 128 : hp * 128 + 128]
            kp = qkv[g, :, HB + hp * 128 : HB + hp * 128 + 128]
            vp = qkv[g, :, 2 * HB + hp * 128 : 2 * HB + hp * 128 + 128]
            dop = act[g, :, 3 * HB + hp * 128 : 3 * HB + hp * 128 + 128]
            k2 = jnp.concatenate([kp * lmb[0], kp * lmb[1]], axis=0)
            v2 = jnp.concatenate([vp * lmb[0], vp * lmb[1]], axis=0)
            s = dot_t(jnp.concatenate([k2, mk2], axis=1), jnp.concatenate([qp, oq], axis=1))
            dp = dot_t(v2, dop)
            probs, dss = [], []
            for h in range(2):
                sh = s[h * 256 : h * 256 + 256]
                dph = dp[h * 256 : h * 256 + 256]
                e = jnp.exp(sh - jnp.max(sh, axis=0, keepdims=True))
                prob = e * (1.0 / jnp.sum(e, axis=0, keepdims=True))
                delta = jnp.sum(prob * dph, axis=0, keepdims=True)
                probs.append(prob.astype(BF))
                dss.append((prob * (dph - delta)).astype(BF))
            ds2 = jnp.concatenate(dss, axis=0)
            dv2 = dot(jnp.concatenate(probs, axis=0), dop)
            dk2 = dot(ds2, qp)
            dq = dot_l(ds2, k2) * 0.125
            dv = dv2[0:256] * lmf[0] + dv2[256:512] * lmf[1]
            dk = dk2[0:256] * lmf[0] + dk2[256:512] * lmf[1]
            dqkv[g, :, hp * 128 : hp * 128 + 128] = dq.astype(BF)
            dqkv[g, :, HB + hp * 128 : HB + hp * 128 + 128] = dk.astype(BF)
            dqkv[g, :, 2 * HB + hp * 128 : 2 * HB + hp * 128 + 128] = dv.astype(BF)
        return 0

    lax.fori_loop(0, 4, heads_back, 0)
    all1.end(0)
    all1.go(1)
    line_u.s1()

    def proj_back(g, _):
        upg[g, :, 0:D] = dot_t(dqkv[g, :, 0 : 3 * HB], wq[...]).astype(BF)
        return 0

    lax.fori_loop(0, 4, proj_back, 0)
    cg_cp = swap(upg.at[:, :, pl.ds(0, D)], bg, sib)

    def grad_qkv(nt, _):
        ln = pl.ds(pl.multiple_of(nt * HB, 128), HB)
        got = dot(c1t[...], dqkv[:, :, ln].reshape(1024, HB)).astype(BF)
        for b in range(4):
            wup[pl.ds(pl.multiple_of(192 * pos_of(b), 64), 192), ln] = got[b * 192 : b * 192 + 192]
        for t in range(3):

            @pl.when(nt == t)
            def _(t=t):
                sum_q.s0(t)

        return 0

    lax.fori_loop(0, 3, grad_qkv, 0)
    all1.end(1)
    all1.go(2)
    gat1.s1()
    sg2[9:10, pl.ds(kcol, HB)] = jnp.sum(
        jnp.sum(dqkv[:, :, 0:HB].astype(F32), axis=0), axis=0, keepdims=True
    )
    sg2[10:11, pl.ds(kcol, HB)] = jnp.sum(
        jnp.sum(dqkv[:, :, 2 * HB : 3 * HB].astype(F32), axis=0), axis=0, keepdims=True
    )
    def grad_out(pos, _):
        rows = pl.ds(pl.multiple_of(96 * (2 * block_at(pos) + k), 32), 96)
        gwo[pos] = dot(fint[rows, :], tmpa[...].reshape(1024, D)).astype(BF)
        pl.when(pos == 0)(sum_o.s0)
        return 0

    lax.fori_loop(0, 4, grad_out, 0)
    for t in range(3):
        sum_q.s1(t)
    all1.plane()
    line_a.s0()
    cg_cp.wait_recv()

    def cg_sum(pr, _):
        for pc in range(2):
            g = 2 * pr + pc
            t = (upg[g, :, 0:D].astype(F32) + bg[g].astype(F32)).astype(BF)
            sh = shifted(t.astype(F32), pc).astype(BF)
            ub[g, 16:272, :] = t[:, 0:HB]
            gb[g, 16:272, :] = t[:, HB:D]
            us[g, 16:272, :] = sh[:, 0:HB]
            gs[g, 16:272, :] = sh[:, HB:D]
        return 0

    lax.fori_loop(0, 2, cg_sum, 0)
    sum_o.s1()
    sum_o.s2()
    gat1.s2()
    for hh in range(2):
        base, side = (ub, us) if hh == 0 else (gb, gs)

        def conv_one_back(lt, _, hh=hh, base=base, side=side):
            l0 = pl.multiple_of(lt * 128, 128)
            la = pl.multiple_of(hh * HB + lt * 128, 128)
            kr = [par[11 + t // 4 : 12 + t // 4, pl.ds((t % 4) * D + la, 128)] for t in range(9)]
            gk = [jnp.zeros((8, 128), F32) for _ in range(9)]
            for pc in range(2):
                for h in range(2):
                    here = ain[2 * k + pc, 16 + 128 * h : 144 + 128 * h, pl.ds(la, 128)].astype(F32)

                    def load(gsrc, ro, moved):
                        at = pl.ds(pl.multiple_of(16 + 16 * ro + 128 * h, 16), 128)
                        return (side if moved else base)[gsrc, at, pl.ds(l0, 128)]

                    acc = conv_both(load, here, kr, gk, taps_of(k, pc, True))
                    gp[pc, h * 128 : h * 128 + 128, pl.ds(la, 128)] = acc
            for t in range(9):
                sg2[t : t + 1, pl.ds(la, 128)] = jnp.sum(gk[t], axis=0, keepdims=True)
            return 0

        lax.fori_loop(0, 3, conv_one_back, 0)
    all2.go(0)
    sum_q.s3(0)
    sum_q.s3(1)
    line_u.s2()
    sum_q.s4(0)

    def one_back(n, _):
        jj = n % 2
        g = 2 * k + jj
        rows = pl.ds(pl.multiple_of((n // 2) * 128, 128), 128)
        h64 = pl.ds((n // 2) * 2, 2)
        nrm, inv = norm_parts(tok[g, rows, :].astype(F32))
        ig = gp[jj, rows, :]
        gi = mid[jj, rows, :] + norm_back(ig * (1.0 + piece(oh[g, rows, :], 1)), nrm, inv)
        stg_t[jj, h64] = gi.astype(BF).reshape(2, 64, D)
        ids = lv[g, rows, :]
        low = ig.astype(BF)
        scl = (ig * nrm).astype(BF)
        total = dot_l(place_rows(ids, 0), low[:, 0:HB]) + dot_l(place_rows(ids, 1), low[:, HB:D])
        total = total + dot_l(place_rows(ids, 2), scl[:, 0:HB]) + dot_l(place_rows(ids, 3), scl[:, HB:D])
        mg2[...] += total[0:16]
        return 0

    lax.fori_loop(0, 2, one_back, 0)
    hand_back(stg_t, v.gland, ro_gin, range(2))
    sum_q.s4(1)
    lax.fori_loop(2, 4, one_back, 0)
    mgs2[...] = mg2[...].astype(BF)
    mg2_cp = swap(mgs2, mgr2, sib)

    sum_q.s3(2)
    mg2_cp.wait_recv()
    gat2.s0()
    hand_back(stg_t, v.gland, ro_gin, range(2, 4))
    sum_q.s4(2)
    o_wout[...] = sum_o.s3().astype(BF)
    line_o.s0()
    all2.end(0)
    all2.go(1)

    def load_again(p):
        return local(wada_h.at[:, pl.ds(p * D, D)], wdn.at[pl.ds((p % 2) * D, D), :], s_wa + p % 2)

    load_again(2).start()
    load_again(3).start()

    def pick(p):
        ri, ci = iota((16, 16), 0), iota((16, 16), 1)
        return ones_where((ri // 4 == r) & (ci == 4 * p + ri % 4))

    my1 = mga1[slot]
    my2 = mga2[slot]
    cg = jnp.zeros((16, D), F32)
    for p in range(2, 6):
        load_again(p).wait()
        lhs = dot(pick(p - 2), my1).astype(BF)
        cg = cg + dot_t(lhs, wdn[(p % 2) * D : (p % 2) * D + D, :])
        load_again((p + 2) % 6).start()
    for p in range(2):
        load_again(p).wait()
        for h in range(2):
            lhs = dot(pick(2 * p + h), my2).astype(BF)
            cg = cg + dot_t(lhs, wdn[p * D : p * D + D, h * HB : h * HB + HB])
    cond = condc[...]
    sig = 1.0 / (1.0 + jnp.exp(-cond))
    cgsum = v.cgsum
    cgsum[...] = cg * (sig * (1.0 + cond * (1.0 - sig)))
    crcv = v.crcv
    cr, cs = sem(2), sem(4)
    for s in range(4):
        src = cgsum.at[pl.ds(pl.multiple_of(8 * owner, 8), 8), :]
        dst = crcv.at[r % 2]
        far = remote(src, dst, cs + s, cr + r % 2, (c, s))
        near = local(src, dst, cr + r % 2)

        @pl.when(is_own & (r != s))
        def _(far=far):
            far.start()

        @pl.when(is_own & (r == s))
        def _(near=near):
            near.start()

        def done(far=far, s=s):
            @pl.when(is_own & (r != s))
            def _():
                far.wait_send()

        last.append(done)

    all2.end(1)
    all2.go(2)
    line_a.s1()
    line_q.s1()
    line_o.s1()
    all2.plane()
    line_b.s0()
    gat2.s1()
    line_a.s2()
    line_q.s2()
    line_o.s2()
    gat2.s2()
    line_b.s1()
    for done in tok_passed:
        done()
    landed(v.oland, ro_out, o_out, 0)

    low_y.wait_recv()
    ri, ci = iota((96, D), 0), iota((96, D), 1)
    cond_t = dot_t(ones_where(ci == 96 * c + ri), clow[...].reshape(64, D)).astype(BF)
    ej, en = iota((64, 256), 0), iota((64, 256), 1)
    bn = iota((8, 256), 1)

    def spread(p):
        return dot(cond_t, ones_where((en // 16 == ej // 4) & (en % 16 == 4 * p + ej % 4))).astype(BF)

    gat1.s3()
    o_bada[...] = jnp.zeros((8, 6 * D), F32)
    every1 = mga1[...].reshape(256, D)

    def ada_out(p):
        cp = local(wdn.at[pl.ds(96 * p, 96), :], o_wada.at[:, pl.ds(p * D, D)], sem())
        cp.start()
        last.append(cp.wait)

    for p in range(4):
        wdn[(p + 2) * 96 : (p + 3) * 96, :] = dot(spread(p), every1).astype(BF)
        ada_out(p + 2)
        o_bada[0:1, (p + 2) * D : (p + 3) * D] = dot(ones_where((bn % 16) // 4 == p), every1)[0:1]
    gat2.s3()
    every2 = mga2[...].reshape(256, HB)
    for p in range(4):
        half = (p % 2) * HB
        wdn[p // 2 * 96 : p // 2 * 96 + 96, half : half + HB] = dot(spread(p), every2).astype(BF)
        o_bada[0:1, p * HB : (p + 1) * HB] = dot(ones_where((bn % 16) // 4 == p), every2)[0:1]
    ada_out(0)
    ada_out(1)
    line_b.s2()
    line_d.s3()
    line_u.s3()
    landed(v.gland, ro_gin, o_gin, 2)
    for i in range(2):
        local(crcv.at[i], crcv.at[i], cr + i).wait()
    both = crcv[0] + crcv[1]
    for i in range(2):
        o_cond[i] = both[4 * i : 4 * i + 4]
    line_a.s3()
    o_sg1[...] = v.sg1s[0].astype(F32)
    line_b.s3()
    o_sg2[...] = v.sg2s[0].astype(F32)
    line_o.s3()
    line_q.s3()
    for done in last:
        done()
    for s in (sum_d, sum_u, sum_o, sum_q):
        s.sent()
    assert count[0] <= N_SEMS, count[0]


def finish(
    out, gin, gcond, wada, bada_h, sg1_h, sg2_h, wqkv, wout, wup, wdn,
    f_out, f_gin, f_gcond, f_wada, f_bada, f_conv1, f_wqkv, f_bqv, f_wout, f_bout, f_wup, f_bup, f_conv2, f_wdn,
    f_bdn, sems, *bufs,
):
    c = lax.axis_index("canvas")
    bada, sg1, sg2, narrow, wide = bufs[0], bufs[1], bufs[2], bufs[3:9], bufs[9:15]
    small = ((sg1_h, sg1), (sg2_h, sg2), (bada_h, bada))
    large = ((wada, f_wada), (gin, f_gin), (wup, f_wup), (wdn, f_wdn), (wqkv, f_wqkv), (wout, f_wout))
    ins = [pltpu.make_async_copy(src, buf, sems.at[i]) for i, ((src, _), buf) in enumerate(zip(large, narrow))]
    ins += [pltpu.make_async_copy(src, buf, sems.at[6 + i]) for i, (src, buf) in enumerate(small)]
    outs = [pltpu.make_async_copy(buf, dst, sems.at[9 + i]) for i, ((_, dst), buf) in enumerate(zip(large, wide))]
    ins.append(pltpu.make_async_copy(out, bufs[15], sems.at[15]))
    ins.append(pltpu.make_async_copy(gcond, f_gcond, sems.at[16]))
    outs.append(pltpu.make_async_copy(bufs[15], f_out, sems.at[15]))
    for cp in ins:
        cp.start()
    for i in range(6):
        ins[i].wait()
        wide[i][...] = narrow[i][...].astype(F32)
        outs[i].start()
    for cp in ins[6:]:
        cp.wait()
    outs[6].start()

    def cut(rows, n):
        wide = rows.shape[1]
        return pltpu.roll(rows, lax.rem(wide - c * n, wide), 1)[:, 0:n]

    f_bada[...] = cut(bada[...], 576)[0]
    f_conv1[...] = cut(sg2[...], 96)[0:9]
    both = jnp.concatenate([sg2[8:16, :], sg2[8:16, :]], axis=1)
    f_bqv[...] = cut(jnp.where(iota((8, 2 * D), 1) < D, both, pltpu.roll(both, 7, 0)), 192)[1]
    f_bout[...] = cut(sg1[8:16, D : 2 * D], 96)[2:3]
    f_bdn[...] = cut(sg1[8:16, 0:D], 96)[2:3]
    ln = pl.ds(pl.multiple_of(c * HB, 128), HB)
    f_bup[...] = sg1[9:10, ln]
    f_conv2[...] = sg1[0:9, ln]
    for cp in outs:
        cp.wait()


def fast_shards(
    tokens, latent, condition, w_ada, b_ada, conv_attn, w_qkv, bias_qv, w_out, b_out,
    w_up, b_up, conv_ffn, w_down, b_down, cotangent,
):
    anyspace = pl.BlockSpec(memory_space=pl.ANY)
    vm = pl.BlockSpec(memory_space=pltpu.VMEM)
    outs = (
        ((2, 256, D), BF),
        ((2, 256, D), BF),
        ((2, 4, D), F32),
        ((96, 6 * D), BF),
        ((8, 6 * D), F32),
        ((16, FF), F32),
        ((16, D), F32),
        ((96, 3 * D), BF),
        ((96, D), BF),
        ((96, FF), BF),
        ((HB, D), BF),
    )
    got = pl.pallas_call(
        whole_block,
        out_shape=[jax.ShapeDtypeStruct(s, t) for s, t in outs],
        in_specs=[anyspace, anyspace, vm, vm] + [anyspace] * 5 + [vm] * 7,
        out_specs=[anyspace, anyspace, vm, anyspace] + [vm] * (len(outs) - 4),
        scratch_shapes=[pltpu.SemaphoreType.DMA((N_SEMS,))] + [pltpu.VMEM(s, t) for s, t in SCRATCH.values()],
        compiler_params=pltpu.CompilerParams(
            collective_id=0, has_side_effects=True, vmem_limit_bytes=VMEM_LIMIT
        ),
        name="block",
    )(
        tokens, cotangent, latent, condition, w_ada, w_qkv, w_out, w_up, w_down,
        b_ada, conv_attn, bias_qv, b_out, b_up, conv_ffn, b_down,
    )
    big = ((96, 6 * D), (2, 256, D), (96, FF), (HB, D), (96, 3 * D), (96, D))
    shapes = (
        (2, 256, D), (2, 256, D), (2, 4, D), (96, 6 * D), (576,), (9, 96), (96, 3 * D), (192,), (96, D), (1, 96),
        (96, FF), (1, HB), (9, HB), (HB, D), (1, 96),
    )
    out, gin, gcond, wada, bada, conv1, wqkv, bqv, wout, bout, wup, bup, conv2, wdn, bdn = pl.pallas_call(
        finish,
        out_shape=[jax.ShapeDtypeStruct(s, F32 if i else BF) for i, s in enumerate(shapes)],
        in_specs=[anyspace] * 11,
        out_specs=[anyspace if i in (0, 1, 3, 6, 8, 10, 13) else vm for i in range(len(shapes))],
        scratch_shapes=[pltpu.SemaphoreType.DMA((17,))]
        + [pltpu.VMEM(s, F32) for s in ((8, 6 * D), (16, FF), (16, D))]
        + [pltpu.VMEM(s, BF) for s in big]
        + [pltpu.VMEM(s, F32) for s in big]
        + [pltpu.VMEM((2, 256, D), BF)],
        compiler_params=pltpu.CompilerParams(vmem_limit_bytes=VMEM_LIMIT),
        name="finish",
    )(*got)
    flat = lambda a: a.reshape(a.shape[1])
    return (
        out, gin, gcond, wada, bada, conv1, wqkv, bqv, wout, flat(bout),
        wup, flat(bup), conv2, wdn, flat(bdn),
    )


def solution(mesh):
    placed = (
        P("canvas", "rows", None),
        P("canvas", "rows"),
        P("canvas", None, None),
        P(),
        P(),
        P(),
        P(),
        P(),
        P(),
        P(),
        P(),
        P(),
        P(),
        P(),
        P(),
        P("canvas", "rows", None),
    )
    fits = mesh.shape["rows"] == 4 and mesh.shape["canvas"] == 8
    return jax.shard_map(
        fast_shards if fits else shards,
        mesh=mesh,
        in_specs=placed,
        out_specs=(
            P("canvas", "rows", None),
            P("canvas", "rows", None),
            P("canvas", None, None),
            P("canvas", None),
            P("canvas"),
            P(None, "canvas"),
            P("canvas", None),
            P("canvas"),
            P("canvas", None),
            P("canvas"),
            P("canvas", None),
            P("canvas"),
            P(None, "canvas"),
            P("canvas", None),
            P("canvas"),
        ),
        check_vma=False,
    )
```

```python
from types import SimpleNamespace

import jax
import jax.numpy as jnp
from jax import lax
from jax.experimental import pallas as pl
from jax.experimental.pallas import tpu as pltpu
from jax.sharding import PartitionSpec as P

HEADS = 12
HEAD_DIM = 64
SIDE = 32


EPSILON = 1e-06
NEG_FILL = -1e30
PRECISE = lax.Precision.HIGHEST
VMEM_LIMIT = 65400 * 2**10


def padded_2(cells, sides, width):
    for axis, dim in sides:
        count = lax.axis_size(axis)
        ends = count - 1
        head = lax.slice_in_dim(cells, 0, width, axis=dim)
        tail = lax.slice_in_dim(cells, cells.shape[dim] - width, cells.shape[dim], axis=dim)
        cells = jnp.concatenate(
            [
                lax.ppermute(tail, axis, [(i, (i + 1) % count) for i in range(ends)]),
                cells,
                lax.ppermute(head, axis, [((i + 1) % count, i) for i in range(ends)]),
            ],
            axis=dim,
        )
    return cells


def passed_along(block, axis, distance):
    devices = range(lax.axis_size(axis))
    route = [((i - distance) % len(devices), i) for i in devices]
    return lax.ppermute(block, axis, route)


def layer_norm(values):
    centered = values - jnp.mean(values, axis=-1, keepdims=True)
    return centered * lax.rsqrt(jnp.mean(centered * centered, axis=-1, keepdims=True) + EPSILON)


def modulate_norm(values, shift, scale_part):
    return layer_norm(values) * (1.0 + scale_part) + shift


def gelu_tanh(values):
    return jax.nn.gelu(values, approximate=True)


def pad_columns(field):
    return jnp.pad(field, ((0, 0), (0, 0), (1, 1), (0, 0)))


def grid_taps(padded, kernel, rows_here, cols_here):
    summed = padded[:, 0:rows_here, 0:cols_here].astype(jnp.float32) * kernel[0]
    for tap_row in range(3):
        for tap_col in range(3):
            if tap_row + tap_col > 0:
                window = padded[
                    :, tap_row : tap_row + rows_here, tap_col : tap_col + cols_here
                ].astype(jnp.float32)
                summed = summed + window * kernel[3 * tap_row + tap_col]
    return summed


def kernel_grad(padded, grad_grid):
    rows_here = grad_grid.shape[1]
    cols_here = grad_grid.shape[2]
    grad_f = grad_grid.astype(jnp.float32)
    tap_sums = []
    for tap_row in range(3):
        for tap_col in range(3):
            window = padded[:, tap_row : tap_row + rows_here, tap_col : tap_col + cols_here].astype(
                jnp.float32
            )
            tap_sums.append(jnp.sum(window * grad_f, axis=(0, 1, 2)))
    return jnp.stack(tap_sums)


def to_groups(field, rows_here):
    canvases = field.shape[0]
    channels = field.shape[-1]
    shaped = field.reshape(canvases, rows_here // 2, 2, SIDE // 2, 2, channels)
    return shaped.transpose(0, 2, 4, 1, 3, 5).reshape(
        canvases, 4, rows_here // 2 * (SIDE // 2), channels
    )


def from_groups(field, rows_here):
    canvases = field.shape[0]
    channels = field.shape[-1]
    shaped = field.reshape(canvases, 2, 2, rows_here // 2, SIDE // 2, channels)
    return shaped.transpose(0, 3, 1, 4, 2, 5).reshape(canvases, rows_here * SIDE, channels)


def block_scores(query_heads, key_piece, query_lat, key_lat):
    canvases = key_piece.shape[0]
    count = key_piece.shape[2]
    key_heads = key_piece.reshape(canvases, 4, count, HEADS, HEAD_DIM)
    scores = jnp.einsum(
        "cgqhe,cgkhe->cghqk", query_heads, key_heads, preferred_element_type=jnp.float32
    ) * HEAD_DIM ** (-0.5)
    same_latent = query_lat[:, :, None, :, None] == key_lat[:, :, None, None, :]
    return (scores, same_latent, key_heads)


def shards(
    tokens,
    latent,
    condition,
    w_ada,
    b_ada,
    conv_attn,
    w_qkv,
    bias_qv,
    w_out,
    b_out,
    w_up,
    b_up,
    conv_ffn,
    w_down,
    b_down,
    cotangent,
):
    canvases = tokens.shape[0]
    local_tokens = tokens.shape[1]
    model_width = tokens.shape[2]
    ffn_width = w_up.shape[1]
    rows_here = local_tokens // SIDE
    group_len = local_tokens // 4
    score_scale = HEAD_DIM ** (-0.5)
    tokens_f = tokens.astype(jnp.float32)
    onehot = (latent[..., None] == jnp.arange(4)).astype(jnp.float32)
    silu_cond, silu_pull = jax.vjp(jax.nn.silu, condition)
    cond_low = silu_cond.astype(jnp.bfloat16)
    modulation = jnp.einsum(
        "ckd,df->ckf", cond_low, w_ada, preferred_element_type=jnp.float32
    ) + b_ada.astype(jnp.float32)
    per_token = jnp.einsum("cnk,ckf->cnf", onehot, modulation, precision=PRECISE)
    shift_one, scale_one, gate_one, shift_two, scale_two, gate_two = jnp.split(
        per_token, 6, axis=-1
    )
    h_one, norm_one_pull = jax.vjp(modulate_norm, tokens_f, shift_one, scale_one)
    attn_in = h_one.astype(jnp.bfloat16).reshape(canvases, rows_here, SIDE, model_width)
    attn_pad = pad_columns(padded_2(attn_in, (("rows", 1),), 1))
    conv_attn_f = conv_attn.astype(jnp.float32)
    conv_low = (
        grid_taps(attn_pad, conv_attn_f, rows_here, SIDE)
        .astype(jnp.bfloat16)
        .reshape(-1, model_width)
    )
    bias_full = jnp.concatenate(
        [bias_qv[:model_width], jnp.zeros((model_width,), jnp.bfloat16), bias_qv[model_width:]]
    ).astype(jnp.float32)
    projected = (jnp.dot(conv_low, w_qkv, preferred_element_type=jnp.float32) + bias_full).astype(
        jnp.bfloat16
    )
    grouped = to_groups(projected.reshape(canvases, local_tokens, 3 * model_width), rows_here)
    queries = grouped[..., :model_width]
    key_rows = grouped[..., model_width : 2 * model_width]
    value_rows = grouped[..., 2 * model_width :]
    lat_groups = to_groups(latent[..., None], rows_here)[..., 0]
    all_lat = lax.all_gather(lat_groups, "rows", axis=2, tiled=True)
    query_heads = queries.reshape(canvases, 4, group_len, HEADS, HEAD_DIM)
    start_best = jnp.full((canvases, 4, HEADS, group_len), NEG_FILL, jnp.float32)
    best = start_best
    key_piece = lax.all_gather(key_rows, "rows", axis=2, tiled=True)
    value_piece = lax.all_gather(value_rows, "rows", axis=2, tiled=True)
    count = key_piece.shape[2]
    fold_scores, fold_same_latent, fold_key_heads = block_scores(
        query_heads, key_piece, lat_groups, all_lat
    )
    masked = jnp.where(fold_same_latent, fold_scores, NEG_FILL)
    newest = jnp.maximum(best, jnp.max(masked, axis=-1))
    weights = jnp.where(fold_same_latent, jnp.exp(masked - newest[..., None]), 0.0)
    fold_value_heads = value_piece.astype(jnp.float32).reshape(canvases, 4, count, HEADS, HEAD_DIM)
    accum = jnp.einsum("cghqk,cgkhe->cghqe", weights, fold_value_heads, precision=PRECISE)
    best, weight_sum, accum = (newest, jnp.sum(weights, axis=-1), accum)
    attn_heads = accum / weight_sum[..., None]
    log_norm = best + jnp.log(weight_sum)
    attended = from_groups(
        attn_heads.transpose(0, 1, 3, 2, 4).reshape(canvases, 4, group_len, model_width), rows_here
    )
    attended_low = attended.astype(jnp.bfloat16).reshape(-1, model_width)
    attn_out = (
        jnp.dot(attended_low, w_out, preferred_element_type=jnp.float32) + b_out.astype(jnp.float32)
    ).reshape(canvases, local_tokens, model_width)
    middle = tokens_f + gate_one * attn_out
    h_two, norm_two_pull = jax.vjp(modulate_norm, middle, shift_two, scale_two)
    ffn_in = h_two.astype(jnp.bfloat16).reshape(-1, model_width)
    up_rows = (
        jnp.dot(ffn_in, w_up, preferred_element_type=jnp.float32) + b_up.astype(jnp.float32)
    ).astype(jnp.bfloat16)
    up_grid = up_rows.reshape(canvases, rows_here, SIDE, ffn_width)
    up_pad = pad_columns(padded_2(up_grid, (("rows", 1),), 1))
    conv_ffn_f = conv_ffn.astype(jnp.float32)
    conv_two = grid_taps(up_pad, conv_ffn_f, rows_here, SIDE)
    activated, gelu_pull = jax.vjp(gelu_tanh, conv_two)
    act_low = activated.astype(jnp.bfloat16).reshape(-1, ffn_width)
    branch = (
        jnp.dot(act_low, w_down, preferred_element_type=jnp.float32) + b_down.astype(jnp.float32)
    ).reshape(canvases, local_tokens, model_width)
    result = (middle + gate_two * branch).astype(jnp.bfloat16)
    out_grad = cotangent.astype(jnp.float32)
    branch_grad = (gate_two * out_grad).astype(jnp.bfloat16).reshape(-1, model_width)
    gate_two_grad = out_grad * branch
    g_b_down = jnp.sum(branch_grad.astype(jnp.float32), axis=0)
    g_w_down = jnp.dot(act_low.T, branch_grad, preferred_element_type=jnp.float32)
    act_grad = jnp.dot(branch_grad, w_down.T, preferred_element_type=jnp.float32).reshape(
        canvases, rows_here, SIDE, ffn_width
    )
    conv_two_grad = gelu_pull(act_grad)[0].astype(jnp.bfloat16)
    conv_two_pad = pad_columns(padded_2(conv_two_grad, (("rows", 1),), 1))
    up_grad = (
        grid_taps(conv_two_pad, conv_ffn_f[::-1], rows_here, SIDE)
        .astype(jnp.bfloat16)
        .reshape(-1, ffn_width)
    )
    g_conv_ffn = kernel_grad(up_pad, conv_two_grad)
    g_b_up = jnp.sum(up_grad.astype(jnp.float32), axis=0)
    g_w_up = jnp.dot(ffn_in.T, up_grad, preferred_element_type=jnp.float32)
    ffn_grad = jnp.dot(up_grad, w_up.T, preferred_element_type=jnp.float32).reshape(
        canvases, local_tokens, model_width
    )
    middle_part, shift_two_grad, scale_two_grad = norm_two_pull(ffn_grad)
    middle_grad = middle_part + out_grad
    gate_one_grad = middle_grad * attn_out
    attn_grad = (gate_one * middle_grad).astype(jnp.bfloat16).reshape(-1, model_width)
    g_b_out = jnp.sum(attn_grad.astype(jnp.float32), axis=0)
    g_w_out = jnp.dot(attended_low.T, attn_grad, preferred_element_type=jnp.float32)
    attended_grad = jnp.dot(attn_grad, w_out.T, preferred_element_type=jnp.float32).astype(
        jnp.bfloat16
    )
    grad_heads = to_groups(
        attended_grad.reshape(canvases, local_tokens, model_width), rows_here
    ).reshape(canvases, 4, group_len, HEADS, HEAD_DIM)
    grad_heads_f = grad_heads.astype(jnp.float32)
    delta = jnp.sum(grad_heads_f.transpose(0, 1, 3, 2, 4) * attn_heads, axis=-1)
    row_count = lax.axis_size("rows")
    here = lax.axis_index("rows")
    carried = jnp.stack([key_rows, value_rows])
    pending = jnp.zeros((2,) + key_rows.shape, jnp.float32)
    query_grad = jnp.zeros((canvases, 4, group_len, HEADS, HEAD_DIM), jnp.float32)
    for turn_index in range(row_count):
        source = (here - turn_index) % row_count
        key_lat = lax.dynamic_slice_in_dim(all_lat, source * group_len, group_len, 2)
        scores, same_latent, key_heads = block_scores(query_heads, carried[0], lat_groups, key_lat)
        value_heads = carried[1].reshape(canvases, 4, group_len, HEADS, HEAD_DIM)
        softmax_weights = jnp.where(same_latent, jnp.exp(scores - log_norm[..., None]), 0.0)
        weight_grad = jnp.einsum(
            "cgqhe,cgkhe->cghqk", grad_heads, value_heads, preferred_element_type=jnp.float32
        )
        score_grad = (softmax_weights * (weight_grad - delta[..., None])).astype(jnp.bfloat16)
        query_grad = query_grad + score_scale * jnp.einsum(
            "cghqk,cgkhe->cgqhe", score_grad, key_heads, preferred_element_type=jnp.float32
        )
        key_part = score_scale * jnp.einsum(
            "cghqk,cgqhe->cgkhe", score_grad, query_heads, preferred_element_type=jnp.float32
        )
        value_part = jnp.einsum(
            "cghqk,cgqhe->cgkhe", softmax_weights, grad_heads_f, precision=PRECISE
        )
        pending = pending + jnp.stack([key_part, value_part]).reshape(pending.shape)
        if turn_index + 1 < row_count:
            carried = passed_along(carried, "rows", 1)
        pending = passed_along(pending.astype(jnp.bfloat16), "rows", 1).astype(pending.dtype)
    query_low = query_grad.reshape(canvases, 4, group_len, model_width).astype(jnp.bfloat16)
    grouped_grad = jnp.concatenate(
        [query_low, pending[0].astype(jnp.bfloat16), pending[1].astype(jnp.bfloat16)], axis=-1
    )
    qkv_grad = from_groups(grouped_grad, rows_here).reshape(-1, 3 * model_width)
    qkv_grad_f = qkv_grad.astype(jnp.float32)
    g_bias_qv = jnp.concatenate(
        [
            jnp.sum(qkv_grad_f[:, :model_width], axis=0),
            jnp.sum(qkv_grad_f[:, 2 * model_width :], axis=0),
        ]
    )
    g_w_qkv = jnp.dot(conv_low.T, qkv_grad, preferred_element_type=jnp.float32)
    conv_one_grad = (
        jnp.dot(qkv_grad, w_qkv.T, preferred_element_type=jnp.float32)
        .astype(jnp.bfloat16)
        .reshape(canvases, rows_here, SIDE, model_width)
    )
    conv_one_pad = pad_columns(padded_2(conv_one_grad, (("rows", 1),), 1))
    attn_in_grad = grid_taps(conv_one_pad, conv_attn_f[::-1], rows_here, SIDE).reshape(
        canvases, local_tokens, model_width
    )
    g_conv_attn = kernel_grad(attn_pad, conv_one_grad)
    token_part, shift_one_grad, scale_one_grad = norm_one_pull(attn_in_grad)
    input_grad = token_part + middle_grad
    token_mod_grad = jnp.concatenate(
        [
            shift_one_grad,
            scale_one_grad,
            gate_one_grad,
            shift_two_grad,
            scale_two_grad,
            gate_two_grad,
        ],
        axis=-1,
    )
    mod_grad = jnp.einsum("cnk,cnf->ckf", onehot, token_mod_grad, precision=PRECISE)
    cond_f = cond_low.astype(jnp.float32)
    summed = (
        lax.psum(g_conv_attn.astype(jnp.bfloat16), "rows").astype(jnp.float32),
        lax.psum(g_w_qkv.astype(jnp.bfloat16), "rows").astype(jnp.float32),
        lax.psum(g_bias_qv.astype(jnp.bfloat16), "rows").astype(jnp.float32),
        lax.psum(g_w_out.astype(jnp.bfloat16), "rows").astype(jnp.float32),
        lax.psum(g_b_out.astype(jnp.bfloat16), "rows").astype(jnp.float32),
        lax.psum(g_w_up.astype(jnp.bfloat16), "rows").astype(jnp.float32),
        lax.psum(g_b_up.astype(jnp.bfloat16), "rows").astype(jnp.float32),
        lax.psum(g_conv_ffn.astype(jnp.bfloat16), "rows").astype(jnp.float32),
        lax.psum(g_w_down.astype(jnp.bfloat16), "rows").astype(jnp.float32),
        lax.psum(g_b_down.astype(jnp.bfloat16), "rows").astype(jnp.float32),
        lax.psum(mod_grad.astype(jnp.bfloat16), "rows").astype(jnp.float32),
    )
    mod_total = summed[10]
    g_w_ada = jnp.einsum("ckd,ckf->df", cond_f, mod_total, precision=PRECISE)
    g_b_ada = jnp.sum(mod_total, axis=(0, 1))
    shares = (
        lax.psum_scatter(
            g_w_ada.astype(jnp.bfloat16), "canvas", scatter_dimension=0, tiled=True
        ).astype(jnp.float32),
        lax.psum_scatter(
            g_b_ada.astype(jnp.bfloat16), "canvas", scatter_dimension=0, tiled=True
        ).astype(jnp.float32),
        lax.psum_scatter(
            summed[0].astype(jnp.bfloat16), "canvas", scatter_dimension=1, tiled=True
        ).astype(jnp.float32),
        lax.psum_scatter(
            summed[1].astype(jnp.bfloat16), "canvas", scatter_dimension=0, tiled=True
        ).astype(jnp.float32),
        lax.psum_scatter(
            summed[2].astype(jnp.bfloat16), "canvas", scatter_dimension=0, tiled=True
        ).astype(jnp.float32),
        lax.psum_scatter(
            summed[3].astype(jnp.bfloat16), "canvas", scatter_dimension=0, tiled=True
        ).astype(jnp.float32),
        lax.psum_scatter(
            summed[4].astype(jnp.bfloat16), "canvas", scatter_dimension=0, tiled=True
        ).astype(jnp.float32),
        lax.psum_scatter(
            summed[5].astype(jnp.bfloat16), "canvas", scatter_dimension=0, tiled=True
        ).astype(jnp.float32),
        lax.psum_scatter(
            summed[6].astype(jnp.bfloat16), "canvas", scatter_dimension=0, tiled=True
        ).astype(jnp.float32),
        lax.psum_scatter(
            summed[7].astype(jnp.bfloat16), "canvas", scatter_dimension=1, tiled=True
        ).astype(jnp.float32),
        lax.psum_scatter(
            summed[8].astype(jnp.bfloat16), "canvas", scatter_dimension=0, tiled=True
        ).astype(jnp.float32),
        lax.psum_scatter(
            summed[9].astype(jnp.bfloat16), "canvas", scatter_dimension=0, tiled=True
        ).astype(jnp.float32),
    )
    cond_grad = silu_pull(
        jnp.einsum("ckf,df->ckd", mod_total, w_ada.astype(jnp.float32), precision=PRECISE)
    )[0]
    return (
        result,
        input_grad,
        cond_grad,
        shares[0],
        shares[1],
        shares[2],
        shares[3],
        shares[4],
        shares[5],
        shares[6],
        shares[7],
        shares[8],
        shares[9],
        shares[10],
        shares[11],
    )

BF = jnp.bfloat16
F32 = jnp.float32
D = 768
FF = 3072
HB = 384
BIG = -1e30


def dot(a, b):
    return jnp.dot(a, b, preferred_element_type=F32)


def dot_t(a, b):
    return lax.dot_general(a, b, (((1,), (1,)), ((), ())), preferred_element_type=F32)


def dot_l(a, b):
    return lax.dot_general(a, b, (((0,), (0,)), ((), ())), preferred_element_type=F32)


def iota(shape, dim):
    return lax.broadcasted_iota(jnp.int32, shape, dim)


def ones_where(mask):
    return jnp.where(mask, 1.0, 0.0).astype(BF)


def taps_of(pr, pc, back):
    found = []
    for i in range(3):
        for j in range(3):
            di, dj = (1 - i, 1 - j) if back else (i - 1, j - 1)
            gr = pr if di == 0 else 1 - pr
            gc = pc if dj == 0 else 1 - pc
            ro = 0 if di == 0 else (pr - 1 if di < 0 else pr)
            co = 0 if dj == 0 else (2 * pc + dj - 1) // 2
            found.append((3 * i + j, 2 * gr + gc, ro, co != 0))
    return found


def shifted(rows, pc):
    n = rows.shape[0]
    col = iota(rows.shape, 0) % 16
    if pc == 1:
        return jnp.where(col == 0, 0.0, pltpu.roll(rows, 1, 0))
    return jnp.where(col == 15, 0.0, pltpu.roll(rows, n - 1, 0))


def conv_sum(load, kr, taps):
    total = None
    for t, gsrc, ro, moved in taps:
        term = load(gsrc, ro, moved).astype(F32) * kr[t]
        total = term if total is None else total + term
    return total


def conv_both(load, here, kr, gk, taps):
    total = None
    for t, gsrc, ro, moved in taps:
        src = load(gsrc, ro, moved).astype(F32)
        term = src * kr[t]
        total = term if total is None else total + term
        gk[t] = gk[t] + fold_rows(src * here)
    return total


def fold_rows(rows):
    return jnp.sum(rows.reshape(rows.shape[0] // 8, 8, 128), axis=0)


def norm_parts(v):
    mean = jnp.mean(v, axis=-1, keepdims=True)
    cen = v - mean
    inv = lax.rsqrt(jnp.mean(cen * cen, axis=-1, keepdims=True) + EPSILON)
    return cen * inv, inv


def norm_back(n, nrm, inv):
    m1 = jnp.mean(n, axis=-1, keepdims=True)
    m2 = jnp.mean(n * nrm, axis=-1, keepdims=True)
    return (n - m1 - nrm * m2) * inv


SCRATCH = dict(
    stg_t=((2, 4, 64, D), BF),
    stg_c=((2, 4, 64, D), BF),
    tok=((4, 256, D), BF),
    cot=((4, 256, D), BF),
    latc=((4, 1, 256), jnp.int32),
    lv=((4, 256, 128), F32),
    oh=((4, 256, 128), BF),
    modhl=((32, 6 * D), BF),
    pm=((256, 256), BF),
    ain=((4, 288, D), BF),
    c1t=((D, 1024), BF),
    tmpa=((4, 256, D), BF),
    qkv=((4, 256, 3 * HB), BF),
    att=((4, 256, D), BF),
    fint=((D, 1024), BF),
    bg=((4, 256, D), BF),
    mid=((2, 256, D), F32),
    ub=((4, 288, HB), BF),
    us=((4, 288, HB), BF),
    gb=((4, 288, HB), BF),
    gs=((4, 288, HB), BF),
    gp=((2, 256, D), F32),
    act=((4, 256, 2 * D), BF),
    upg=((4, 256, 2 * D), BF),
    upr=((4, 256, 2 * D), BF),
    actt=((HB, 1024), BF),
    wup=((D, 2 * D), BF),
    wdn=((2 * D, D), BF),
    wq=((D, 3 * HB), BF),
    wo=((D, D), BF),
    gwd=((4, HB, D), BF),
    gwo=((4, 96, D), BF),
    rd_a=((192, D), BF),
    rd_b=((192, D), BF),
    rd_x=((HB, D), BF),
    rd_y=((HB, D), BF),
    ru_a=((96, 2 * D), BF),
    ru_b=((96, 2 * D), BF),
    ru_x=((192, 2 * D), BF),
    ru_y=((192, 2 * D), BF),
    rq_a=((96, 3 * HB), BF),
    rq_b=((96, 3 * HB), BF),
    rq_x=((192, 3 * HB), BF),
    rq_y=((192, 3 * HB), BF),
    ro_a=((48, D), BF),
    ro_b=((48, D), BF),
    ro_x=((96, D), BF),
    ro_y=((96, D), BF),
    su=((96, 2 * D), BF),
    sq=((96, 3 * HB), BF),
    zd_a=((HB, D), BF),
    zd_b=((HB, D), BF),
    zu_a=((96, FF), BF),
    zu_b=((96, FF), BF),
    zq_a=((96, 3 * D), BF),
    zq_b=((96, 3 * D), BF),
    zo_a=((96, D), BF),
    zo_b=((96, D), BF),
    frcv=((2, 4, 64, D), BF),
    brcv=((2, 4, 64, D), BF),
    oland=((2, 4, 64, D), BF),
    gland=((2, 4, 64, D), BF),
    condc=((16, D), F32),
    clow=((4, 16, D), BF),
    mg1=((16, D), F32),
    mg2=((16, HB), F32),
    mgs1=((16, D), BF),
    mgr1=((16, D), BF),
    mgs2=((16, HB), BF),
    mgr2=((16, HB), BF),
    mga1=((16, 16, D), BF),
    mga2=((16, 16, HB), BF),
    sg1=((16, FF), F32),
    sg1s=((1, 16, FF), BF),
    sg1r=((5, 16, FF), BF),
    sg2=((16, D), F32),
    sg2s=((1, 16, D), BF),
    sg2r=((5, 16, D), BF),
    cgsum=((16, D), F32),
    crcv=((2, 8, D), F32),
    lat_own=((2, 1, 256), jnp.int32),
    cond_own=((8, D), F32),
    par=((16, FF), F32),
)
N_SEMS = 340


def whole_block(
    tok_h, cot_h, lat_in, cond_in, wada_h, wqkv_h, wout_h, wup_h, wdn_h,
    p_bada, p_conv1, p_bqv, p_bout, p_bup, p_conv2, p_bdn,
    o_out, o_gin, o_cond, o_wada, o_bada, o_sg1, o_sg2, o_wqkv, o_wout, o_wup, o_wdn,
    sems, *bufs,
):
    v = SimpleNamespace(**dict(zip(SCRATCH, bufs)))
    stg_t, stg_c, tok, cot, latc, lv, oh = v.stg_t, v.stg_c, v.tok, v.cot, v.latc, v.lv, v.oh
    modhl, pm, ain, c1t, tmpa, qkv, att = v.modhl, v.pm, v.ain, v.c1t, v.tmpa, v.qkv, v.att
    fint, bg, mid, ub, us, gb, gs = v.fint, v.bg, v.mid, v.ub, v.us, v.gb, v.gs
    gp, act, upg, actt, wup, wdn, wq, wo = v.gp, v.act, v.upg, v.actt, v.wup, v.wdn, v.wq, v.wo
    upr = v.upr
    gwd, gwo, condc, clow = v.gwd, v.gwo, v.condc, v.clow

    c = lax.axis_index("canvas")
    r = lax.axis_index("rows")
    k = c % 2
    x = (c // 2) % 2
    y = c // 4
    col = 2 * y + x
    r1 = r + 1 - 2 * (r % 2)
    r2 = (r + 2) % 4
    r3 = 3 - r
    sib = (y * 4 + x * 2 + 1 - k, r)
    px = (y * 4 + (1 - x) * 2 + k, r)
    py = ((1 - y) * 4 + x * 2 + k, r)
    owner = r // 2
    is_own = k == owner
    owner_c = y * 4 + x * 2 + owner

    count = [0]

    def sem(n=1):
        first = count[0]
        count[0] += n
        return first

    last = []

    def remote(src, dst, ss, rs, dev):
        return pltpu.make_async_remote_copy(
            src_ref=src, dst_ref=dst, send_sem=sems.at[ss], recv_sem=sems.at[rs],
            device_id=dev, device_id_type=pl.DeviceIdType.MESH,
        )

    def local(src, dst, s):
        return pltpu.make_async_copy(src, dst, sems.at[s])

    def swap(src, dst, dev):
        cp = remote(src, dst, sem(), sem(), dev)
        cp.start()
        last.append(cp.wait_send)
        return cp

    barrier = pltpu.get_barrier_semaphore()
    for dev in (sib, px, py, (c, r1), (c, r2), (c, r3), (sib[0], r1), (sib[0], r2), (sib[0], r3)):
        pl.semaphore_signal(barrier, inc=1, device_id=dev, device_id_type=pl.DeviceIdType.MESH)
    s_tok = sem()
    s_cot = sem()
    ld_tok = local(tok_h, act.at[pl.ds(0, 2), :, pl.ds(0, D)], s_tok)
    ld_tok.start()
    ld_cot = local(cot_h, act.at[pl.ds(0, 2), :, pl.ds(D, D)], s_cot)
    ld_cot.start()
    s_wa = sem(2)

    def load_ada(p):
        return local(wada_h.at[:, pl.ds(p * D, D)], wup.at[:, pl.ds((p % 2) * D, D)], s_wa + p % 2)

    load_ada(0).start()
    load_ada(1).start()
    s_w = sem(3)
    ld_wq = [
        local(wqkv_h.at[:, pl.ds(pl.multiple_of(part * D + HB * k, 128), HB)], wq.at[:, pl.ds(part * HB, HB)], s_w + part)
        for part in range(3)
    ]
    for cp in ld_wq:
        cp.start()
    ld_wo = local(wout_h, wo, sem())
    ld_wo.start()
    s_wd = sem(4)
    ld_wd = [
        local(wdn_h.at[pl.ds(pl.multiple_of(HB * (2 * b + k), 128), HB), :], wdn.at[pl.ds(HB * b, HB), :], s_wd + b)
        for b in range(4)
    ]
    for cp in ld_wd:
        cp.start()
    pi = iota((256, 256), 0)
    group, place = pi // 64, pi % 64
    nat = (2 * (place // 16) + group // 2) * 32 + 2 * (place % 16) + group % 2
    pm[...] = ones_where(iota((256, 256), 1) == nat)
    for buf in (ain, ub, us, gb, gs):
        wide = buf.shape[2]
        for g in range(4):
            buf[g, 0:16, :] = jnp.zeros((16, wide), BF)
            buf[g, 272:288, :] = jnp.zeros((16, wide), BF)
    lat_h, par = v.lat_own, v.par
    for i in range(2):
        lat_h[i] = lat_in[i : i + 1, :]
        v.cond_own[4 * i : 4 * i + 4, :] = cond_in[i]
    condc[pl.ds(pl.multiple_of(8 * k, 8), 8), :] = v.cond_own[...]
    par[0:9, :] = p_conv2[...].astype(F32)

    def row_of(ref):
        return ref[...].astype(F32).reshape(1, ref.shape[0])

    par[9:10, :] = row_of(p_bup)
    par[10:11, 0:D] = row_of(p_bdn)
    par[10:11, D : 2 * D] = row_of(p_bout)
    par[10:11, 2 * D : 4 * D] = row_of(p_bqv)
    taps1 = p_conv1[...].astype(F32)
    for t in range(9):
        par[11 + t // 4 : 12 + t // 4, (t % 4) * D : (t % 4) * D + D] = taps1[t : t + 1]
    ada = row_of(p_bada)
    par[14:15, :] = ada[:, 0 : 4 * D]
    par[15:16, 0 : 2 * D] = ada[:, 4 * D : 6 * D]
    pl.semaphore_wait(barrier, 9)

    cond_cp = swap(
        condc.at[pl.ds(pl.multiple_of(8 * k, 8), 8), :], condc.at[pl.ds(pl.multiple_of(8 * k, 8), 8), :], sib
    )
    mine64 = pl.ds(pl.multiple_of(r * 64, 64), 64)
    rt, rl, rc = sem(4), sem(4), sem(4)
    st, sl, sc = sem(2), sem(2), sem(2)

    def give(src, dst, ss, rs, i):
        q = 2 * k + i
        far = remote(src, dst, ss, rs, (c, q))
        near = local(src, dst, rs)

        @pl.when(q != r)
        def _():
            far.start()

        @pl.when(q == r)
        def _():
            near.start()

        def done():
            @pl.when(q != r)
            def _():
                far.wait_send()

        return done

    tok_sent, cot_sent = [], []
    ld_tok.wait()
    for i in range(2):
        stg_t[i] = dot(pm[...], act[i, :, 0:D]).astype(BF).reshape(4, 64, D)
        tok_sent.append(give(stg_t.at[i], tok.at[:, mine64, :], st + i, rt + r, i))
        last.append(give(lat_h.at[i], latc.at[r], sl + i, rl + r, i))

    ld_cot.wait()
    for i in range(2):
        stg_c[i] = dot(pm[...], act[i, :, D : 2 * D]).astype(BF).reshape(4, 64, D)

    cond_cp.wait_recv()
    cond = condc[...]
    sig = 1.0 / (1.0 + jnp.exp(-cond))
    mine_low = (cond * sig).astype(BF)
    clow[col] = mine_low
    low_x = swap(clow.at[col], clow.at[col], px)
    for p in range(6):
        load_ada(p).wait()
        mod = dot(mine_low, wup[:, (p % 2) * D : (p % 2) * D + D])
        mod = mod + par[14 + p // 4 : 15 + p // 4, (p % 4) * D : (p % 4) * D + D]
        high = mod.astype(BF)
        modhl[0:16, p * D : (p + 1) * D] = high
        modhl[16:32, p * D : (p + 1) * D] = (mod - high.astype(F32)).astype(BF)
        if p + 2 < 6:
            load_ada(p + 2).start()
    s_wu = sem(4)
    ld_wu = [
        local(wup_h.at[:, pl.ds(pl.multiple_of(HB * (2 * b + k), 128), HB)], wup.at[:, pl.ds(HB * b, HB)], s_wu + b)
        for b in range(4)
    ]
    for cp in ld_wu:
        cp.start()

    def piece(o, p):
        return dot(o[:, 0:32], modhl[:, p * D : (p + 1) * D])

    ft, fl, fc = sem(4), sem(4), sem(4)
    order = (r, r1, r2, r3)

    def arrive(buf, of, rs, fs, then=None):
        passed = []
        for d in range(4):
            s = order[d]
            place = of(s)
            cp = remote(buf.at[place], buf.at[place], fs + d, rs + s, sib)
            cp.wait_recv()

            @pl.when(is_own)
            def _():
                cp.start()

            def done(cp=cp):
                @pl.when(is_own)
                def _():
                    cp.wait_send()

            passed.append(done)
            if then is not None:
                then(s)
        return passed

    def slab(s):
        return (slice(None), pl.ds(pl.multiple_of(s * 64, 64), 64), slice(None))

    last.extend(arrive(latc, lambda s: s, rl, fl))
    def norm_one(s):
        rows = jnp.broadcast_to(latc[s].astype(F32), (128, 256)).astype(BF)
        ids = dot_t(pm[...], rows)
        lane = iota((256, 128), 1)
        want = (lane % 16 - 4 * r).astype(F32)
        o = ones_where((want == ids) & (lane < 32))
        at = pl.ds(pl.multiple_of(s * 64, 64), 64)
        lv[:, at, :] = ids.reshape(4, 64, 128)
        oh[:, at, :] = o.reshape(4, 64, 128)
        nrm, _inv = norm_parts(tok[:, at, :].reshape(256, D).astype(F32))
        h = (nrm * (1.0 + piece(o, 1)) + piece(o, 0)).astype(BF)
        padded = pl.ds(pl.multiple_of(s * 64 + 16, 16), 64)
        ain[:, padded, :] = h.reshape(4, 64, D)
        for g in range(4):
            sh = shifted(h[g * 64 : g * 64 + 64].astype(F32), g % 2).astype(BF)
            us[g, padded, :] = sh[:, 0:HB]
            gs[g, padded, :] = sh[:, HB:D]

    tok_passed = arrive(tok, slab, rt, ft, norm_one)
    for i in range(2):
        cot_sent.append(give(stg_c.at[i], cot.at[:, mine64, :], sc + i, rc + r, i))

    for hh in range(2):
        side = us if hh == 0 else gs

        def conv_one(lt, _, hh=hh, side=side):
            l0 = pl.multiple_of(lt * 128, 128)
            la = pl.multiple_of(hh * HB + lt * 128, 128)
            kr = [par[11 + t // 4 : 12 + t // 4, pl.ds((t % 4) * D + la, 128)] for t in range(9)]
            for g in range(4):
                for h in range(2):

                    def load(gsrc, ro, moved):
                        rows = pl.ds(16 + 16 * ro + 128 * h, 128)
                        return side[gsrc, rows, pl.ds(l0, 128)] if moved else ain[gsrc, rows, pl.ds(la, 128)]

                    low = conv_sum(load, kr, taps_of(g // 2, g % 2, False)).astype(BF)
                    tmpa[g, h * 128 : h * 128 + 128, pl.ds(la, 128)] = low
                    c1t[pl.ds(la, 128), g * 256 + h * 128 : g * 256 + h * 128 + 128] = low.astype(F32).T.astype(BF)
            return 0

        lax.fori_loop(0, 3, conv_one, 0)

    for cp in ld_wq:
        cp.wait()
    kcol = pl.multiple_of(HB * k, 128)
    b_q = par[10:11, pl.ds(2 * D + kcol, HB)]
    b_v = par[10:11, pl.ds(3 * D + kcol, HB)]

    def project(n, _):
        two = pl.ds(2 * n, 2)
        rows = tmpa[two].reshape(512, D)
        got = dot(rows, wq[:, 0:HB]) + b_q
        qkv[two, :, 0:HB] = (got.astype(BF).astype(F32) * 0.125).astype(BF).reshape(2, 256, HB)
        qkv[two, :, HB : 2 * HB] = dot(rows, wq[:, HB : 2 * HB]).astype(BF).reshape(2, 256, HB)
        got = dot(rows, wq[:, 2 * HB : 3 * HB]) + b_v
        qkv[two, :, 2 * HB : 3 * HB] = got.astype(BF).reshape(2, 256, HB)
        return 0

    lax.fori_loop(0, 2, project, 0)

    lane1 = iota((1, 128), 1)
    lmf = [jnp.where(lane1 < 64, 1.0, 0.0), jnp.where(lane1 < 64, 0.0, 1.0)]
    lmb = [m.astype(BF) for m in lmf]
    sa, ra = sem(4), sem(4)

    def masks_of(g):
        lane = iota((256, 128), 1)
        same = lane.astype(F32) == lv[g]
        oq = jnp.where(same & (lane < 4), 1.0, 0.0).astype(BF)
        mk = jnp.where(same | (lane >= 4), 0.0, BIG).astype(BF)
        return oq, mk

    def att_copy(g):
        place = att.at[g, :, pl.ds(kcol, HB)]
        return remote(place, place, sa + g, ra + g, sib)

    def attend(g, _):
        oq, mk = masks_of(g)
        oq2 = jnp.concatenate([oq, oq], axis=0)
        for hp in range(3):
            qp = qkv[g, :, hp * 128 : hp * 128 + 128]
            ka = jnp.concatenate([qkv[g, :, HB + hp * 128 : HB + hp * 128 + 128], mk], axis=1)
            vp = qkv[g, :, 2 * HB + hp * 128 : 2 * HB + hp * 128 + 128]
            qa = jnp.concatenate([qp * lmb[0], qp * lmb[1]], axis=0)
            s = dot_t(jnp.concatenate([qa, oq2], axis=1), ka)
            e = jnp.exp(s - jnp.max(s, axis=1, keepdims=True))
            o = dot(e.astype(BF), vp) * (1.0 / jnp.sum(e, axis=1, keepdims=True))
            mixed = o[0:256] * lmf[0] + o[256:512] * lmf[1]
            att[g, :, pl.ds(pl.multiple_of(kcol + hp * 128, 128), 128)] = mixed.astype(BF)
        att_copy(g).start()
        return 0

    lax.fori_loop(0, 4, attend, 0)
    low_x.wait_recv()
    low_y = swap(clow.at[pl.ds(2 * y, 2)], clow.at[pl.ds(2 * y, 2)], py)

    ld_wo.wait()
    kother = pl.multiple_of(HB * (1 - k), 128)

    def norm_two(g, _):
        for h in range(2):
            rows = slice(h * 128, h * 128 + 128)
            a = att[g, rows, :]
            ao = dot(a, wo[...]) + par[10:11, D : 2 * D]
            o = oh[g, rows, :]
            m = tok[g, rows, :].astype(F32) + piece(o, 2) * ao
            nrm, _inv = norm_parts(m)
            f = (nrm * (1.0 + piece(o, 4)) + piece(o, 3)).astype(BF)
            tmpa[g, rows, :] = f
            at = pl.ds(pl.multiple_of(g * 256 + h * 128, 128), 128)
            fint[:, at] = f.astype(F32).T.astype(BF)
        return 0

    for g in range(4):
        att_copy(g).wait()
    lax.fori_loop(0, 4, norm_two, 0)
    last.extend(arrive(cot, slab, rc, fc))

    def gate_cot(g, _):
        bg[g] = (piece(oh[g], 5) * cot[g].astype(F32)).astype(BF)
        return 0

    lax.fori_loop(0, 4, gate_cot, 0)

    class Scatter:
        def __init__(self, src, a, b, rx, ry):
            self.src, self.a, self.b, self.rx, self.ry = src, a, b, rx, ry
            n = a.shape[0]
            self.n = n
            ss = sem(8)
            self.ca = remote(src(0, 0, n), a, ss, ss + 1, px)
            self.cb = remote(src(0, n, n), b, ss + 2, ss + 3, py)
            self.cx = remote(src(1, 0, 2 * n), rx, ss + 4, ss + 5, px)
            self.cy = remote(src(2, 0, 2 * n), ry, ss + 6, ss + 7, py)

        def s0(self):
            self.ca.start()
            self.cb.start()

        def s1(self):
            self.cb.wait_recv()
            part = self.src(1, self.n, self.n)
            part[...] = (part[...].astype(F32) + self.b[...].astype(F32)).astype(BF)
            self.cx.start()

        def s2(self):
            self.ca.wait_recv()
            part = self.src(2, 0, self.n)
            part[...] = (part[...].astype(F32) + self.a[...].astype(F32)).astype(BF)
            self.cy.start()

        def s3(self):
            self.cx.wait_recv()
            self.cy.wait_recv()
            part = self.src(3, 0, 2 * self.n)
            return part[...].astype(F32) + self.rx[...].astype(F32) + self.ry[...].astype(F32)

        def sent(self):
            for cp in (self.ca, self.cb, self.cx, self.cy):
                cp.wait_send()

    inner = (r % 3) != 0

    class Line:
        def __init__(self, pieces):
            self.parts = []
            for o, a, b in pieces:
                ss = sem(6)
                up = remote(o, a, ss, ss + 1, (c, r1))
                mid = remote(o, b, ss + 2, ss + 3, (c, r3))
                down = remote(o, a, ss + 4, ss + 5, (c, r1))
                self.parts.append((o, a, b, up, mid, down))

        def s0(self, which=None):
            @pl.when(jnp.logical_not(inner))
            def _():
                for i, part in enumerate(self.parts):
                    if which is None or which == i:
                        part[3].start()

        def s1(self):
            @pl.when(inner)
            def _():
                for o, a, _b, up, mid, _down in self.parts:
                    up.wait_recv()
                    o[...] = (o[...].astype(F32) + a[...].astype(F32)).astype(BF)
                    mid.start()

        def s2(self):
            @pl.when(inner)
            def _():
                for o, _a, b, _up, mid, down in self.parts:
                    mid.wait()
                    o[...] = (o[...].astype(F32) + b[...].astype(F32)).astype(BF)
                    down.start()

        def s3(self):
            @pl.when(inner)
            def _():
                for part in self.parts:
                    part[5].wait_send()

            @pl.when(jnp.logical_not(inner))
            def _():
                for o, a, _b, up, _mid, down in self.parts:
                    up.wait_send()
                    down.wait_recv()
                    o[...] = a[...]

    class Gather:
        def __init__(self, own, got, everyone):
            self.own, self.got, self.everyone = own, got, everyone
            self.zr, self.zs = sem(4), sem(3)
            self.xy = sem(4)

        def s0(self):
            self.everyone[slot] = (self.own[...].astype(F32) + self.got[...].astype(F32)).astype(BF)
            place = self.everyone.at[slot]
            for d, s in enumerate((r1, r2, r3)):
                cp = remote(place, place, self.zs + d, self.zr + r, (c, s))
                cp.start()
                last.append(cp.wait_send)

        def s1(self):
            for s in (r1, r2, r3):
                place = self.everyone.at[4 * col + s]
                local(place, place, self.zr + s).wait()
            place = self.everyone.at[pl.ds(4 * col, 4)]
            self.cx = remote(place, place, self.xy, self.xy + 1, px)
            self.cx.start()
            last.append(self.cx.wait_send)

        def s2(self):
            self.cx.wait_recv()
            place = self.everyone.at[pl.ds(8 * y, 8)]
            self.cy = remote(place, place, self.xy + 2, self.xy + 3, py)
            self.cy.start()
            last.append(self.cy.wait_send)

        def s3(self):
            self.cy.wait_recv()

    def by_rows(out, za, zb, cuts):
        n = out.shape[0] // cuts
        rows = [pl.ds(i * n, n) for i in range(cuts)]
        return Line([(out.at[at], za.at[at], zb.at[at]) for at in rows])

    class Columns:
        def __init__(self, src, a, b, rx, ry, su, out, za, zb):
            self.src, self.a, self.b, self.rx, self.ry, self.su, self.out = src, a, b, rx, ry, su, out
            count = su.shape[1] // HB
            self.lanes = [pl.ds(t * HB, HB) for t in range(count)]
            self.cps = []
            for ln in self.lanes:
                ss = sem(10)
                self.cps.append(
                    (
                        remote(src(0, 0, 96, ln), a.at[:, ln], ss, ss + 1, px),
                        remote(src(0, 96, 96, ln), b.at[:, ln], ss + 2, ss + 3, py),
                        remote(src(1, 0, 192, ln), rx.at[:, ln], ss + 4, ss + 5, px),
                        remote(src(2, 0, 192, ln), ry.at[:, ln], ss + 6, ss + 7, py),
                        remote(
                            src(3, pl.multiple_of(96 * (1 - k), 32), 96, ln), su.at[:, ln], ss + 8, ss + 9, sib
                        ),
                    )
                )
            both = [pl.ds(t * D, D) for t in range(count)]
            self.line = Line([(out.at[:, at], za.at[:, at], zb.at[:, at]) for at in both])

        def s0(self, t):
            self.cps[t][0].start()
            self.cps[t][1].start()

        def s1(self, t):
            ca, cb, cx, cy, _ = self.cps[t]
            ln = self.lanes[t]
            cb.wait_recv()
            part = self.src(1, 96, 96, ln)
            part[...] = (part[...].astype(F32) + self.b[:, ln].astype(F32)).astype(BF)
            cx.start()
            ca.wait_recv()
            part = self.src(2, 0, 96, ln)
            part[...] = (part[...].astype(F32) + self.a[:, ln].astype(F32)).astype(BF)
            cy.start()

        def s3(self, t):
            ln = self.lanes[t]
            self.cps[t][2].wait_recv()
            self.cps[t][3].wait_recv()
            part = self.src(3, 0, 192, ln)
            part[...] = (part[...].astype(F32) + self.rx[:, ln].astype(F32) + self.ry[:, ln].astype(F32)).astype(BF)
            self.cps[t][4].start()
            mine = self.src(3, pl.multiple_of(96 * k, 32), 96, ln)
            self.out[:, pl.ds(pl.multiple_of(t * D + HB * k, 128), HB)] = mine[...]

        def s4(self, t):
            self.cps[t][4].wait()
            self.out[:, pl.ds(pl.multiple_of(t * D + HB * (1 - k), 128), HB)] = self.su[:, self.lanes[t]]
            self.line.s0(t)

        def sent(self):
            for cps in self.cps:
                for cp in cps[0:4]:
                    cp.wait_send()

    class Everyone:
        def __init__(self, total, send, recv):
            self.total, self.send, self.recv = total, send, recv
            ss = sem(6)
            devs = (sib, px, py)
            self.cps = [remote(send.at[0], recv.at[i], ss + 2 * i, ss + 2 * i + 1, devs[i]) for i in range(3)]

        def go(self, i):
            self.send[0] = self.total[...].astype(BF)
            self.cps[i].start()

        def end(self, i):
            self.cps[i].wait()
            self.total[...] = self.send[0].astype(F32) + self.recv[i].astype(F32)

        def plane(self):
            self.end(2)
            self.send[0] = self.total[...].astype(BF)

    mga1, mga2 = v.mga1, v.mga2
    mgs1, mgr1, mgs2, mgr2 = v.mgs1, v.mgr1, v.mgs2, v.mgr2
    slot = 4 * col + r
    gat1 = Gather(mgs1, mgr1, mga1)
    gat2 = Gather(mgs2, mgr2, mga2)
    sum_d = Scatter(lambda p, r0, n: gwd.at[p, pl.ds(r0, n)], v.rd_a, v.rd_b, v.rd_x, v.rd_y)
    sum_u = Columns(
        lambda p, r0, n, ln: upr.at[p, pl.ds(r0, n), ln],
        v.ru_a, v.ru_b, v.ru_x, v.ru_y, v.su, o_wup, v.zu_a, v.zu_b,
    )
    sum_q = Columns(
        lambda p, r0, n, ln: wup.at[pl.ds(192 * p + r0, n), ln],
        v.rq_a, v.rq_b, v.rq_x, v.rq_y, v.sq, o_wqkv, v.zq_a, v.zq_b,
    )
    sum_o = Scatter(lambda p, r0, n: gwo.at[p, pl.ds(r0, n)], v.ro_a, v.ro_b, v.ro_x, v.ro_y)
    line_d = by_rows(o_wdn, v.zd_a, v.zd_b, 4)
    line_u = sum_u.line
    line_o = by_rows(o_wout, v.zo_a, v.zo_b, 1)
    line_q = sum_q.line
    sg1, sg2 = v.sg1, v.sg2
    all1 = Everyone(sg1, v.sg1s, v.sg1r)
    all2 = Everyone(sg2, v.sg2s, v.sg2r)
    line_a = Line([(v.sg1s.at[0], v.sg1r.at[3], v.sg1r.at[4])])
    line_b = Line([(v.sg2s.at[0], v.sg2r.at[3], v.sg2r.at[4])])
    sg1[...] = jnp.zeros((16, FF), F32)
    sg2[...] = jnp.zeros((16, D), F32)

    def block_at(pos):
        fx = 1 - pos // 2
        fy = 1 - pos % 2
        bx = x + fx - 2 * x * fx
        by = y + fy - 2 * y * fy
        return 2 * by + bx

    for cp in ld_wd + ld_wu:
        cp.wait()

    def hidden(pos, _):
        b = block_at(pos)
        lo = pl.multiple_of(b * HB, 128)
        wide = pl.multiple_of(HB * (2 * b + k), 128)

        def up(pr, _):
            both = dot(tmpa[pl.ds(2 * pr, 2)].reshape(512, D), wup[:, pl.ds(lo, HB)])
            for pc in range(2):
                g = 2 * pr + pc
                u = (both[pc * 256 : pc * 256 + 256] + par[9:10, pl.ds(wide, HB)]).astype(BF)
                ub[g, 16:272, :] = u
                upr[g, :, pl.ds(lo, HB)] = u
                us[g, 16:272, :] = shifted(u.astype(F32), pc).astype(BF)
            return 0

        lax.fori_loop(0, 2, up, 0)

        def conv_gelu(lt, _):
            l0 = pl.multiple_of(lt * 128, 128)
            ln = pl.ds(l0, 128)
            kr = [par[t : t + 1, pl.ds(wide + l0, 128)] for t in range(9)]
            for g in range(4):
                for h in range(2):

                    def load(gsrc, ro, moved):
                        return (us if moved else ub)[gsrc, pl.ds(16 + 16 * ro + 128 * h, 128), ln]

                    acc = conv_sum(load, kr, taps_of(g // 2, g % 2, False))
                    sq = acc * acc
                    th = jnp.tanh(0.7978845608028654 * acc * (1.0 + 0.044715 * sq))
                    half = 0.5 + 0.5 * th
                    low = (acc * half).astype(BF)
                    slope = half + half * (1.0 - th) * acc * (0.7978845608028654 + 0.10703222440890037 * sq)
                    rows = slice(h * 128, h * 128 + 128)
                    act[g, rows, pl.ds(lo + l0, 128)] = low
                    upg[g, rows, pl.ds(lo + l0, 128)] = slope.astype(BF)
                    actt[ln, g * 256 + h * 128 : g * 256 + h * 128 + 128] = low.astype(F32).T.astype(BF)
            return 0

        lax.fori_loop(0, 3, conv_gelu, 0)

        def grad_down(n, _):
            ln = pl.ds(pl.multiple_of(n * 256, 128), 256)
            gwd[pos, :, ln] = dot(actt[...], bg[:, :, ln].reshape(1024, 256)).astype(BF)
            return 0

        lax.fori_loop(0, 3, grad_down, 0)
        pl.when(pos == 0)(sum_d.s0)

        @pl.when(pos == 2)
        def _():
            sum_d.s1()
            sum_d.s2()

        return 0

    lax.fori_loop(0, 4, hidden, 0)

    for done in tok_sent + cot_sent:
        done()
    other2 = pl.ds(2 * (1 - k), 2)
    mine2 = pl.ds(2 * k, 2)

    def half_f(which, n):
        return dot_t(upg[which].reshape(512, 2 * D), wup[n * HB : n * HB + HB, :])

    def half_b(which, n):
        return dot(act[which].reshape(512, 2 * D), wdn[:, n * HB : n * HB + HB])

    for n in range(2):
        cols = slice(n * HB, n * HB + HB)
        stg_c[:, :, :, cols] = half_b(other2, n).astype(BF).reshape(2, 4, 64, HB)
    b_cp = remote(stg_c, v.brcv, sem(), sem(), sib)
    b_cp.start()
    for n in range(2):
        cols = slice(n * HB, n * HB + HB)
        mid[:, :, cols] = half_b(mine2, n).reshape(2, 256, HB)

    def down_total():
        o_wdn[...] = sum_d.s3().astype(BF)
        line_d.s0()

    mg1, mg2 = v.mg1, v.mg2
    mg1[...] = jnp.zeros((16, D), F32)
    mg2[...] = jnp.zeros((16, HB), F32)
    o_rows = jnp.zeros((1, D), F32)

    def place_rows(ids, p):
        lane = iota((128, 128), 1)
        return ones_where((lane - 4 * p).astype(F32) == ids)

    def hand_back(src, land, rs, slabs):
        for s in slabs:
            ss = sem()
            dst = land.at[r % 2, pl.ds(2 * k, 2)]
            at = rs + (r % 2) * 2 + k
            far = remote(src.at[:, s], dst, ss, at, (owner_c, s))
            near = local(src.at[:, s], dst, at)
            here = is_own & (r == s)

            @pl.when(jnp.logical_not(here))
            def _(far=far):
                far.start()

            @pl.when(here)
            def _(near=near):
                near.start()

            def done(far=far, here=here):
                @pl.when(jnp.logical_not(here))
                def _():
                    far.wait_send()

            last.append(done)

    def landed(land, rs, out, first):
        for i in range(2):
            for kk in range(2):
                place = land.at[i, pl.ds(2 * kk, 2)]
                local(place, place, rs + 2 * i + kk).wait()
        for i in range(2):
            tok[first + i] = dot_l(pm[...], land[i].reshape(256, D)).astype(BF)
        cp = local(tok.at[pl.ds(first, 2)], out, sem())
        cp.start()
        last.append(cp.wait)

    ro_out, ro_gin = sem(4), sem(4)

    b_cp.wait()

    def out_half(n, bd):
        jj = n // 2
        g = 2 * k + jj
        rows = pl.ds(pl.multiple_of((n % 2) * 128, 128), 128)
        h64 = pl.ds((n % 2) * 2, 2)
        o = oh[g, rows, :]
        ao = dot(att[g, rows, :], wo[...]) + par[10:11, D : 2 * D]
        m = tok[g, rows, :].astype(F32) + piece(o, 2) * ao
        gp[jj, rows, :] = m
        branch = mid[jj, rows, :] + v.brcv[jj, h64].reshape(128, D).astype(F32) + par[10:11, 0:D]
        v.brcv[jj, h64] = ao.astype(BF).reshape(2, 64, D)
        stg_c[jj, h64] = (m + piece(o, 5) * branch).astype(BF).reshape(2, 64, D)
        low = (cot[g, rows, :].astype(F32) * branch).astype(BF)
        mg1[...] += dot_l(place_rows(lv[g, rows, :], 3), low)[0:16]
        return bd + jnp.sum(bg[g, rows, :].astype(F32), axis=0, keepdims=True)

    sg1[10:11, 0:D] = lax.fori_loop(0, 4, out_half, o_rows)
    hand_back(stg_c, v.oland, ro_out, range(4))
    def pos_of(b):
        bx, by = b % 2, b // 2
        fx = (bx - x) * (bx - x)
        fy = (by - y) * (by - y)
        return 2 * (1 - fx) + 1 - fy

    def hidden_back(b, _):
        lo = pl.multiple_of(b * HB, 128)
        wide = pl.multiple_of(HB * (2 * b + k), 128)
        pl.when(b == 2)(down_total)

        def down_grad(pr, _):
            both = dot_t(bg[pl.ds(2 * pr, 2)].reshape(512, D), wdn[pl.ds(lo, HB), :])
            for pc in range(2):
                g = 2 * pr + pc
                t = both[pc * 256 : pc * 256 + 256] * upg[g, :, pl.ds(lo, HB)].astype(F32)
                t = t.astype(BF)
                gb[g, 16:272, :] = t
                gs[g, 16:272, :] = shifted(t.astype(F32), pc).astype(BF)
            return 0

        lax.fori_loop(0, 2, down_grad, 0)

        def conv_back(lt, _):
            l0 = pl.multiple_of(lt * 128, 128)
            ln = pl.ds(l0, 128)
            kr = [par[t : t + 1, pl.ds(wide + l0, 128)] for t in range(9)]
            gk = [jnp.zeros((8, 128), F32) for _ in range(10)]
            for g in range(4):
                for h in range(2):
                    here = upr[g, h * 128 : h * 128 + 128, pl.ds(lo + l0, 128)].astype(F32)

                    def load(gsrc, ro, moved):
                        return (gs if moved else gb)[gsrc, pl.ds(16 + 16 * ro + 128 * h, 128), ln]

                    acc = conv_both(load, here, kr, gk, taps_of(g // 2, g % 2, True))
                    low = acc.astype(BF)
                    upg[g, h * 128 : h * 128 + 128, pl.ds(lo + l0, 128)] = low
                    gk[9] = gk[9] + fold_rows(low.astype(F32))
            for t in range(10):
                sg1[t : t + 1, pl.ds(wide + l0, 128)] = jnp.sum(gk[t], axis=0, keepdims=True)
            return 0

        lax.fori_loop(0, 3, conv_back, 0)
        got = dot(fint[...], upg[:, :, pl.ds(lo, HB)].reshape(1024, HB)).astype(BF)
        for rb in range(4):
            upr[pos_of(rb), 0:192, pl.ds(lo, HB)] = got[rb * 192 : rb * 192 + 192]
        for t in range(4):

            @pl.when(b == t)
            def _(t=t):
                sum_u.s0(t)
                if t >= 1:
                    sum_u.s1(t - 1)
                if t >= 3:
                    sum_u.s3(t - 3)

        return 0

    lax.fori_loop(0, 4, hidden_back, 0)

    for n in range(2):
        cols = slice(n * HB, n * HB + HB)
        stg_t[:, :, :, cols] = half_f(other2, n).astype(BF).reshape(2, 4, 64, HB)
    f_cp = remote(stg_t, v.frcv, sem(), sem(), sib)
    f_cp.start()
    sum_u.s3(1)
    sum_u.s4(0)
    for n in range(2):
        cols = slice(n * HB, n * HB + HB)
        mid[:, :, cols] = half_f(mine2, n).reshape(2, 256, HB)

    sum_u.s1(3)
    sum_u.s4(1)
    f_cp.wait()

    def two_back(n, bo):
        pl.when(n == 3)(line_d.s1)
        jj = n // 2
        g = 2 * k + jj
        rows = pl.ds(pl.multiple_of((n % 2) * 128, 128), 128)
        h64 = pl.ds((n % 2) * 2, 2)
        o = oh[g, rows, :]
        gate1 = piece(o, 2)
        nrm, inv = norm_parts(gp[jj, rows, :])
        fg = mid[jj, rows, :] + v.frcv[jj, h64].reshape(128, D).astype(F32)
        mg = cot[g, rows, :].astype(F32) + norm_back(fg * (1.0 + piece(o, 4)), nrm, inv)
        mid[jj, rows, :] = mg
        ag = (gate1 * mg).astype(BF)
        tmpa[g, rows, :] = ag
        ids = lv[g, rows, :]
        ao = v.brcv[jj, h64].reshape(128, D).astype(F32)
        total = dot_l(place_rows(ids, 0), (mg * ao).astype(BF))
        total = total + dot_l(place_rows(ids, 1), fg.astype(BF))
        total = total + dot_l(place_rows(ids, 2), (fg * nrm).astype(BF))
        mg1[...] += total[0:16]
        return bo + jnp.sum(ag.astype(F32), axis=0, keepdims=True)

    sg1[10:11, D : 2 * D] = lax.fori_loop(0, 4, two_back, o_rows)
    ag_place = tmpa.at[pl.ds(2 * k, 2)]
    ag_cp = swap(ag_place, ag_place, sib)

    sum_u.s3(2)
    sum_u.s3(3)
    sum_u.s4(2)
    mgs1[...] = mg1[...].astype(BF)
    mg_cp = swap(mgs1, mgr1, sib)
    all1.go(0)

    ag_cp.wait_recv()
    mg_cp.wait_recv()
    sum_u.s4(3)
    gat1.s0()
    dqkv = act
    kr_rows = pl.ds(kcol, HB)

    def heads_back(g, _):
        pl.when(g == 3)(line_d.s2)
        oq, mk = masks_of(g)
        mk2 = jnp.concatenate([mk, mk], axis=0)
        for h in range(2):
            at = pl.ds(pl.multiple_of(g * 256 + h * 128, 128), 128)
            fint[:, at] = att[g, h * 128 : h * 128 + 128, :].astype(F32).T.astype(BF)
        act[g, :, 3 * HB : 4 * HB] = dot_t(tmpa[g], wo[kr_rows, :]).astype(BF)
        for hp in range(3):
            qp = qkv[g, :, hp * 128 : hp * 128 + 128]
            kp = qkv[g, :, HB + hp * 128 : HB + hp * 128 + 128]
            vp = qkv[g, :, 2 * HB + hp * 128 : 2 * HB + hp * 128 + 128]
            dop = act[g, :, 3 * HB + hp * 128 : 3 * HB + hp * 128 + 128]
            k2 = jnp.concatenate([kp * lmb[0], kp * lmb[1]], axis=0)
            v2 = jnp.concatenate([vp * lmb[0], vp * lmb[1]], axis=0)
            s = dot_t(jnp.concatenate([k2, mk2], axis=1), jnp.concatenate([qp, oq], axis=1))
            dp = dot_t(v2, dop)
            probs, dss = [], []
            for h in range(2):
                sh = s[h * 256 : h * 256 + 256]
                dph = dp[h * 256 : h * 256 + 256]
                e = jnp.exp(sh - jnp.max(sh, axis=0, keepdims=True))
                prob = e * (1.0 / jnp.sum(e, axis=0, keepdims=True))
                delta = jnp.sum(prob * dph, axis=0, keepdims=True)
                probs.append(prob.astype(BF))
                dss.append((prob * (dph - delta)).astype(BF))
            ds2 = jnp.concatenate(dss, axis=0)
            dv2 = dot(jnp.concatenate(probs, axis=0), dop)
            dk2 = dot(ds2, qp)
            dq = dot_l(ds2, k2) * 0.125
            dv = dv2[0:256] * lmf[0] + dv2[256:512] * lmf[1]
            dk = dk2[0:256] * lmf[0] + dk2[256:512] * lmf[1]
            dqkv[g, :, hp * 128 : hp * 128 + 128] = dq.astype(BF)
            dqkv[g, :, HB + hp * 128 : HB + hp * 128 + 128] = dk.astype(BF)
            dqkv[g, :, 2 * HB + hp * 128 : 2 * HB + hp * 128 + 128] = dv.astype(BF)
        return 0

    lax.fori_loop(0, 4, heads_back, 0)
    all1.end(0)
    all1.go(1)
    line_u.s1()

    def proj_back(g, _):
        upg[g, :, 0:D] = dot_t(dqkv[g, :, 0 : 3 * HB], wq[...]).astype(BF)
        return 0

    lax.fori_loop(0, 4, proj_back, 0)
    cg_cp = swap(upg.at[:, :, pl.ds(0, D)], bg, sib)

    def grad_qkv(nt, _):
        ln = pl.ds(pl.multiple_of(nt * HB, 128), HB)
        got = dot(c1t[...], dqkv[:, :, ln].reshape(1024, HB)).astype(BF)
        for b in range(4):
            wup[pl.ds(pl.multiple_of(192 * pos_of(b), 64), 192), ln] = got[b * 192 : b * 192 + 192]
        for t in range(3):

            @pl.when(nt == t)
            def _(t=t):
                sum_q.s0(t)

        return 0

    lax.fori_loop(0, 3, grad_qkv, 0)
    all1.end(1)
    all1.go(2)
    gat1.s1()
    sg2[9:10, pl.ds(kcol, HB)] = jnp.sum(
        jnp.sum(dqkv[:, :, 0:HB].astype(F32), axis=0), axis=0, keepdims=True
    )
    sg2[10:11, pl.ds(kcol, HB)] = jnp.sum(
        jnp.sum(dqkv[:, :, 2 * HB : 3 * HB].astype(F32), axis=0), axis=0, keepdims=True
    )
    def grad_out(pos, _):
        rows = pl.ds(pl.multiple_of(96 * (2 * block_at(pos) + k), 32), 96)
        gwo[pos] = dot(fint[rows, :], tmpa[...].reshape(1024, D)).astype(BF)
        pl.when(pos == 0)(sum_o.s0)
        return 0

    lax.fori_loop(0, 4, grad_out, 0)
    for t in range(3):
        sum_q.s1(t)
    all1.plane()
    line_a.s0()
    cg_cp.wait_recv()

    def cg_sum(pr, _):
        for pc in range(2):
            g = 2 * pr + pc
            t = (upg[g, :, 0:D].astype(F32) + bg[g].astype(F32)).astype(BF)
            sh = shifted(t.astype(F32), pc).astype(BF)
            ub[g, 16:272, :] = t[:, 0:HB]
            gb[g, 16:272, :] = t[:, HB:D]
            us[g, 16:272, :] = sh[:, 0:HB]
            gs[g, 16:272, :] = sh[:, HB:D]
        return 0

    lax.fori_loop(0, 2, cg_sum, 0)
    sum_o.s1()
    sum_o.s2()
    gat1.s2()
    for hh in range(2):
        base, side = (ub, us) if hh == 0 else (gb, gs)

        def conv_one_back(lt, _, hh=hh, base=base, side=side):
            l0 = pl.multiple_of(lt * 128, 128)
            la = pl.multiple_of(hh * HB + lt * 128, 128)
            kr = [par[11 + t // 4 : 12 + t // 4, pl.ds((t % 4) * D + la, 128)] for t in range(9)]
            gk = [jnp.zeros((8, 128), F32) for _ in range(9)]
            for pc in range(2):
                for h in range(2):
                    here = ain[2 * k + pc, 16 + 128 * h : 144 + 128 * h, pl.ds(la, 128)].astype(F32)

                    def load(gsrc, ro, moved):
                        at = pl.ds(pl.multiple_of(16 + 16 * ro + 128 * h, 16), 128)
                        return (side if moved else base)[gsrc, at, pl.ds(l0, 128)]

                    acc = conv_both(load, here, kr, gk, taps_of(k, pc, True))
                    gp[pc, h * 128 : h * 128 + 128, pl.ds(la, 128)] = acc
            for t in range(9):
                sg2[t : t + 1, pl.ds(la, 128)] = jnp.sum(gk[t], axis=0, keepdims=True)
            return 0

        lax.fori_loop(0, 3, conv_one_back, 0)
    all2.go(0)
    sum_q.s3(0)
    sum_q.s3(1)
    line_u.s2()
    sum_q.s4(0)

    def sums_back(n, _):
        jj = n // 2
        g = 2 * k + jj
        rows = pl.ds(pl.multiple_of((n % 2) * 128, 128), 128)
        nrm, _inv = norm_parts(tok[g, rows, :].astype(F32))
        ig = gp[jj, rows, :]
        ids = lv[g, rows, :]
        low = ig.astype(BF)
        scl = (ig * nrm).astype(BF)
        total = dot_l(place_rows(ids, 0), low[:, 0:HB]) + dot_l(place_rows(ids, 1), low[:, HB:D])
        total = total + dot_l(place_rows(ids, 2), scl[:, 0:HB]) + dot_l(place_rows(ids, 3), scl[:, HB:D])
        mg2[...] += total[0:16]
        return 0

    lax.fori_loop(0, 4, sums_back, 0)
    mgs2[...] = mg2[...].astype(BF)
    mg2_cp = swap(mgs2, mgr2, sib)

    def one_back(n, _):
        jj = n % 2
        g = 2 * k + jj
        rows = pl.ds(pl.multiple_of((n // 2) * 128, 128), 128)
        h64 = pl.ds((n // 2) * 2, 2)
        nrm, inv = norm_parts(tok[g, rows, :].astype(F32))
        ig = gp[jj, rows, :]
        gi = mid[jj, rows, :] + norm_back(ig * (1.0 + piece(oh[g, rows, :], 1)), nrm, inv)
        stg_t[jj, h64] = gi.astype(BF).reshape(2, 64, D)
        return 0

    lax.fori_loop(0, 2, one_back, 0)
    mg2_cp.wait_recv()
    gat2.s0()
    hand_back(stg_t, v.gland, ro_gin, range(2))
    sum_q.s4(1)
    lax.fori_loop(2, 4, one_back, 0)

    sum_q.s3(2)
    hand_back(stg_t, v.gland, ro_gin, range(2, 4))
    sum_q.s4(2)
    o_wout[...] = sum_o.s3().astype(BF)
    line_o.s0()
    all2.end(0)
    all2.go(1)

    def load_again(p):
        return local(wada_h.at[:, pl.ds(p * D, D)], wdn.at[pl.ds((p % 2) * D, D), :], s_wa + p % 2)

    load_again(2).start()
    load_again(3).start()

    def pick(p):
        ri, ci = iota((16, 16), 0), iota((16, 16), 1)
        return ones_where((ri // 4 == r) & (ci == 4 * p + ri % 4))

    my1 = mga1[slot]
    my2 = mga2[slot]
    cg = jnp.zeros((16, D), F32)
    for p in range(2, 6):
        load_again(p).wait()
        lhs = dot(pick(p - 2), my1).astype(BF)
        cg = cg + dot_t(lhs, wdn[(p % 2) * D : (p % 2) * D + D, :])
        load_again((p + 2) % 6).start()
    for p in range(2):
        load_again(p).wait()
        for h in range(2):
            lhs = dot(pick(2 * p + h), my2).astype(BF)
            cg = cg + dot_t(lhs, wdn[p * D : p * D + D, h * HB : h * HB + HB])
    cond = condc[...]
    sig = 1.0 / (1.0 + jnp.exp(-cond))
    cgsum = v.cgsum
    cgsum[...] = cg * (sig * (1.0 + cond * (1.0 - sig)))
    crcv = v.crcv
    cr, cs = sem(2), sem(4)
    for s in range(4):
        src = cgsum.at[pl.ds(pl.multiple_of(8 * owner, 8), 8), :]
        dst = crcv.at[r % 2]
        far = remote(src, dst, cs + s, cr + r % 2, (c, s))
        near = local(src, dst, cr + r % 2)

        @pl.when(is_own & (r != s))
        def _(far=far):
            far.start()

        @pl.when(is_own & (r == s))
        def _(near=near):
            near.start()

        def done(far=far, s=s):
            @pl.when(is_own & (r != s))
            def _():
                far.wait_send()

        last.append(done)

    all2.end(1)
    all2.go(2)
    line_a.s1()
    line_q.s1()
    line_o.s1()
    all2.plane()
    line_b.s0()
    gat2.s1()
    line_a.s2()
    line_q.s2()
    line_o.s2()
    gat2.s2()
    line_b.s1()
    for done in tok_passed:
        done()
    landed(v.oland, ro_out, o_out, 0)

    low_y.wait_recv()
    ri, ci = iota((96, D), 0), iota((96, D), 1)
    cond_t = dot_t(ones_where(ci == 96 * c + ri), clow[...].reshape(64, D)).astype(BF)
    ej, en = iota((64, 256), 0), iota((64, 256), 1)
    bn = iota((8, 256), 1)

    def spread(p):
        return dot(cond_t, ones_where((en // 16 == ej // 4) & (en % 16 == 4 * p + ej % 4))).astype(BF)

    gat1.s3()
    o_bada[...] = jnp.zeros((8, 6 * D), F32)
    every1 = mga1[...].reshape(256, D)

    def ada_out(p):
        cp = local(wdn.at[pl.ds(96 * p, 96), :], o_wada.at[:, pl.ds(p * D, D)], sem())
        cp.start()
        last.append(cp.wait)

    for p in range(4):
        wdn[(p + 2) * 96 : (p + 3) * 96, :] = dot(spread(p), every1).astype(BF)
        ada_out(p + 2)
        o_bada[0:1, (p + 2) * D : (p + 3) * D] = dot(ones_where((bn % 16) // 4 == p), every1)[0:1]
    gat2.s3()
    every2 = mga2[...].reshape(256, HB)
    for p in range(4):
        half = (p % 2) * HB
        wdn[p // 2 * 96 : p // 2 * 96 + 96, half : half + HB] = dot(spread(p), every2).astype(BF)
        o_bada[0:1, p * HB : (p + 1) * HB] = dot(ones_where((bn % 16) // 4 == p), every2)[0:1]
    ada_out(0)
    ada_out(1)
    line_b.s2()
    line_d.s3()
    line_u.s3()
    landed(v.gland, ro_gin, o_gin, 2)
    for i in range(2):
        local(crcv.at[i], crcv.at[i], cr + i).wait()
    both = crcv[0] + crcv[1]
    for i in range(2):
        o_cond[i] = both[4 * i : 4 * i + 4]
    line_a.s3()
    o_sg1[...] = v.sg1s[0].astype(F32)
    line_b.s3()
    o_sg2[...] = v.sg2s[0].astype(F32)
    line_o.s3()
    line_q.s3()
    for done in last:
        done()
    for s in (sum_d, sum_u, sum_o, sum_q):
        s.sent()
    assert count[0] <= N_SEMS, count[0]


def finish(
    out, gin, gcond, wada, bada_h, sg1_h, sg2_h, wqkv, wout, wup, wdn,
    f_out, f_gin, f_gcond, f_wada, f_bada, f_conv1, f_wqkv, f_bqv, f_wout, f_bout, f_wup, f_bup, f_conv2, f_wdn,
    f_bdn, sems, *bufs,
):
    c = lax.axis_index("canvas")
    bada, sg1, sg2, narrow, wide = bufs[0], bufs[1], bufs[2], bufs[3:9], bufs[9:15]
    small = ((sg1_h, sg1), (sg2_h, sg2), (bada_h, bada))
    large = ((wada, f_wada), (gin, f_gin), (wup, f_wup), (wdn, f_wdn), (wqkv, f_wqkv), (wout, f_wout))
    ins = [pltpu.make_async_copy(src, buf, sems.at[i]) for i, ((src, _), buf) in enumerate(zip(large, narrow))]
    ins += [pltpu.make_async_copy(src, buf, sems.at[6 + i]) for i, (src, buf) in enumerate(small)]
    outs = [pltpu.make_async_copy(buf, dst, sems.at[9 + i]) for i, ((_, dst), buf) in enumerate(zip(large, wide))]
    ins.append(pltpu.make_async_copy(out, bufs[15], sems.at[15]))
    ins.append(pltpu.make_async_copy(gcond, f_gcond, sems.at[16]))
    outs.append(pltpu.make_async_copy(bufs[15], f_out, sems.at[15]))
    for cp in ins:
        cp.start()
    for i in range(6):
        ins[i].wait()
        wide[i][...] = narrow[i][...].astype(F32)
        outs[i].start()
    for cp in ins[6:]:
        cp.wait()
    outs[6].start()

    def cut(rows, n):
        wide = rows.shape[1]
        return pltpu.roll(rows, lax.rem(wide - c * n, wide), 1)[:, 0:n]

    f_bada[...] = cut(bada[...], 576)[0]
    f_conv1[...] = cut(sg2[...], 96)[0:9]
    both = jnp.concatenate([sg2[8:16, :], sg2[8:16, :]], axis=1)
    f_bqv[...] = cut(jnp.where(iota((8, 2 * D), 1) < D, both, pltpu.roll(both, 7, 0)), 192)[1]
    f_bout[...] = cut(sg1[8:16, D : 2 * D], 96)[2]
    f_bdn[...] = cut(sg1[8:16, 0:D], 96)[2]
    ln = pl.ds(pl.multiple_of(c * HB, 128), HB)
    f_bup[...] = sg1[9:10, ln][0]
    f_conv2[...] = sg1[0:9, ln]
    for cp in outs:
        cp.wait()


def fast_shards(
    tokens, latent, condition, w_ada, b_ada, conv_attn, w_qkv, bias_qv, w_out, b_out,
    w_up, b_up, conv_ffn, w_down, b_down, cotangent,
):
    anyspace = pl.BlockSpec(memory_space=pl.ANY)
    vm = pl.BlockSpec(memory_space=pltpu.VMEM)
    outs = (
        ((2, 256, D), BF),
        ((2, 256, D), BF),
        ((2, 4, D), F32),
        ((96, 6 * D), BF),
        ((8, 6 * D), F32),
        ((16, FF), F32),
        ((16, D), F32),
        ((96, 3 * D), BF),
        ((96, D), BF),
        ((96, FF), BF),
        ((HB, D), BF),
    )
    got = pl.pallas_call(
        whole_block,
        out_shape=[jax.ShapeDtypeStruct(s, t) for s, t in outs],
        in_specs=[anyspace, anyspace, vm, vm] + [anyspace] * 5 + [vm] * 7,
        out_specs=[anyspace, anyspace, vm, anyspace] + [vm] * (len(outs) - 4),
        scratch_shapes=[pltpu.SemaphoreType.DMA((N_SEMS,))] + [pltpu.VMEM(s, t) for s, t in SCRATCH.values()],
        compiler_params=pltpu.CompilerParams(
            collective_id=0, has_side_effects=True, vmem_limit_bytes=VMEM_LIMIT
        ),
        name="block",
    )(
        tokens, cotangent, latent, condition, w_ada, w_qkv, w_out, w_up, w_down,
        b_ada, conv_attn, bias_qv, b_out, b_up, conv_ffn, b_down,
    )
    big = ((96, 6 * D), (2, 256, D), (96, FF), (HB, D), (96, 3 * D), (96, D))
    shapes = (
        (2, 256, D), (2, 256, D), (2, 4, D), (96, 6 * D), (576,), (9, 96), (96, 3 * D), (192,), (96, D), (96,),
        (96, FF), (HB,), (9, HB), (HB, D), (96,),
    )
    out, gin, gcond, wada, bada, conv1, wqkv, bqv, wout, bout, wup, bup, conv2, wdn, bdn = pl.pallas_call(
        finish,
        out_shape=[jax.ShapeDtypeStruct(s, F32 if i else BF) for i, s in enumerate(shapes)],
        in_specs=[anyspace] * 11,
        out_specs=[anyspace if i in (0, 1, 3, 6, 8, 10, 13) else vm for i in range(len(shapes))],
        scratch_shapes=[pltpu.SemaphoreType.DMA((17,))]
        + [pltpu.VMEM(s, F32) for s in ((8, 6 * D), (16, FF), (16, D))]
        + [pltpu.VMEM(s, BF) for s in big]
        + [pltpu.VMEM(s, F32) for s in big]
        + [pltpu.VMEM((2, 256, D), BF)],
        compiler_params=pltpu.CompilerParams(vmem_limit_bytes=VMEM_LIMIT),
        name="finish",
    )(*got)
    return (
        out, gin, gcond, wada, bada, conv1, wqkv, bqv, wout, bout,
        wup, bup, conv2, wdn, bdn,
    )


def solution(mesh):
    placed = (
        P("canvas", "rows", None),
        P("canvas", "rows"),
        P("canvas", None, None),
        P(),
        P(),
        P(),
        P(),
        P(),
        P(),
        P(),
        P(),
        P(),
        P(),
        P(),
        P(),
        P("canvas", "rows", None),
    )
    fits = mesh.shape["rows"] == 4 and mesh.shape["canvas"] == 8
    return jax.shard_map(
        fast_shards if fits else shards,
        mesh=mesh,
        in_specs=placed,
        out_specs=(
            P("canvas", "rows", None),
            P("canvas", "rows", None),
            P("canvas", None, None),
            P("canvas", None),
            P("canvas"),
            P(None, "canvas"),
            P("canvas", None),
            P("canvas"),
            P("canvas", None),
            P("canvas"),
            P("canvas", None),
            P("canvas"),
            P(None, "canvas"),
            P("canvas", None),
            P("canvas"),
        ),
        check_vma=False,
    )
```
